256 devices in a mesh: dp: 64 (over x, y_hi, z), tp: 4 (over y_lo, core).
Axes of the slice: x: 4, y: 4 (y_hi: 2, y_lo: 2; y = y_hi * 2 + y_lo), z: 8, core: 2. Of those that a mesh axis runs over, the one named last changes fastest.
Arguments:
- partials: bfloat16 [64, 7168, 1024], P('dp', None, 'tp'), may hold values from -4 to 4, as said below
- momentum: float32 [7168, 1024], P('dp', 'tp'), may hold values from -6 to 6
- weights: float32 [7168, 1024], P('dp', 'tp'), may hold values from -6 to 6
Outputs:
- update: float32 [7168, 1024], P('dp', 'tp')
- new_weights: float32 [7168, 1024], P('dp', 'tp')
- new_momentum: float32 [7168, 1024], P('dp', 'tp')
The draws below stay inside these ranges and needn't reach their ends.
Inputs may be any that keep to these rules, and one draw needn't show every extreme that they name: `partials`: real-valued partial gradients.
All inputs are finite; a program needn't handle non-finite values.
Results may differ from the reference program's by a relative error of at most 0.0003.
Values sent between devices are 32-bit elements; how exact they have to be, the bound alone decides.
A program may use at most 64 MiB of HBM per device.

```python
import math
import jax
import jax.numpy as jnp
from jax import lax

D = 7168
FF = 1024
ITERS = 2
N_DP = 64


def draw_partials(key, part):
    key = jax.random.fold_in(key, 11)
    noise_key, row_key, col_key = jax.random.split(key, 3)
    position = jnp.arange(D, dtype=jnp.float32) / (D - 1)
    row_scale = 10.0 ** (0.5 * position + 0.5 * jax.random.uniform(row_key, (D,), jnp.float32))
    col_scale = 10.0 ** jax.random.uniform(col_key, (FF,), jnp.float32)
    profile = row_scale[:, None] * col_scale[None, :]
    private = jnp.clip(jax.random.normal(noise_key, (N_DP, D, FF), jnp.float32), -4.0, 4.0)
    values = 0.01 * private * profile[None]
    return values.astype(jnp.bfloat16)


def shard_levels(own_key, shape, shards, least, high):
    factor_of, own = 1.0, jax.random.fold_in(own_key, 6)
    for axis_at, parts in shards:
        steps = jnp.exp(jax.random.uniform(jax.random.fold_in(own, axis_at), (parts,), jnp.float32, least / len(shards), high / len(shards)))
        factor_of = factor_of * jnp.repeat(steps, shape[axis_at] // parts).reshape([-1 if axis == axis_at else 1 for axis in range(len(shape))])
    return factor_of


def gaussian(key, dims, deviation, limit, cuts=(), kind=jnp.bfloat16):
    level = shard_levels(key, dims, cuts, -0.22, 0.18) if cuts else 1.0
    result = jax.random.normal(key, dims, jnp.float32) * deviation * level
    return jnp.minimum(jnp.maximum(result, -limit), limit).astype(kind)


def setup_inputs(seed: int = 0) -> dict:
    arg_keys = jax.random.split(jax.random.key(seed), 4)
    partials = draw_partials(jax.random.fold_in(arg_keys[3], 71), 0)
    momentum = gaussian(arg_keys[1], (D, FF), 1.0, 6.0, ((0, 64), (1, 4)), jnp.float32)
    weights = gaussian(arg_keys[2], (D, FF), 1.0, 6.0, ((0, 64), (1, 4)), jnp.float32)
    return {"partials": partials, "momentum": momentum, "weights": weights}


COEF_A = 3.4445
COEF_B = -4.775
COEF_C = 2.0315
MOMENTUM_DECAY = 0.95
LEARN_RATE = 0.02
WEIGHT_DECAY = 0.1
NORM_EPS = 1e-07

def reference(partials, momentum, weights):

    def accumulate(replica, running):
        piece = lax.dynamic_index_in_dim(partials, replica, 0, keepdims=False)
        return running + piece.astype(jnp.float32)
    gradient = lax.fori_loop(0, partials.shape[0], accumulate, jnp.zeros(momentum.shape, jnp.float32))
    new_momentum = MOMENTUM_DECAY * momentum + gradient
    nesterov = gradient + MOMENTUM_DECAY * new_momentum
    inverse_norm = 1.0 / (jnp.sqrt(jnp.sum(nesterov * nesterov)) + NORM_EPS)
    current = nesterov * inverse_norm
    for iteration in range(ITERS):
        square = lax.dot_general(current, current, (((0,), (0,)), ((), ())), precision=lax.Precision.HIGHEST, preferred_element_type=jnp.float32)
        mixing = COEF_B * square + COEF_C * jnp.dot(square, square, precision=lax.Precision.HIGHEST, preferred_element_type=jnp.float32)
        current = COEF_A * current + jnp.dot(current, mixing, precision=lax.Precision.HIGHEST, preferred_element_type=jnp.float32)
    update = 0.2 * math.sqrt(max(D, FF)) * current
    new_weights = weights - LEARN_RATE * (update + WEIGHT_DECAY * weights)
    return (update, new_weights, new_momentum)
```

```python
import math

import jax
import jax.numpy as jnp
from jax import lax
from jax.sharding import PartitionSpec as P

D = 7168
FF = 1024

COEF_A = 3.4445
COEF_B = -4.775
COEF_C = 2.0315
MOMENTUM_DECAY = 0.95
LEARN_RATE = 0.02
WEIGHT_DECAY = 0.1
NORM_EPS = 1e-07


def mm(left, right):
    return jnp.dot(left, right, precision=lax.Precision.HIGH, preferred_element_type=jnp.float32)


def on_device(partials, momentum, weights):
    gradient = lax.psum_scatter(partials[0].astype(jnp.float32), "dp", scatter_dimension=0, tiled=True)
    new_momentum = MOMENTUM_DECAY * momentum + gradient
    nesterov = gradient + MOMENTUM_DECAY * new_momentum
    width = nesterov.shape[1]
    rows = lax.all_gather(nesterov, "tp", axis=1, tiled=True)
    gram = lax.psum(
        lax.dot_general(
            rows, rows, (((0,), (0,)), ((), ())),
            precision=lax.Precision.HIGH, preferred_element_type=jnp.float32,
        ),
        "dp",
    )
    inverse_norm = 1.0 / (jnp.sqrt(jnp.trace(gram)) + NORM_EPS)
    square = gram * (inverse_norm * inverse_norm)
    first = lax.axis_index("tp") * width
    eye = (lax.broadcasted_iota(jnp.int32, (FF, width), 0) == lax.broadcasted_iota(jnp.int32, (FF, width), 1) + first).astype(jnp.float32)

    def mix(block):
        once = mm(square, block)
        return COEF_A * block + COEF_B * once + COEF_C * mm(square, once)

    def next_gram(block):
        return mix(mm(square, mix(block)))

    own = lax.dynamic_slice_in_dim(square, first, width, 1)
    mixed = COEF_A * eye + COEF_B * own + COEF_C * mm(square, own)
    gram_one = mix(mm(square, mixed))
    mixed_one = COEF_A * eye + COEF_B * gram_one + COEF_C * next_gram(gram_one)
    total = mix(mixed_one)
    result = mm(rows * inverse_norm, total)
    update = 0.2 * math.sqrt(max(D, FF)) * result
    new_weights = weights - LEARN_RATE * (update + WEIGHT_DECAY * weights)
    return (update, new_weights, new_momentum)


def solution(mesh):
    return jax.shard_map(
        on_device,
        mesh=mesh,
        in_specs=(P("dp", None, "tp"), P("dp", "tp"), P("dp", "tp")),
        out_specs=(P("dp", "tp"), P("dp", "tp"), P("dp", "tp")),
        check_vma=False,
    )
```

```python
import functools
import math

import jax
import jax.numpy as jnp
from jax import lax
from jax.experimental import pallas as pl
from jax.experimental.pallas import tpu as pltpu
from jax.sharding import PartitionSpec as P

MESH = pl.DeviceIdType.MESH
F32 = jnp.float32
NX, NY, NZ = 4, 2, 8
ROWS = 112
HEAD = 48
TAIL = ROWS - HEAD
W = 256
FAR = (2, 3, 4, 5, 6)
NEAR = (7, 0, 1)
D = 7168
FF = 1024
COEF_A = 3.4445
COEF_B = -4.775
COEF_C = 2.0315
MOMENTUM_DECAY = 0.95
LEARN_RATE = 0.02
WEIGHT_DECAY = 0.1
NORM_EPS = 1e-07


class Ring:
    def __init__(self, n, place, send, recv, send_sem, recv_sem):
        self.n, self.place, self.send, self.recv = n, place, send, recv
        self.send_sem, self.recv_sem = send_sem, recv_sem

    def copy(self, d, k):
        return pltpu.make_async_remote_copy(
            src_ref=self.send.at[d, k], dst_ref=self.recv.at[d, k],
            send_sem=self.send_sem.at[d, k], recv_sem=self.recv_sem.at[d, k],
            device_id=self.place(1 if d == 0 else -1), device_id_type=MESH,
        )

    def offset(self, d, k):
        return (1 if d == 0 else -1) * (self.n // 2 - (k + 1) // 2)

    def issue(self, k, own):
        for d in range(2):
            value = own(self.offset(d, k), (k + d) % 2)
            if k >= 2:
                value = value + self.recv[d, k - 2]
            self.send[d, k] = value
            self.copy(d, k).start()

    def arrive(self, k):
        for d in range(2):
            self.copy(d, k).wait_recv()

    def sent(self):
        for d in range(2):
            for k in range(self.n - 1):
                self.copy(d, k).wait_send()


class ShortRing:
    def __init__(self, n, place, sign, own, send, recv, send_sem, recv_sem):
        self.n, self.place, self.sign, self.own = n, place, sign, own
        self.send, self.recv, self.send_sem, self.recv_sem = send, recv, send_sem, recv_sem

    def copy(self, d, k):
        return pltpu.make_async_remote_copy(
            src_ref=self.send.at[d, k], dst_ref=self.recv.at[d, k],
            send_sem=self.send_sem.at[d, k], recv_sem=self.recv_sem.at[d, k],
            device_id=self.place(self.sign if d == 0 else -self.sign), device_id_type=MESH,
        )

    def issue(self, d, k):
        value = self.own((self.sign if d == 0 else -self.sign) * (self.n // 2 - k))
        if k > d:
            value = value + self.recv[d, k - 1]
        self.send[d, k] = value
        self.copy(d, k).start()

    def start(self):
        self.issue(0, 0)
        self.issue(1, 1)

    def arrive(self, d, k):
        self.copy(d, k).wait_recv()

    def step(self, k):
        for d in range(2):
            if k >= d:
                self.arrive(d, k)
                if k + 1 < self.n // 2:
                    self.issue(d, k + 1)

    def total(self):
        return self.own(0) + self.recv[0, self.n // 2 - 1] + self.recv[1, self.n // 2 - 1]

    def sent(self):
        for d in range(2):
            for k in range(d, self.n // 2):
                self.copy(d, k).wait_send()


def split(value):
    high = value.astype(jnp.bfloat16)
    return high, (value - high.astype(F32)).astype(jnp.bfloat16)


def cross(left, right):
    (lh, ll), (rh, rl) = split(left), split(right)
    dims = (((0,), (0,)), ((), ()))
    dot = functools.partial(lax.dot_general, dimension_numbers=dims, preferred_element_type=F32)
    return dot(lh, rh) + (dot(lh, rl) + dot(ll, rh))


def kernel(part_hbm, mom_ref, newm_ref, xg, gp, gq, part, fin, yrecv, acc_p, acc_q,
           p_send, p_recv, p2_send, p2_recv, qa_send, qa_recv, qb_send, qb_recv, q2_send, q2_recv,
           src_p, src_q, gacc_p, gacc_q, piece, yrecv2,
           gp1_send, gp1_recv, gp2_send, gp2_recv, gq1_send, gq1_recv, gq2_send, gq2_recv,
           load_sem, p_s, p_r, p2_s, p2_r, qa_s, qa_r, qb_s, qb_r, q2_s, q2_r, y_sems,
           x_s, x_r, gp1_s, gp1_r, gp2_s, gp2_r, gq1_s, gq1_r, gq2_s, gq2_r,
           ap_s, ap_r, aq_s, aq_r, az_s, az_r, ax_s, ax_r, cp_s, cp_r, cq_s, cq_r):
    dp = lax.axis_index("dp")
    tp = lax.axis_index("tp")
    x, yh, z = dp // 16, (dp // 8) % 2, dp % 8

    def at(xx, yy, zz):
        return (lax.rem(xx + 2 * NX, NX) * 16 + lax.rem(yy + NY, NY) * 8 + lax.rem(zz + 2 * NZ, NZ), tp)

    def along_z(step):
        return at(x, yh, z + step)

    def along_x(step):
        return at(x + step, yh, z)

    load = pltpu.make_async_copy(part_hbm, part, load_sem)
    load.start()
    peers = [(at(x + dx, yh, z)[0], tp_to) for dx in range(NX) for tp_to in (tp, tp ^ 2) if dx or tp_to is not tp]
    peers += [(at(x, yh, z + dz)[0], tp_to) for dz in range(1, NZ) for tp_to in (tp, tp ^ 2)]
    peers += [at(x, yh + 1, z), (dp, tp ^ 1), (dp, tp ^ 3)]
    barrier = pltpu.get_barrier_semaphore()
    for peer in peers:
        pl.semaphore_signal(barrier, inc=1, device_id=peer, device_id_type=MESH)
    load.wait()
    pl.semaphore_wait(barrier, len(peers))

    p1 = Ring(NZ, along_z, p_send, p_recv, p_s, p_r)
    p2 = Ring(NX, along_x, p2_send, p2_recv, p2_s, p2_r)
    qa = Ring(NX, along_x, qa_send, qa_recv, qa_s, qa_r)
    qb = Ring(NX, along_x, qb_send, qb_recv, qb_s, qb_r)
    q2 = Ring(NZ, along_z, q2_send, q2_recv, q2_s, q2_r)

    def dest(xx, yy, zz):
        return lax.rem(xx + NX, NX) * 16 + yy * 8 + lax.rem(zz + NZ, NZ)

    def own_p1(off, half):
        return jnp.stack([part[dest(xx, half, z + off), :HEAD, :].astype(F32) for xx in range(NX)])

    def own_p2(off, half):
        return acc_p[half, lax.rem(x + off + NX, NX)]

    def own_q(rels):
        def own(off, half):
            return jnp.stack([part[dest(x + off, half, z + rel), HEAD:, :].astype(F32) for rel in rels])
        return own

    own_qa, own_qb = own_q(FAR), own_q(NEAR)

    def own_q2(off, half):
        return acc_q[half, off % NZ]

    def p1_final():
        for half in range(2):
            acc_p[half] = own_p1(0, half) + p_recv[0, 5 + (half + 1) % 2] + p_recv[1, 5 + half]

    def p2_final():
        for half in range(2):
            fin[half, :HEAD] = own_p2(0, half) + p2_recv[0, 1 + (half + 1) % 2] + p2_recv[1, 1 + half]

    def q_final(rels, own, recv):
        first = rels[0]
        for half in range(2):
            value = own(0, half) + recv[0, 1 + (half + 1) % 2] + recv[1, 1 + half]
            for i, rel in enumerate(rels):
                acc_q[half, rel] = value[i]

    def q2_final():
        for half in range(2):
            fin[half, HEAD:] = own_q2(0, half) + q2_recv[0, 5 + (half + 1) % 2] + q2_recv[1, 5 + half]

    p1.issue(0, own_p1)
    qa.issue(0, own_qa)
    p1.issue(1, own_p1)
    qa.issue(1, own_qa)
    p1.arrive(0)
    p1.issue(2, own_p1)
    qa.arrive(0)
    qa.issue(2, own_qa)
    p1.arrive(1)
    p1.issue(3, own_p1)
    p1.arrive(2)
    p1.issue(4, own_p1)
    qa.arrive(1)
    qb.issue(0, own_qb)
    p1.arrive(3)
    p1.issue(5, own_p1)
    qa.arrive(2)
    qb.issue(1, own_qb)
    q_final(FAR, own_qa, qa_recv)
    p1.arrive(4)
    p1.issue(6, own_p1)
    q2.issue(0, own_q2)
    q2.issue(1, own_q2)
    qb.arrive(0)
    qb.issue(2, own_qb)
    p1.arrive(5)
    q2.arrive(0)
    q2.issue(2, own_q2)
    p1.arrive(6)
    p1_final()
    p2.issue(0, own_p2)
    p2.issue(1, own_p2)
    q2.arrive(1)
    q2.issue(3, own_q2)
    qb.arrive(1)
    q2.arrive(2)
    q2.issue(4, own_q2)
    qb.arrive(2)
    q_final(NEAR, own_qb, qb_recv)
    q2.arrive(3)
    q2.issue(5, own_q2)
    q2.arrive(4)
    q2.issue(6, own_q2)
    p2.arrive(0)
    p2.issue(2, own_p2)
    p2.arrive(1)
    p2.arrive(2)
    p2_final()
    q2.arrive(5)
    q2.arrive(6)
    q2_final()


    def remote(src, dst, send_sem, recv_sem, device):
        return pltpu.make_async_remote_copy(
            src_ref=src, dst_ref=dst, send_sem=send_sem, recv_sem=recv_sem, device_id=device, device_id_type=MESH,
        )

    swap = remote(fin.at[1 - yh], yrecv, y_sems.at[0], y_sems.at[1], at(x, yh + 1, z))
    swap.start()
    for ring in (p1, p2, qa, qb, q2):
        ring.sent()
    swap.wait()
    gradient = fin[yh] + yrecv[...]
    new_momentum = MOMENTUM_DECAY * mom_ref[...] + gradient
    newm_ref[...] = new_momentum
    xg[tp] = gradient + MOMENTUM_DECAY * new_momentum

    gather = [remote(xg.at[tp], xg.at[tp], x_s.at[m - 1], x_r.at[m - 1], (dp, tp ^ m)) for m in (1, 2, 3)]
    gather[1].start()
    gather[2].start()
    gather[0].start()

    own_x = xg[tp]
    diag = cross(own_x, own_x)
    src_p[0] = diag[:, :128]
    src_p[1] = diag[:, 128:]
    for copy in gather:
        copy.wait_recv()
    side = cross(xg[lax.rem(tp + 1, 4)], own_x)
    high_x = xg[tp % 2 + 2]
    left = jnp.where(tp < 2, high_x[:, :128], high_x[:, 128:])
    far = cross(left, xg[tp % 2])
    for c in range(2):
        src_q[c, :256] = side[:, 128 * c:128 * c + 128]
        src_q[c, 256:] = far[:, 128 * c:128 * c + 128]

    def rows_of(xx, zz, rows):
        return pl.ds(pl.multiple_of(((xx % 2) * 8 + zz) * rows, 8), rows)

    def own_gp1(off):
        zz = lax.rem(z + off + NZ, NZ)
        return jnp.stack([src_p[xx // 2, rows_of(xx, zz, 16), :] for xx in range(NX)])

    def own_gq1(off):
        xx = lax.rem(x + off + NX, NX)
        return jnp.stack([src_q[xx // 2, rows_of(xx, zz, 24), :] for zz in range(NZ)])

    def own_gp2(off):
        return gacc_p[lax.rem(x + off + NX, NX)]

    def own_gq2(off):
        return gacc_q[lax.rem(z + off + NZ, NZ)]

    gp1 = ShortRing(NZ, along_z, 1, own_gp1, gp1_send, gp1_recv, gp1_s, gp1_r)
    gp2 = ShortRing(NX, along_x, -1, own_gp2, gp2_send, gp2_recv, gp2_s, gp2_r)
    gq1 = ShortRing(NX, along_x, 1, own_gq1, gq1_send, gq1_recv, gq1_s, gq1_r)
    gq2 = ShortRing(NZ, along_z, -1, own_gq2, gq2_send, gq2_recv, gq2_s, gq2_r)

    gp1.start()
    gq1.start()
    gp1.step(0)
    gq1.step(0)
    gp1.step(1)
    gq1.step(1)
    gacc_q[...] = gq1.total()
    gq2.start()
    gp1.step(2)
    gq2.step(0)
    gp1.step(3)
    gacc_p[...] = gp1.total()
    gp2.start()
    gq2.step(1)
    gp2.step(0)
    gq2.step(2)
    gp2.step(1)
    gq2.step(3)
    piece[:16] = gp2.total()
    piece[16:] = gq2.total()
    swap2 = remote(piece, yrecv2, y_sems.at[2], y_sems.at[3], at(x, yh + 1, z))
    swap2.start()
    for ring in (gp1, gp2, gq1, gq2):
        ring.sent()
    for copy in gather:
        copy.wait_send()
    swap2.wait()

    lo, core = tp // 2, tp % 2
    sibling = (dp, tp ^ 1)
    gp[core, z, x, lo] = piece[:16] + yrecv2[:16]
    gq[core, x, z, lo] = piece[16:] + yrecv2[16:]

    near_p, near_q = [], []
    for dy in range(2):
        for dx in range(NX):
            if dx or dy:
                mine = gp.at[core, z, x, lo]
                i = dy * NX + dx
                near_p.append(remote(mine, mine, ap_s.at[i], ap_r.at[i], (at(x + dx, yh, z)[0], tp ^ (2 * dy))))
        for dz in range(NZ):
            if dz or dy:
                mine = gq.at[core, x, z, lo]
                i = dy * NZ + dz
                near_q.append(remote(mine, mine, aq_s.at[i], aq_r.at[i], (at(x, yh, z + dz)[0], tp ^ (2 * dy))))
    for copy in near_p + near_q:
        copy.start()

    def z_at(off):
        return lax.rem(z + off + NZ, NZ)

    def x_at(off):
        return lax.rem(x + off + NX, NX)

    def pass_z(d, hop):
        sign = 1 if d == 0 else -1
        chunk = gp.at[core, z_at(-sign * hop)]
        if hop == 3:
            chunk = chunk.at[pl.ds(2 * d, 2)]
        return remote(chunk, chunk, az_s.at[d, hop], az_r.at[d, hop], along_z(sign))

    def pass_x(d, part_at):
        sign = 1 if d == 0 else -1
        half = d if part_at != 1 else 1 - d
        chunk = gq.at[core, x if part_at < 2 else x_at(-sign), pl.ds(4 * half, 4)]
        return remote(chunk, chunk, ax_s.at[d, part_at], ax_r.at[d, part_at], along_x(sign))

    shared = []

    def share_p(off, first=0, count=NX):
        i = len(shared)
        chunk = gp.at[core, z_at(off), pl.ds(first, count)]
        shared.append((chunk, remote(chunk, chunk, cp_s.at[i], cp_r.at[i], sibling)))
        shared[-1][1].start()

    def share_q(off, half):
        i = len(shared)
        chunk = gq.at[core, x_at(off), pl.ds(4 * half, 4)]
        shared.append((chunk, remote(chunk, chunk, cp_s.at[i], cp_r.at[i], sibling)))
        shared[-1][1].start()

    for copy in near_p:
        copy.wait_recv()
    for d in range(2):
        pass_z(d, 0).start()
    share_p(0)
    for copy in near_q:
        copy.wait_recv()
    for d in range(2):
        pass_x(d, 0).start()
    for d in range(2):
        pass_x(d, 1).start()
    share_q(0, 0)
    share_q(0, 1)

    def z_step(hop):
        for d in range(2):
            pass_z(d, hop).wait_recv()
            if hop < 3:
                pass_z(d, hop + 1).start()
        for d in range(2):
            sign = 1 if d == 0 else -1
            if hop < 3:
                share_p(-sign * (hop + 1))
            else:
                share_p(4, 2 * d, 2)

    def x_step(part_at):
        for d in range(2):
            pass_x(d, part_at).wait_recv()
            if part_at == 0:
                pass_x(d, 2).start()
        for d in range(2):
            sign = 1 if d == 0 else -1
            half = d if part_at != 1 else 1 - d
            share_q(-sign if part_at < 2 else 2, half)

    z_step(0)
    z_step(1)
    x_step(0)
    z_step(2)
    x_step(1)
    z_step(3)
    x_step(2)
    for _, copy in shared:
        copy.wait()
    for copy in near_p + near_q:
        copy.wait_send()
    for d in range(2):
        for hop in range(4):
            pass_z(d, hop).wait_send()
        for part_at in range(3):
            pass_x(d, part_at).wait_send()


def communicate(partials, momentum):
    def ring(n, *block):
        return [pltpu.VMEM((2, n - 1) + block, F32)] * 2

    def short(n, *block):
        return [pltpu.VMEM((2, n // 2) + block, F32)] * 2

    def sems(*shape):
        return [pltpu.SemaphoreType.DMA(shape)] * 2

    vmem = pl.BlockSpec(memory_space=pltpu.VMEM)
    return pl.pallas_call(
        kernel,
        out_shape=[
            jax.ShapeDtypeStruct((ROWS, W), F32),
            jax.ShapeDtypeStruct((4, ROWS, W), F32),
            jax.ShapeDtypeStruct((2, NZ, NX, 2, 16, 128), F32),
            jax.ShapeDtypeStruct((2, NX, NZ, 2, 24, 128), F32),
        ],
        in_specs=[pl.BlockSpec(memory_space=pl.ANY), vmem],
        out_specs=[vmem] * 4,
        scratch_shapes=[
            pltpu.VMEM((64, ROWS, W), jnp.bfloat16),
            pltpu.VMEM((2, ROWS, W), F32),
            pltpu.VMEM((ROWS, W), F32),
            pltpu.VMEM((2, NX, HEAD, W), F32),
            pltpu.VMEM((2, NZ, TAIL, W), F32),
            *ring(NZ, NX, HEAD, W), *ring(NX, HEAD, W),
            *ring(NX, len(FAR), TAIL, W), *ring(NX, len(NEAR), TAIL, W), *ring(NZ, TAIL, W),
            pltpu.VMEM((2, 256, 128), F32), pltpu.VMEM((2, 384, 128), F32),
            pltpu.VMEM((NX, 16, 128), F32), pltpu.VMEM((NZ, 24, 128), F32),
            pltpu.VMEM((40, 128), F32), pltpu.VMEM((40, 128), F32),
            *short(NZ, NX, 16, 128), *short(NX, 16, 128), *short(NX, NZ, 24, 128), *short(NZ, 24, 128),
            pltpu.SemaphoreType.DMA,
            *sems(2, NZ - 1), *sems(2, NX - 1), *sems(2, NX - 1), *sems(2, NX - 1), *sems(2, NZ - 1),
            pltpu.SemaphoreType.DMA((4,)),
            *sems(3),
            *sems(2, NZ // 2), *sems(2, NX // 2), *sems(2, NX // 2), *sems(2, NZ // 2),
            *sems(2 * NX), *sems(2 * NZ), *sems(2, 4), *sems(2, 3), *sems(18), *sems(1),
        ],
        compiler_params=pltpu.CompilerParams(collective_id=0, has_side_effects=True, vmem_limit_bytes=52 * 1024 * 1024),
    )(partials.reshape(64, ROWS, W), momentum)


def finish(x_ref, gp, gq, w_ref, m_ref, update_ref, neww_ref, newm_ref,
           a, a2, low, ah, al, a2h, a2l, mh, ml, vh, vl, y, w):
    tp = lax.axis_index("tp")
    newm_ref[...] = m_ref[...]
    trace = jnp.zeros((1, 1), F32)
    for t in range(4):
        core, lo, base = t % 2, t // 2, 256 * t
        for xx in range(NX):
            for zz in range(NZ):
                r, c = (xx % 2) * 8 + zz, xx // 2
                a[base + 16 * r:base + 16 * r + 16, base + 128 * c:base + 128 * c + 128] = gp[core, zz, xx, lo]
                low[t, 24 * r:24 * r + 24, 128 * c:128 * c + 128] = gq[core, xx, zz, lo]
        block = a[base:base + 256, base:base + 256]
        on_diag = lax.broadcasted_iota(jnp.int32, (256, 256), 0) == lax.broadcasted_iota(jnp.int32, (256, 256), 1)
        trace = trace + jnp.sum(jnp.where(on_diag, block, 0.0), keepdims=True)
    for t in range(4):
        nxt = (t + 1) % 4
        side = low[t, :256, :]
        a[256 * nxt:256 * nxt + 256, 256 * t:256 * t + 256] = side
        a[256 * t:256 * t + 256, 256 * nxt:256 * nxt + 256] = side.T
        far = low[t, 256:, :]
        i, j = 256 * (t % 2 + 2) + 128 * (t // 2), 256 * (t % 2)
        a[i:i + 128, j:j + 256] = far
        a[j:j + 256, i:i + 128] = far.T
    inverse = 1.0 / (jnp.sqrt(trace) + NORM_EPS)
    scale = inverse * inverse

    def tiles(body):
        def step(i, carry):
            body(pl.ds(pl.multiple_of(i * 256, 256), 256), i)
            return carry
        lax.fori_loop(0, 4, step, 0)

    def prepare(rows, _):
        block = a[rows, :] * scale
        a[rows, :] = block
        ah[rows, :], al[rows, :] = split(block)

    tiles(prepare)

    def dot3(lh, ll, rh, rl):
        dot = functools.partial(jnp.dot, preferred_element_type=F32)
        return dot(lh, rh) + (dot(lh, rl) + dot(ll, rh))

    for i in range(4):
        rows = slice(256 * i, 256 * i + 256)
        for j in range(i, 4):
            cols = slice(256 * j, 256 * j + 256)
            block = dot3(ah[rows, :], al[rows, :], ah[:, cols], al[:, cols])
            a2[rows, cols] = block
            if j > i:
                a2[cols, rows] = block.T

    def mix(rows, i):
        square = a2[rows, :]
        a2h[rows, :], a2l[rows, :] = split(square)
        same = lax.broadcasted_iota(jnp.int32, (256, FF), 0) + i * 256 == lax.broadcasted_iota(jnp.int32, (256, FF), 1)
        value = COEF_B * a[rows, :] + COEF_C * square + jnp.where(same, COEF_A, 0.0)
        mh[rows, :], ml[rows, :] = split(value)

    tiles(mix)

    own = pl.ds(pl.multiple_of(tp * 256, 256), 256)

    def eye(i):
        return jnp.where(
            lax.broadcasted_iota(jnp.int32, (256, W), 0) + i * 256 == lax.broadcasted_iota(jnp.int32, (256, W), 1) + tp * 256,
            COEF_A, 0.0,
        )

    def start(rows, i):
        w[rows, :] = a[rows, own]
        value = COEF_B * a[rows, own] + COEF_C * a2[rows, own] + eye(i)
        vh[rows, :], vl[rows, :] = split(value)

    tiles(start)

    def product(high, lowp, after):
        def body(rows, i):
            y[rows, :] = after(dot3(high[rows, :], lowp[rows, :], vh[...], vl[...]), rows, i)
        tiles(body)

        def again(rows, i):
            vh[rows, :], vl[rows, :] = split(y[rows, :])
        tiles(again)

    product(mh, ml, lambda value, rows, i: value)
    product(a2h, a2l, lambda value, rows, i: COEF_B * w[rows, :] + COEF_C * value)
    product(mh, ml, lambda value, rows, i: value)
    product(mh, ml, lambda value, rows, i: value + eye(i))

    xh, xl = split(jnp.concatenate([x_ref[t] for t in range(4)], axis=1) * inverse)
    result = jnp.zeros((ROWS, W), F32)
    for t in range(4):
        cols = slice(256 * t, 256 * t + 256)
        once_h, once_l = split(dot3(xh, xl, mh[:, cols], ml[:, cols]))
        result = result + dot3(once_h, once_l, vh[cols, :], vl[cols, :])
    update = 0.2 * math.sqrt(max(D, FF)) * result
    update_ref[...] = update
    neww_ref[...] = w_ref[...] - LEARN_RATE * (update + WEIGHT_DECAY * w_ref[...])


def orthogonalize(x, gp, gq, weights, new_momentum):
    vmem = pl.BlockSpec(memory_space=pltpu.VMEM)
    block = jax.ShapeDtypeStruct((ROWS, W), F32)
    half = jnp.bfloat16
    return pl.pallas_call(
        finish,
        out_shape=[block] * 3,
        in_specs=[vmem] * 5,
        out_specs=[vmem] * 3,
        scratch_shapes=[
            pltpu.VMEM((FF, FF), F32), pltpu.VMEM((FF, FF), F32), pltpu.VMEM((4, 384, W), F32),
            *[pltpu.VMEM((FF, FF), half)] * 6,
            pltpu.VMEM((FF, W), half), pltpu.VMEM((FF, W), half),
            pltpu.VMEM((FF, W), F32), pltpu.VMEM((FF, W), F32),
        ],
        compiler_params=pltpu.CompilerParams(vmem_limit_bytes=52 * 1024 * 1024),
    )(x, gp, gq, weights, new_momentum)


def on_device(partials, momentum, weights):
    new_momentum, x, gp, gq = communicate(partials[0], momentum)
    return tuple(orthogonalize(x, gp, gq, weights, new_momentum))


def solution(mesh):
    return jax.shard_map(
        on_device,
        mesh=mesh,
        in_specs=(P("dp", None, "tp"), P("dp", "tp"), P("dp", "tp")),
        out_specs=(P("dp", "tp"), P("dp", "tp"), P("dp", "tp")),
        check_vma=False,
    )
```

```python
import functools
import math

import jax
import jax.numpy as jnp
from jax import lax
from jax.experimental import pallas as pl
from jax.experimental.pallas import tpu as pltpu
from jax.sharding import PartitionSpec as P

MESH = pl.DeviceIdType.MESH
F32 = jnp.float32
NX, NY, NZ = 4, 2, 8
ROWS = 112
HEAD = 48
TAIL = ROWS - HEAD
W = 256
FAR = (2, 3, 4, 5, 6)
MID = (7, 1)
NEAR = (0,)
D = 7168
FF = 1024
COEF_A = 3.4445
COEF_B = -4.775
COEF_C = 2.0315
MOMENTUM_DECAY = 0.95
LEARN_RATE = 0.02
WEIGHT_DECAY = 0.1
NORM_EPS = 1e-07
NESTEROV_GRAD = 1.0 + MOMENTUM_DECAY


class Ring:
    def __init__(self, n, place, send, recv, send_sem, recv_sem):
        self.n, self.place, self.send, self.recv = n, place, send, recv
        self.send_sem, self.recv_sem = send_sem, recv_sem

    def copy(self, d, k):
        return pltpu.make_async_remote_copy(
            src_ref=self.send.at[d, k], dst_ref=self.recv.at[d, k],
            send_sem=self.send_sem.at[d, k], recv_sem=self.recv_sem.at[d, k],
            device_id=self.place(1 if d == 0 else -1), device_id_type=MESH,
        )

    def offset(self, d, k):
        return (1 if d == 0 else -1) * (self.n // 2 - (k + 1) // 2)

    def issue(self, k, own):
        for d in range(2):
            value = own(self.offset(d, k), (k + d) % 2)
            if k >= 2:
                value = value + self.recv[d, k - 2]
            self.send[d, k] = value
            self.copy(d, k).start()

    def arrive(self, k):
        for d in range(2):
            self.copy(d, k).wait_recv()

    def sent(self):
        for d in range(2):
            for k in range(self.n - 1):
                self.copy(d, k).wait_send()


def split(value):
    high = value.astype(jnp.bfloat16)
    return high, (value - high.astype(F32)).astype(jnp.bfloat16)


def cross(left, right):
    (lh, ll), (rh, rl) = split(left), split(right)
    dims = (((0,), (0,)), ((), ()))
    dot = functools.partial(lax.dot_general, dimension_numbers=dims, preferred_element_type=F32)
    return dot(lh, rh) + (dot(lh, rl) + dot(ll, rh))


def kernel(part_hbm, mom_ref, newm_ref, xg, gp, gq, part, fin, acc_p, acc_q,
           p_send, p_recv, p2_send, p2_recv, qa_send, qa_recv, qb_send, qb_recv, qc_send, qc_recv, q2_send, q2_recv,
           same_recv, side_send, side_recv, cross_send, cross_recv,
           src_p, src_q, one_p, one_q, tot_p, tot_q, two_p, two_q,
           load_sem, p_s, p_r, p2_s, p2_r, qa_s, qa_r, qb_s, qb_r, qc_s, qc_r, q2_s, q2_r, y_s, y_r,
           x_s, x_r, g1p_s, g1p_r, g1q_s, g1q_r, g2p_s, g2p_r, g2q_s, g2q_r,
           ap_s, ap_r, aq_s, aq_r, az_s, az_r, ax_s, ax_r, c_s, c_r):
    dp = lax.axis_index("dp")
    tp = lax.axis_index("tp")
    x, yh, z = dp // 16, (dp // 8) % 2, dp % 8
    lo, core = tp // 2, tp % 2
    sibling = (dp, tp ^ 1)
    pending = []

    def x_at(off):
        return lax.rem(x + off + 2 * NX, NX)

    def z_at(off):
        return lax.rem(z + off + 2 * NZ, NZ)

    def at(dx, dy, dz, other=0):
        return (x_at(dx) * 16 + lax.rem(yh + dy, NY) * 8 + z_at(dz), tp ^ (2 * other))

    def remote(src, dst, send_sem, recv_sem, device):
        return pltpu.make_async_remote_copy(
            src_ref=src, dst_ref=dst, send_sem=send_sem, recv_sem=recv_sem, device_id=device, device_id_type=MESH,
        )

    def begin(copy):
        copy.start()
        pending.append(copy)
        return copy

    def drain():
        for copy in pending:
            copy.wait_send()

    load = pltpu.make_async_copy(part_hbm, part, load_sem)
    load.start()
    peers = [at(dx, dy, 0, o) for dx in range(1, NX) for dy, o in ((0, 0), (1, 0), (0, 1))]
    peers += [at(0, dy, dz, o) for dz in range(1, NZ) for dy, o in ((0, 0), (1, 0), (0, 1))]
    peers += [at(0, 1, 0), at(0, 0, 0, 1), at(0, 1, 0, 1), sibling]
    barrier = pltpu.get_barrier_semaphore()
    for peer in peers:
        pl.semaphore_signal(barrier, inc=1, device_id=peer, device_id_type=MESH)
    load.wait()
    pl.semaphore_wait(barrier, len(peers))

    def along_z(step):
        return at(0, 0, step)

    def along_x(step):
        return at(step, 0, 0)

    p1 = Ring(NZ, along_z, p_send, p_recv, p_s, p_r)
    p2 = Ring(NX, along_x, p2_send, p2_recv, p2_s, p2_r)
    qa = Ring(NX, along_x, qa_send, qa_recv, qa_s, qa_r)
    qb = Ring(NX, along_x, qb_send, qb_recv, qb_s, qb_r)
    qc = Ring(NX, along_x, qc_send, qc_recv, qc_s, qc_r)
    q2 = Ring(NZ, along_z, q2_send, q2_recv, q2_s, q2_r)

    def own_p1(off, half):
        return jnp.stack([part[xx * 16 + half * 8 + z_at(off), :HEAD, :].astype(F32) for xx in range(NX)])

    def own_p2(off, half):
        return acc_p[half, x_at(off)]

    def own_q(rels):
        def own(off, half):
            return jnp.stack([part[x_at(off) * 16 + half * 8 + z_at(rel), HEAD:, :].astype(F32) for rel in rels])
        return own

    own_qa, own_qb, own_qc = own_q(FAR), own_q(MID), own_q(NEAR)

    def own_q2(off, half):
        return acc_q[half, off % NZ]

    def p1_final():
        for half in range(2):
            acc_p[half] = own_p1(0, half) + p_recv[0, 5 + (half + 1) % 2] + p_recv[1, 5 + half]

    def p2_final():
        for half in range(2):
            fin[half, :HEAD] = own_p2(0, half) + p2_recv[0, 1 + (half + 1) % 2] + p2_recv[1, 1 + half]

    def q_final(rels, own, recv):
        for half in range(2):
            value = own(0, half) + recv[0, 1 + (half + 1) % 2] + recv[1, 1 + half]
            for i, rel in enumerate(rels):
                acc_q[half, rel] = value[i]

    def q2_final():
        for half in range(2):
            fin[half, HEAD:] = own_q2(0, half) + q2_recv[0, 5 + (half + 1) % 2] + q2_recv[1, 5 + half]

    def columns_start(i):
        rows = pl.ds(0, HEAD) if i == 0 else pl.ds(HEAD, TAIL)
        begin(remote(fin.at[1 - yh, rows], same_recv.at[rows], y_s.at[0, i], y_r.at[0, i], at(0, 1, 0)))
        cross_send[rows] = NESTEROV_GRAD * fin[1 - yh, rows]
        begin(remote(cross_send.at[rows], cross_recv.at[rows], y_s.at[1, i], y_r.at[1, i], at(0, 1, 0, 1)))
        side_send[rows] = NESTEROV_GRAD * fin[yh, rows] + MOMENTUM_DECAY * MOMENTUM_DECAY * mom_ref[rows]
        begin(remote(side_send.at[rows], side_recv.at[rows], y_s.at[2, i], y_r.at[2, i], at(0, 0, 0, 1)))

    def columns_end(i):
        rows = pl.ds(0, HEAD) if i == 0 else pl.ds(HEAD, TAIL)
        for buf, j in ((same_recv, 0), (cross_recv, 1), (side_recv, 2)):
            remote(buf.at[rows], buf.at[rows], y_s.at[j, i], y_r.at[j, i], sibling).wait_recv()
        gradient = fin[yh, rows] + same_recv[rows]
        new_momentum = MOMENTUM_DECAY * mom_ref[rows] + gradient
        newm_ref[rows] = new_momentum
        xg[tp, rows] = gradient + MOMENTUM_DECAY * new_momentum
        xg[tp ^ 2, rows] = side_recv[rows] + cross_recv[rows]
        for j, slot in enumerate((tp, tp ^ 2)):
            mine = xg.at[slot, rows]
            begin(remote(mine, mine, x_s.at[j, i], x_r.at[j, i], sibling))

    def columns_wait(i):
        rows = pl.ds(0, HEAD) if i == 0 else pl.ds(HEAD, TAIL)
        for j, slot in enumerate((tp ^ 1, tp ^ 3)):
            other = xg.at[slot, rows]
            remote(other, other, x_s.at[j, i], x_r.at[j, i], sibling).wait_recv()

    p1.issue(0, own_p1)
    qa.issue(0, own_qa)
    p1.issue(1, own_p1)
    qa.issue(1, own_qa)
    p1.arrive(0)
    p1.issue(2, own_p1)
    qa.arrive(0)
    qa.issue(2, own_qa)
    p1.arrive(1)
    p1.issue(3, own_p1)
    p1.arrive(2)
    p1.issue(4, own_p1)
    qa.arrive(1)
    qb.issue(0, own_qb)
    qb.issue(1, own_qb)
    p1.arrive(3)
    p1.issue(5, own_p1)
    qa.arrive(2)
    qc.issue(0, own_qc)
    q_final(FAR, own_qa, qa_recv)
    q2.issue(0, own_q2)
    q2.issue(1, own_q2)
    p1.arrive(4)
    p1.issue(6, own_p1)
    qb.arrive(0)
    qb.issue(2, own_qb)
    q2.arrive(0)
    q2.issue(2, own_q2)
    q2.arrive(1)
    q2.issue(3, own_q2)
    qb.arrive(1)
    qc.issue(1, own_qc)
    p1.arrive(5)
    qb.arrive(2)
    q_final(MID, own_qb, qb_recv)
    qc.arrive(0)
    qc.issue(2, own_qc)
    p1.arrive(6)
    p1_final()
    p2.issue(0, own_p2)
    p2.issue(1, own_p2)
    q2.arrive(2)
    q2.issue(4, own_q2)
    q2.arrive(3)
    q2.issue(5, own_q2)
    q2.arrive(4)
    q2.issue(6, own_q2)
    p2.arrive(0)
    p2.issue(2, own_p2)
    qc.arrive(1)
    qc.arrive(2)
    q_final(NEAR, own_qc, qc_recv)
    p2.arrive(1)
    p2.arrive(2)
    p2_final()
    columns_start(0)
    q2.arrive(5)
    q2.arrive(6)
    q2_final()
    columns_start(1)
    columns_end(0)
    for ring in (p1, p2, qa, qb, qc, q2):
        ring.sent()
    columns_end(1)
    columns_wait(0)

    def place(block, rows):
        for xx in range(NX):
            for zz in range(NZ):
                r = rows * ((xx % 2) * 8 + zz)
                yield xx, zz, block[r:r + rows, 128 * (xx // 2):128 * (xx // 2) + 128]

    own_x = xg[tp]
    for xx, zz, value in place(cross(own_x, own_x), 16):
        src_p[zz, xx] = value
    rp = [(dz, remote(src_p.at[z_at(dz)], one_p.at[dz - 1], g1p_s.at[dz - 1], g1p_r.at[dz - 1], along_z(dz)))
          for dz in (4, 3, 5, 2, 6, 1, 7)]
    for _, copy in rp:
        begin(copy)
    columns_wait(1)
    high_x = xg[tp % 2 + 2]
    left = jnp.where(tp < 2, high_x[:, :128], high_x[:, 128:])
    lower = jnp.concatenate([cross(xg[lax.rem(tp + 1, 4)], own_x), cross(left, xg[tp % 2])], axis=0)
    for xx, zz, value in place(lower, 24):
        src_q[xx, zz] = value
    rq = [(dx, remote(src_q.at[x_at(dx)], one_q.at[dx - 1], g1q_s.at[dx - 1], g1q_r.at[dx - 1], along_x(dx)))
          for dx in (2, 1, 3)]
    for _, copy in rq:
        begin(copy)

    for _, copy in rp:
        copy.wait_recv()
    total = src_p[z]
    for i in range(NZ - 1):
        total = total + one_p[i]
    tot_p[...] = total
    second_p, second_q = [], []
    for dx in (2, 1, 3, 0):
        for dy in range(2):
            if dx or dy:
                i = dy * NX + dx
                second_p.append(begin(remote(tot_p.at[x_at(dx)], two_p.at[i], g2p_s.at[i], g2p_r.at[i], at(dx, dy, 0))))
    for _, copy in rq:
        copy.wait_recv()
    total = src_q[x]
    for i in range(NX - 1):
        total = total + one_q[i]
    tot_q[...] = total
    for dz in (4, 3, 5, 2, 6, 1, 7, 0):
        for dy in range(2):
            if dz or dy:
                i = dy * NZ + dz
                second_q.append(begin(remote(tot_q.at[z_at(dz)], two_q.at[i], g2q_s.at[i], g2q_r.at[i], at(0, dy, dz))))

    near_p, near_q = [], []
    for copy in second_p:
        copy.wait_recv()
    total = tot_p[x]
    for i in range(1, 2 * NX):
        total = total + two_p[i]
    mine = gp.at[core, z, x, lo]
    mine[...] = total
    for dx in (2, 1, 3, 0):
        for dy in range(2):
            if dx or dy:
                i = dy * NX + dx
                near_p.append(begin(remote(mine, mine, ap_s.at[i], ap_r.at[i], at(dx, 0, 0, dy))))
    for copy in second_q:
        copy.wait_recv()
    total = tot_q[z]
    for i in range(1, 2 * NZ):
        total = total + two_q[i]
    mine_q = gq.at[core, x, z, lo]
    mine_q[...] = total
    for dz in (4, 3, 5, 2, 6, 1, 7, 0):
        for dy in range(2):
            if dz or dy:
                i = dy * NZ + dz
                near_q.append(begin(remote(mine_q, mine_q, aq_s.at[i], aq_r.at[i], at(0, 0, dz, dy))))

    def pass_z(d, hop, sub):
        sign = 1 if d == 0 else -1
        chunk = gp.at[core, z_at(-sign * hop), pl.ds(2 * sub, 2)]
        return remote(chunk, chunk, az_s.at[d, hop, sub], az_r.at[d, hop, sub], along_z(sign))

    def pass_x(d, part_at):
        sign = 1 if d == 0 else -1
        half = d if part_at != 1 else 1 - d
        chunk = gq.at[core, x if part_at < 2 else x_at(-sign), pl.ds(4 * half, 4)]
        return remote(chunk, chunk, ax_s.at[d, part_at], ax_r.at[d, part_at], along_x(sign))

    shared = []

    def share(chunk):
        i = len(shared)
        shared.append(begin(remote(chunk, chunk, c_s.at[i], c_r.at[i], sibling)))

    for copy in near_p:
        copy.wait_recv()
    for turn in range(2):
        for d in range(2):
            begin(pass_z(d, 0, d ^ turn))
    share(gp.at[core, z])

    def z_step(hop, turn):
        for d in range(2):
            sub = d ^ turn
            pass_z(d, hop, sub).wait_recv()
            if hop < 2 or (hop == 2 and turn == 0):
                begin(pass_z(d, hop + 1, sub))
        for d in range(2):
            sign = 1 if d == 0 else -1
            if hop == 3:
                share(gp.at[core, z_at(4), pl.ds(2 * d, 2)])
            elif turn == 1:
                share(gp.at[core, z_at(-sign * (hop + 1))])

    def x_step(part_at):
        for d in range(2):
            pass_x(d, part_at).wait_recv()
            if part_at == 0:
                begin(pass_x(d, 2))
        for d in range(2):
            sign = 1 if d == 0 else -1
            half = d if part_at != 1 else 1 - d
            share(gq.at[core, x_at(-sign if part_at < 2 else 2), pl.ds(4 * half, 4)])

    z_step(0, 0)
    for copy in near_q:
        copy.wait_recv()
    for part_at in range(2):
        for d in range(2):
            begin(pass_x(d, part_at))
    share(gq.at[core, x])
    z_step(0, 1)
    z_step(1, 0)
    z_step(1, 1)
    x_step(0)
    z_step(2, 0)
    z_step(2, 1)
    x_step(1)
    z_step(3, 0)
    x_step(2)
    for copy in shared:
        copy.wait_recv()
    drain()


def communicate(partials, momentum):
    def ring(n, *block):
        return [pltpu.VMEM((2, n - 1) + block, F32)] * 2

    def sems(*shape):
        return [pltpu.SemaphoreType.DMA(shape)] * 2

    vmem = pl.BlockSpec(memory_space=pltpu.VMEM)
    block = pltpu.VMEM((ROWS, W), F32)
    return pl.pallas_call(
        kernel,
        out_shape=[
            jax.ShapeDtypeStruct((ROWS, W), F32),
            jax.ShapeDtypeStruct((4, ROWS, W), F32),
            jax.ShapeDtypeStruct((2, NZ, NX, 2, 16, 128), F32),
            jax.ShapeDtypeStruct((2, NX, NZ, 2, 24, 128), F32),
        ],
        in_specs=[pl.BlockSpec(memory_space=pl.ANY), vmem],
        out_specs=[vmem] * 4,
        scratch_shapes=[
            pltpu.VMEM((64, ROWS, W), jnp.bfloat16),
            pltpu.VMEM((2, ROWS, W), F32),
            pltpu.VMEM((2, NX, HEAD, W), F32),
            pltpu.VMEM((2, NZ, TAIL, W), F32),
            *ring(NZ, NX, HEAD, W), *ring(NX, HEAD, W),
            *ring(NX, len(FAR), TAIL, W), *ring(NX, len(MID), TAIL, W), *ring(NX, len(NEAR), TAIL, W), *ring(NZ, TAIL, W),
            block, block, block, block, block,
            pltpu.VMEM((NZ, NX, 16, 128), F32), pltpu.VMEM((NX, NZ, 24, 128), F32),
            pltpu.VMEM((NZ - 1, NX, 16, 128), F32), pltpu.VMEM((NX - 1, NZ, 24, 128), F32),
            pltpu.VMEM((NX, 16, 128), F32), pltpu.VMEM((NZ, 24, 128), F32),
            pltpu.VMEM((2 * NX, 16, 128), F32), pltpu.VMEM((2 * NZ, 24, 128), F32),
            pltpu.SemaphoreType.DMA,
            *sems(2, NZ - 1), *sems(2, NX - 1), *sems(2, NX - 1), *sems(2, NX - 1), *sems(2, NX - 1), *sems(2, NZ - 1),
            *sems(3, 2), *sems(2, 2),
            *sems(NZ - 1), *sems(NX - 1), *sems(2 * NX), *sems(2 * NZ),
            *sems(2 * NX), *sems(2 * NZ), *sems(2, 4, 2), *sems(2, 3), *sems(18),
        ],
        compiler_params=pltpu.CompilerParams(collective_id=0, has_side_effects=True, vmem_limit_bytes=52 * 1024 * 1024),
    )(partials.reshape(64, ROWS, W), momentum)


def finish(x_ref, gp, gq, w_ref, m_ref, update_ref, neww_ref, newm_ref,
           a, a2, low, ah, al, a2h, a2l, mh, ml, vh, vl, y, w):
    tp = lax.axis_index("tp")
    newm_ref[...] = m_ref[...]
    trace = jnp.zeros((1, 1), F32)
    for t in range(4):
        core, lo, base = t % 2, t // 2, 256 * t
        for xx in range(NX):
            for zz in range(NZ):
                r, c = (xx % 2) * 8 + zz, xx // 2
                a[base + 16 * r:base + 16 * r + 16, base + 128 * c:base + 128 * c + 128] = gp[core, zz, xx, lo]
                low[t, 24 * r:24 * r + 24, 128 * c:128 * c + 128] = gq[core, xx, zz, lo]
        block = a[base:base + 256, base:base + 256]
        on_diag = lax.broadcasted_iota(jnp.int32, (256, 256), 0) == lax.broadcasted_iota(jnp.int32, (256, 256), 1)
        trace = trace + jnp.sum(jnp.where(on_diag, block, 0.0), keepdims=True)
    for t in range(4):
        nxt = (t + 1) % 4
        side = low[t, :256, :]
        a[256 * nxt:256 * nxt + 256, 256 * t:256 * t + 256] = side
        a[256 * t:256 * t + 256, 256 * nxt:256 * nxt + 256] = side.T
        far = low[t, 256:, :]
        i, j = 256 * (t % 2 + 2) + 128 * (t // 2), 256 * (t % 2)
        a[i:i + 128, j:j + 256] = far
        a[j:j + 256, i:i + 128] = far.T
    inverse = 1.0 / (jnp.sqrt(trace) + NORM_EPS)
    scale = inverse * inverse

    def tiles(body):
        def step(i, carry):
            body(pl.ds(pl.multiple_of(i * 256, 256), 256), i)
            return carry
        lax.fori_loop(0, 4, step, 0)

    def prepare(rows, _):
        block = a[rows, :] * scale
        a[rows, :] = block
        ah[rows, :], al[rows, :] = split(block)

    tiles(prepare)

    def dot3(lh, ll, rh, rl):
        dot = functools.partial(jnp.dot, preferred_element_type=F32)
        return dot(lh, rh) + (dot(lh, rl) + dot(ll, rh))

    for i in range(4):
        rows = slice(256 * i, 256 * i + 256)
        for j in range(i, 4):
            cols = slice(256 * j, 256 * j + 256)
            block = dot3(ah[rows, :], al[rows, :], ah[:, cols], al[:, cols])
            a2[rows, cols] = block
            if j > i:
                a2[cols, rows] = block.T

    def mix(rows, i):
        square = a2[rows, :]
        a2h[rows, :], a2l[rows, :] = split(square)
        same = lax.broadcasted_iota(jnp.int32, (256, FF), 0) + i * 256 == lax.broadcasted_iota(jnp.int32, (256, FF), 1)
        value = COEF_B * a[rows, :] + COEF_C * square + jnp.where(same, COEF_A, 0.0)
        mh[rows, :], ml[rows, :] = split(value)

    tiles(mix)

    own = pl.ds(pl.multiple_of(tp * 256, 256), 256)

    def eye(i):
        return jnp.where(
            lax.broadcasted_iota(jnp.int32, (256, W), 0) + i * 256 == lax.broadcasted_iota(jnp.int32, (256, W), 1) + tp * 256,
            COEF_A, 0.0,
        )

    def start(rows, i):
        w[rows, :] = a[rows, own]
        value = COEF_B * a[rows, own] + COEF_C * a2[rows, own] + eye(i)
        vh[rows, :], vl[rows, :] = split(value)

    tiles(start)

    def product(high, lowp, after):
        def body(rows, i):
            y[rows, :] = after(dot3(high[rows, :], lowp[rows, :], vh[...], vl[...]), rows, i)
        tiles(body)

        def again(rows, i):
            vh[rows, :], vl[rows, :] = split(y[rows, :])
        tiles(again)

    product(mh, ml, lambda value, rows, i: value)
    product(a2h, a2l, lambda value, rows, i: COEF_B * w[rows, :] + COEF_C * value)
    product(mh, ml, lambda value, rows, i: value)
    product(mh, ml, lambda value, rows, i: value + eye(i))

    xh, xl = split(jnp.concatenate([x_ref[t] for t in range(4)], axis=1) * inverse)
    result = jnp.zeros((ROWS, W), F32)
    for t in range(4):
        cols = slice(256 * t, 256 * t + 256)
        once_h, once_l = split(dot3(xh, xl, mh[:, cols], ml[:, cols]))
        result = result + dot3(once_h, once_l, vh[cols, :], vl[cols, :])
    update = 0.2 * math.sqrt(max(D, FF)) * result
    update_ref[...] = update
    neww_ref[...] = w_ref[...] - LEARN_RATE * (update + WEIGHT_DECAY * w_ref[...])


def orthogonalize(x, gp, gq, weights, new_momentum):
    vmem = pl.BlockSpec(memory_space=pltpu.VMEM)
    block = jax.ShapeDtypeStruct((ROWS, W), F32)
    half = jnp.bfloat16
    return pl.pallas_call(
        finish,
        out_shape=[block] * 3,
        in_specs=[vmem] * 5,
        out_specs=[vmem] * 3,
        scratch_shapes=[
            pltpu.VMEM((FF, FF), F32), pltpu.VMEM((FF, FF), F32), pltpu.VMEM((4, 384, W), F32),
            *[pltpu.VMEM((FF, FF), half)] * 6,
            pltpu.VMEM((FF, W), half), pltpu.VMEM((FF, W), half),
            pltpu.VMEM((FF, W), F32), pltpu.VMEM((FF, W), F32),
        ],
        compiler_params=pltpu.CompilerParams(vmem_limit_bytes=52 * 1024 * 1024),
    )(x, gp, gq, weights, new_momentum)


def on_device(partials, momentum, weights):
    new_momentum, x, gp, gq = communicate(partials[0], momentum)
    return tuple(orthogonalize(x, gp, gq, weights, new_momentum))


def solution(mesh):
    return jax.shard_map(
        on_device,
        mesh=mesh,
        in_specs=(P("dp", None, "tp"), P("dp", "tp"), P("dp", "tp")),
        out_specs=(P("dp", "tp"), P("dp", "tp"), P("dp", "tp")),
        check_vma=False,
    )
```

```python
import functools
import math

import jax
import jax.numpy as jnp
from jax import lax
from jax.experimental import pallas as pl
from jax.experimental.pallas import tpu as pltpu
from jax.sharding import PartitionSpec as P

MESH = pl.DeviceIdType.MESH
F32 = jnp.float32
NX, NY, NZ = 4, 2, 8
ROWS = 112
HEAD = 48
TAIL = ROWS - HEAD
W = 256
FAR = (2, 3, 4, 5, 6)
MID = (7, 1)
NEAR = (0,)
D = 7168
FF = 1024
COEF_A = 3.4445
COEF_B = -4.775
COEF_C = 2.0315
MOMENTUM_DECAY = 0.95
LEARN_RATE = 0.02
WEIGHT_DECAY = 0.1
NORM_EPS = 1e-07
NESTEROV_GRAD = 1.0 + MOMENTUM_DECAY


class Ring:
    def __init__(self, n, place, send, recv, send_sem, recv_sem):
        self.n, self.place, self.send, self.recv = n, place, send, recv
        self.send_sem, self.recv_sem = send_sem, recv_sem

    def copy(self, d, k):
        return pltpu.make_async_remote_copy(
            src_ref=self.send.at[d, k], dst_ref=self.recv.at[d, k],
            send_sem=self.send_sem.at[d, k], recv_sem=self.recv_sem.at[d, k],
            device_id=self.place(1 if d == 0 else -1), device_id_type=MESH,
        )

    def offset(self, d, k):
        return (1 if d == 0 else -1) * (self.n // 2 - (k + 1) // 2)

    def issue(self, k, own):
        for d in range(2):
            value = own(self.offset(d, k), (k + d) % 2)
            if k >= 2:
                value = value + self.recv[d, k - 2]
            self.send[d, k] = value
            self.copy(d, k).start()

    def arrive(self, k):
        for d in range(2):
            self.copy(d, k).wait_recv()

    def sent(self):
        for d in range(2):
            for k in range(self.n - 1):
                self.copy(d, k).wait_send()


def split(value):
    high = value.astype(jnp.bfloat16)
    return high, (value - high.astype(F32)).astype(jnp.bfloat16)


def cross(left, right):
    (lh, ll), (rh, rl) = split(left), split(right)
    dims = (((0,), (0,)), ((), ()))
    dot = functools.partial(lax.dot_general, dimension_numbers=dims, preferred_element_type=F32)
    return dot(lh, rh) + (dot(lh, rl) + dot(ll, rh))


def kernel(part_hbm, mom_hbm, newm_ref, xg, gp, gq, part, mom_ref, fin, acc_p, acc_q,
           p_send, p_recv, p2_send, p2_recv, qa_send, qa_recv, qb_send, qb_recv, qc_send, qc_recv, q2_send, q2_recv,
           same_recv, side_send, side_recv, cross_send, cross_recv,
           src_p, src_q, one_p, one_q, tot_p, tot_q, two_p, two_q,
           load_sem, p_s, p_r, p2_s, p2_r, qa_s, qa_r, qb_s, qb_r, qc_s, qc_r, q2_s, q2_r, y_s, y_r,
           x_s, x_r, g1p_s, g1p_r, g1q_s, g1q_r, g2p_s, g2p_r, g2q_s, g2q_r,
           ap_s, ap_r, aq_s, aq_r, az_s, az_r, ax_s, ax_r, c_s, c_r):
    dp = lax.axis_index("dp")
    tp = lax.axis_index("tp")
    x, yh, z = dp // 16, (dp // 8) % 2, dp % 8
    lo, core = tp // 2, tp % 2
    sibling = (dp, tp ^ 1)
    pending = []

    def x_at(off):
        return lax.rem(x + off + 2 * NX, NX)

    def z_at(off):
        return lax.rem(z + off + 2 * NZ, NZ)

    def at(dx, dy, dz, other=0):
        return (x_at(dx) * 16 + lax.rem(yh + dy, NY) * 8 + z_at(dz), tp ^ (2 * other))

    def remote(src, dst, send_sem, recv_sem, device):
        return pltpu.make_async_remote_copy(
            src_ref=src, dst_ref=dst, send_sem=send_sem, recv_sem=recv_sem, device_id=device, device_id_type=MESH,
        )

    def begin(copy):
        copy.start()
        pending.append(copy)
        return copy

    def drain():
        for copy in pending:
            copy.wait_send()

    load = pltpu.make_async_copy(part_hbm, part, load_sem.at[0])
    load.start()
    load_momentum = pltpu.make_async_copy(mom_hbm, mom_ref, load_sem.at[1])
    load_momentum.start()
    peers = [at(dx, dy, 0, o) for dx in range(1, NX) for dy, o in ((0, 0), (1, 0), (0, 1))]
    peers += [at(0, dy, dz, o) for dz in range(1, NZ) for dy, o in ((0, 0), (1, 0), (0, 1))]
    peers += [at(0, 1, 0), at(0, 0, 0, 1), at(0, 1, 0, 1), sibling]
    barrier = pltpu.get_barrier_semaphore()
    for peer in peers:
        pl.semaphore_signal(barrier, inc=1, device_id=peer, device_id_type=MESH)
    load.wait()
    load_momentum.wait()
    pl.semaphore_wait(barrier, len(peers))

    def along_z(step):
        return at(0, 0, step)

    def along_x(step):
        return at(step, 0, 0)

    p1 = Ring(NZ, along_z, p_send, p_recv, p_s, p_r)
    p2 = Ring(NX, along_x, p2_send, p2_recv, p2_s, p2_r)
    qa = Ring(NX, along_x, qa_send, qa_recv, qa_s, qa_r)
    qb = Ring(NX, along_x, qb_send, qb_recv, qb_s, qb_r)
    qc = Ring(NX, along_x, qc_send, qc_recv, qc_s, qc_r)
    q2 = Ring(NZ, along_z, q2_send, q2_recv, q2_s, q2_r)

    def own_p1(off, half):
        return jnp.stack([part[xx * 16 + half * 8 + z_at(off), :HEAD, :].astype(F32) for xx in range(NX)])

    def own_p2(off, half):
        return acc_p[half, x_at(off)]

    def own_q(rels):
        def own(off, half):
            return jnp.stack([part[x_at(off) * 16 + half * 8 + z_at(rel), HEAD:, :].astype(F32) for rel in rels])
        return own

    own_qa, own_qb, own_qc = own_q(FAR), own_q(MID), own_q(NEAR)

    def own_q2(off, half):
        return acc_q[half, off % NZ]

    def p1_final():
        for half in range(2):
            acc_p[half] = own_p1(0, half) + p_recv[0, 5 + (half + 1) % 2] + p_recv[1, 5 + half]

    def p2_final():
        for half in range(2):
            fin[half, :HEAD] = own_p2(0, half) + p2_recv[0, 1 + (half + 1) % 2] + p2_recv[1, 1 + half]

    def q_final(rels, own, recv):
        for half in range(2):
            value = own(0, half) + recv[0, 1 + (half + 1) % 2] + recv[1, 1 + half]
            for i, rel in enumerate(rels):
                acc_q[half, rel] = value[i]

    def q2_final():
        for half in range(2):
            fin[half, HEAD:] = own_q2(0, half) + q2_recv[0, 5 + (half + 1) % 2] + q2_recv[1, 5 + half]

    def columns_start(i):
        rows = pl.ds(0, HEAD) if i == 0 else pl.ds(HEAD, TAIL)
        begin(remote(fin.at[1 - yh, rows], same_recv.at[rows], y_s.at[0, i], y_r.at[0, i], at(0, 1, 0)))
        cross_send[rows] = NESTEROV_GRAD * fin[1 - yh, rows]
        begin(remote(cross_send.at[rows], cross_recv.at[rows], y_s.at[1, i], y_r.at[1, i], at(0, 1, 0, 1)))
        side_send[rows] = NESTEROV_GRAD * fin[yh, rows] + MOMENTUM_DECAY * MOMENTUM_DECAY * mom_ref[rows]
        begin(remote(side_send.at[rows], side_recv.at[rows], y_s.at[2, i], y_r.at[2, i], at(0, 0, 0, 1)))

    def columns_end(i):
        rows = pl.ds(0, HEAD) if i == 0 else pl.ds(HEAD, TAIL)
        for buf, j in ((same_recv, 0), (cross_recv, 1), (side_recv, 2)):
            remote(buf.at[rows], buf.at[rows], y_s.at[j, i], y_r.at[j, i], sibling).wait_recv()
        gradient = fin[yh, rows] + same_recv[rows]
        new_momentum = MOMENTUM_DECAY * mom_ref[rows] + gradient
        newm_ref[rows] = new_momentum
        xg[tp, rows] = gradient + MOMENTUM_DECAY * new_momentum
        xg[tp ^ 2, rows] = side_recv[rows] + cross_recv[rows]
        for j, slot in enumerate((tp, tp ^ 2)):
            mine = xg.at[slot, rows]
            begin(remote(mine, mine, x_s.at[j, i], x_r.at[j, i], sibling))

    def columns_wait(i):
        rows = pl.ds(0, HEAD) if i == 0 else pl.ds(HEAD, TAIL)
        for j, slot in enumerate((tp ^ 1, tp ^ 3)):
            other = xg.at[slot, rows]
            remote(other, other, x_s.at[j, i], x_r.at[j, i], sibling).wait_recv()

    p1.issue(0, own_p1)
    qa.issue(0, own_qa)
    p1.issue(1, own_p1)
    qa.issue(1, own_qa)
    p1.arrive(0)
    p1.issue(2, own_p1)
    qa.arrive(0)
    qa.issue(2, own_qa)
    p1.arrive(1)
    p1.issue(3, own_p1)
    p1.arrive(2)
    p1.issue(4, own_p1)
    qa.arrive(1)
    qb.issue(0, own_qb)
    qb.issue(1, own_qb)
    p1.arrive(3)
    p1.issue(5, own_p1)
    qa.arrive(2)
    qc.issue(0, own_qc)
    q_final(FAR, own_qa, qa_recv)
    q2.issue(0, own_q2)
    q2.issue(1, own_q2)
    p1.arrive(4)
    p1.issue(6, own_p1)
    qb.arrive(0)
    qb.issue(2, own_qb)
    q2.arrive(0)
    q2.issue(2, own_q2)
    q2.arrive(1)
    q2.issue(3, own_q2)
    qb.arrive(1)
    qc.issue(1, own_qc)
    p1.arrive(5)
    qb.arrive(2)
    q_final(MID, own_qb, qb_recv)
    qc.arrive(0)
    qc.issue(2, own_qc)
    p1.arrive(6)
    p1_final()
    p2.issue(0, own_p2)
    p2.issue(1, own_p2)
    q2.arrive(2)
    q2.issue(4, own_q2)
    q2.arrive(3)
    q2.issue(5, own_q2)
    q2.arrive(4)
    q2.issue(6, own_q2)
    p2.arrive(0)
    p2.issue(2, own_p2)
    qc.arrive(1)
    qc.arrive(2)
    q_final(NEAR, own_qc, qc_recv)
    p2.arrive(1)
    p2.arrive(2)
    p2_final()
    columns_start(0)
    q2.arrive(5)
    q2.arrive(6)
    q2_final()
    columns_start(1)
    columns_end(0)
    for ring in (p1, p2, qa, qb, qc, q2):
        ring.sent()
    columns_end(1)
    columns_wait(0)

    def place(block, rows):
        for xx in range(NX):
            for zz in range(NZ):
                r = rows * ((xx % 2) * 8 + zz)
                yield xx, zz, block[r:r + rows, 128 * (xx // 2):128 * (xx // 2) + 128]

    own_x = xg[tp]
    for xx, zz, value in place(cross(own_x, own_x), 16):
        src_p[zz, xx] = value
    rp = [(dz, remote(src_p.at[z_at(dz)], one_p.at[dz - 1], g1p_s.at[dz - 1], g1p_r.at[dz - 1], along_z(dz)))
          for dz in (4, 3, 5, 2, 6, 1, 7)]
    for _, copy in rp:
        begin(copy)
    columns_wait(1)
    high_x = xg[tp % 2 + 2]
    left = jnp.where(tp < 2, high_x[:, :128], high_x[:, 128:])
    lower = jnp.concatenate([cross(xg[lax.rem(tp + 1, 4)], own_x), cross(left, xg[tp % 2])], axis=0)
    for xx, zz, value in place(lower, 24):
        src_q[xx, zz] = value
    rq = [(dx, remote(src_q.at[x_at(dx)], one_q.at[dx - 1], g1q_s.at[dx - 1], g1q_r.at[dx - 1], along_x(dx)))
          for dx in (2, 1, 3)]
    for _, copy in rq:
        begin(copy)

    for _, copy in rp:
        copy.wait_recv()
    total = src_p[z]
    for i in range(NZ - 1):
        total = total + one_p[i]
    tot_p[...] = total
    second_p, second_q = [], []
    for dx in (2, 1, 3, 0):
        for dy in range(2):
            if dx or dy:
                i = dy * NX + dx
                second_p.append(begin(remote(tot_p.at[x_at(dx)], two_p.at[i], g2p_s.at[i], g2p_r.at[i], at(dx, dy, 0))))
    for _, copy in rq:
        copy.wait_recv()
    total = src_q[x]
    for i in range(NX - 1):
        total = total + one_q[i]
    tot_q[...] = total
    for dz in (4, 3, 5, 2, 6, 1, 7, 0):
        for dy in range(2):
            if dz or dy:
                i = dy * NZ + dz
                second_q.append(begin(remote(tot_q.at[z_at(dz)], two_q.at[i], g2q_s.at[i], g2q_r.at[i], at(0, dy, dz))))

    near_p, near_q = [], []
    for copy in second_p:
        copy.wait_recv()
    total = tot_p[x]
    for i in range(1, 2 * NX):
        total = total + two_p[i]
    mine = gp.at[core, z, x, lo]
    mine[...] = total
    for dx in (2, 1, 3, 0):
        for dy in range(2):
            if dx or dy:
                i = dy * NX + dx
                near_p.append(begin(remote(mine, mine, ap_s.at[i], ap_r.at[i], at(dx, 0, 0, dy))))
    for copy in second_q:
        copy.wait_recv()
    total = tot_q[z]
    for i in range(1, 2 * NZ):
        total = total + two_q[i]
    mine_q = gq.at[core, x, z, lo]
    mine_q[...] = total
    for dz in (4, 3, 5, 2, 6, 1, 7, 0):
        for dy in range(2):
            if dz or dy:
                i = dy * NZ + dz
                near_q.append(begin(remote(mine_q, mine_q, aq_s.at[i], aq_r.at[i], at(0, 0, dz, dy))))

    def pass_z(d, hop, sub):
        sign = 1 if d == 0 else -1
        chunk = gp.at[core, z_at(-sign * hop), pl.ds(2 * sub, 2)]
        return remote(chunk, chunk, az_s.at[d, hop, sub], az_r.at[d, hop, sub], along_z(sign))

    def pass_x(d, part_at):
        sign = 1 if d == 0 else -1
        half = d if part_at != 1 else 1 - d
        chunk = gq.at[core, x if part_at < 2 else x_at(-sign), pl.ds(4 * half, 4)]
        return remote(chunk, chunk, ax_s.at[d, part_at], ax_r.at[d, part_at], along_x(sign))

    shared = []

    def share(chunk):
        i = len(shared)
        shared.append(begin(remote(chunk, chunk, c_s.at[i], c_r.at[i], sibling)))

    for copy in near_p:
        copy.wait_recv()
    for turn in range(2):
        for d in range(2):
            begin(pass_z(d, 0, d ^ turn))
    share(gp.at[core, z])

    def z_step(hop, turn):
        for d in range(2):
            sub = d ^ turn
            pass_z(d, hop, sub).wait_recv()
            if hop < 2 or (hop == 2 and turn == 0):
                begin(pass_z(d, hop + 1, sub))
        for d in range(2):
            sign = 1 if d == 0 else -1
            if hop == 3:
                share(gp.at[core, z_at(4), pl.ds(2 * d, 2)])
            elif turn == 1:
                share(gp.at[core, z_at(-sign * (hop + 1))])

    def x_step(part_at):
        for d in range(2):
            pass_x(d, part_at).wait_recv()
            if part_at == 0:
                begin(pass_x(d, 2))
        for d in range(2):
            sign = 1 if d == 0 else -1
            half = d if part_at != 1 else 1 - d
            share(gq.at[core, x_at(-sign if part_at < 2 else 2), pl.ds(4 * half, 4)])

    z_step(0, 0)
    for copy in near_q:
        copy.wait_recv()
    for part_at in range(2):
        for d in range(2):
            begin(pass_x(d, part_at))
    share(gq.at[core, x])
    z_step(0, 1)
    z_step(1, 0)
    z_step(1, 1)
    x_step(0)
    z_step(2, 0)
    z_step(2, 1)
    x_step(1)
    z_step(3, 0)
    x_step(2)
    for copy in shared:
        copy.wait_recv()
    drain()


def communicate(partials, momentum):
    def ring(n, *block):
        return [pltpu.VMEM((2, n - 1) + block, F32)] * 2

    def sems(*shape):
        return [pltpu.SemaphoreType.DMA(shape)] * 2

    vmem = pl.BlockSpec(memory_space=pltpu.VMEM)
    block = pltpu.VMEM((ROWS, W), F32)
    return pl.pallas_call(
        kernel,
        out_shape=[
            jax.ShapeDtypeStruct((ROWS, W), F32),
            jax.ShapeDtypeStruct((4, ROWS, W), F32),
            jax.ShapeDtypeStruct((2, NZ, NX, 2, 16, 128), F32),
            jax.ShapeDtypeStruct((2, NX, NZ, 2, 24, 128), F32),
        ],
        in_specs=[pl.BlockSpec(memory_space=pltpu.HBM)] * 2,
        out_specs=[vmem] * 4,
        scratch_shapes=[
            pltpu.VMEM((64, ROWS, W), jnp.bfloat16),
            block,
            pltpu.VMEM((2, ROWS, W), F32),
            pltpu.VMEM((2, NX, HEAD, W), F32),
            pltpu.VMEM((2, NZ, TAIL, W), F32),
            *ring(NZ, NX, HEAD, W), *ring(NX, HEAD, W),
            *ring(NX, len(FAR), TAIL, W), *ring(NX, len(MID), TAIL, W), *ring(NX, len(NEAR), TAIL, W), *ring(NZ, TAIL, W),
            block, block, block, block, block,
            pltpu.VMEM((NZ, NX, 16, 128), F32), pltpu.VMEM((NX, NZ, 24, 128), F32),
            pltpu.VMEM((NZ - 1, NX, 16, 128), F32), pltpu.VMEM((NX - 1, NZ, 24, 128), F32),
            pltpu.VMEM((NX, 16, 128), F32), pltpu.VMEM((NZ, 24, 128), F32),
            pltpu.VMEM((2 * NX, 16, 128), F32), pltpu.VMEM((2 * NZ, 24, 128), F32),
            pltpu.SemaphoreType.DMA((2,)),
            *sems(2, NZ - 1), *sems(2, NX - 1), *sems(2, NX - 1), *sems(2, NX - 1), *sems(2, NX - 1), *sems(2, NZ - 1),
            *sems(3, 2), *sems(2, 2),
            *sems(NZ - 1), *sems(NX - 1), *sems(2 * NX), *sems(2 * NZ),
            *sems(2 * NX), *sems(2 * NZ), *sems(2, 4, 2), *sems(2, 3), *sems(18),
        ],
        compiler_params=pltpu.CompilerParams(collective_id=0, has_side_effects=True, vmem_limit_bytes=49 * 1024 * 1024),
    )(partials.reshape(64, ROWS, W), momentum)


def finish(x_ref, gp, gq, w_ref, m_ref, update_ref, neww_ref, newm_ref,
           a, a2, low, ah, al, a2h, a2l, mh, ml, mine):
    tp = lax.axis_index("tp")
    newm_ref[...] = m_ref[...]
    trace = jnp.zeros((1, 1), F32)
    for t in range(4):
        core, lo, base = t % 2, t // 2, 256 * t
        for xx in range(NX):
            for zz in range(NZ):
                r, c = (xx % 2) * 8 + zz, xx // 2
                a[base + 16 * r:base + 16 * r + 16, base + 128 * c:base + 128 * c + 128] = gp[core, zz, xx, lo]
                low[t, 24 * r:24 * r + 24, 128 * c:128 * c + 128] = gq[core, xx, zz, lo]
        block = a[base:base + 256, base:base + 256]
        on_diag = lax.broadcasted_iota(jnp.int32, (256, 256), 0) == lax.broadcasted_iota(jnp.int32, (256, 256), 1)
        trace = trace + jnp.sum(jnp.where(on_diag, block, 0.0), keepdims=True)
    for t in range(4):
        nxt = (t + 1) % 4
        side = low[t, :256, :]
        a[256 * nxt:256 * nxt + 256, 256 * t:256 * t + 256] = side
        a[256 * t:256 * t + 256, 256 * nxt:256 * nxt + 256] = side.T
        far = low[t, 256:, :]
        i, j = 256 * (t % 2 + 2) + 128 * (t // 2), 256 * (t % 2)
        a[i:i + 128, j:j + 256] = far
        a[j:j + 256, i:i + 128] = far.T
    inverse = 1.0 / (jnp.sqrt(trace) + NORM_EPS)
    scale = inverse * inverse

    def tiles(body):
        def step(i, carry):
            body(pl.ds(pl.multiple_of(i * 256, 256), 256), i)
            return carry
        lax.fori_loop(0, 4, step, 0)

    def prepare(rows, _):
        block = a[rows, :] * scale
        a[rows, :] = block
        ah[rows, :], al[rows, :] = split(block)

    tiles(prepare)

    def dot3(lh, ll, rh, rl):
        dot = functools.partial(jnp.dot, preferred_element_type=F32)
        return dot(lh, rh) + (dot(lh, rl) + dot(ll, rh))

    for i in range(4):
        rows = slice(256 * i, 256 * i + 256)
        for j in range(i, 4):
            cols = slice(256 * j, 256 * j + 256)
            block = dot3(ah[rows, :], al[rows, :], ah[:, cols], al[:, cols])
            a2[rows, cols] = block
            if j > i:
                a2[cols, rows] = block.T

    def mix(rows, i):
        square = a2[rows, :]
        a2h[rows, :], a2l[rows, :] = split(square)
        same = lax.broadcasted_iota(jnp.int32, (256, FF), 0) + i * 256 == lax.broadcasted_iota(jnp.int32, (256, FF), 1)
        value = COEF_B * a[rows, :] + COEF_C * square + jnp.where(same, COEF_A, 0.0)
        mh[rows, :], ml[rows, :] = split(value)

    tiles(mix)

    def times(x, high, lowp, cols=None):
        xh, xl = split(x)
        both = jnp.concatenate([xh, xl], axis=0)
        parts = []
        for at in [cols] if cols is not None else [slice(256 * j, 256 * j + 256) for j in range(4)]:
            first = jnp.dot(both, high[:, at], preferred_element_type=F32)
            second = jnp.dot(xh, lowp[:, at], preferred_element_type=F32)
            parts.append(first[:ROWS] + (first[ROWS:] + second))
        return parts[0] if cols is not None else jnp.concatenate(parts, axis=1)

    own = pl.ds(pl.multiple_of(tp * 256, 256), 256)
    start = jnp.concatenate([x_ref[t] for t in range(4)], axis=1) * inverse
    one = times(start, mh, ml)
    for t in range(4):
        mine[t] = one[:, 256 * t:256 * t + 256]
    turned = times(times(one, mh, ml), mh, ml)
    result = COEF_A * mine[tp] + COEF_B * times(turned, ah, al, own)
    result = result + COEF_C * times(times(times(turned, a2h, a2l), mh, ml), mh, ml, own)
    update = 0.2 * math.sqrt(max(D, FF)) * result
    update_ref[...] = update
    neww_ref[...] = w_ref[...] - LEARN_RATE * (update + WEIGHT_DECAY * w_ref[...])


def orthogonalize(x, gp, gq, weights, new_momentum):
    vmem = pl.BlockSpec(memory_space=pltpu.VMEM)
    block = jax.ShapeDtypeStruct((ROWS, W), F32)
    half = jnp.bfloat16
    return pl.pallas_call(
        finish,
        out_shape=[block] * 3,
        in_specs=[vmem] * 5,
        out_specs=[vmem] * 3,
        scratch_shapes=[
            pltpu.VMEM((FF, FF), F32), pltpu.VMEM((FF, FF), F32), pltpu.VMEM((4, 384, W), F32),
            *[pltpu.VMEM((FF, FF), half)] * 6,
            pltpu.VMEM((4, ROWS, W), F32),
        ],
        compiler_params=pltpu.CompilerParams(vmem_limit_bytes=40 * 1024 * 1024),
    )(x, gp, gq, weights, new_momentum)


def on_device(partials, momentum, weights):
    new_momentum, x, gp, gq = communicate(partials[0], momentum)
    return tuple(orthogonalize(x, gp, gq, weights, new_momentum))


def solution(mesh):
    return jax.shard_map(
        on_device,
        mesh=mesh,
        in_specs=(P("dp", None, "tp"), P("dp", "tp"), P("dp", "tp")),
        out_specs=(P("dp", "tp"), P("dp", "tp"), P("dp", "tp")),
        check_vma=False,
    )
```

```python
import functools
import math

import jax
import jax.numpy as jnp
from jax import lax
from jax.experimental import pallas as pl
from jax.experimental.pallas import tpu as pltpu
from jax.sharding import PartitionSpec as P

MESH = pl.DeviceIdType.MESH
F32 = jnp.float32
NX, NY, NZ = 4, 2, 8
ROWS = 112
HEAD = 48
EARLY = 16
TAIL = ROWS - HEAD
HEAD_RING = HEAD - EARLY
TAIL_RING = TAIL - EARLY
Z_ORDER = (4, 3, 5, 2, 6, 1, 7, 0)
W = 256
X_ORDER = (2, 1, 3, 0)
Z_ORDER = (4, 3, 5, 2, 6, 1, 7, 0)
X_GROUPS = ((0, 1), (1, 2), (3, 1))
Z_GROUPS = ((0, 1), (1, 2), (3, 2), (5, 2), (7, 1))
EARLY_Z = Z_GROUPS
UNIT = 0.026
PRIORITY = ("y", "q4", "p1", "rp", "q0", "rqz", "rpx", "q2", "qz", "p0", "p2", "q1", "px", "rq", "q3")
BACKLOG = 6.0
LATE, FAR_LATE = 2.0, 3.0
D = 7168
FF = 1024
COEF_A = 3.4445
COEF_B = -4.775
COEF_C = 2.0315
MOMENTUM_DECAY = 0.95
LEARN_RATE = 0.02
WEIGHT_DECAY = 0.1
NORM_EPS = 1e-07
NESTEROV_GRAD = 1.0 + MOMENTUM_DECAY


def plan(priority, backlog):
    link, cost, needs = {}, {}, {}

    def add(name, k, axis, rows, after=()):
        link[name, k], cost[name, k], needs[name, k] = axis, rows * UNIT, set(after)

    def chain(name, k):
        return {(name, k - 2)} if k >= 2 else set()

    for g, count in enumerate((1, 2, 1)):
        for k in range(NZ - 1):
            add("p%d" % g, k, "z", count * HEAD_RING, chain("p%d" % g, k))
    for g, count in enumerate((1, 2, 2, 2, 1)):
        for k in range(NX - 1):
            add("q%d" % g, k, "x", count * TAIL_RING, chain("q%d" % g, k))
    for k in range(NX - 1):
        g = (k + 1) // 2
        add("px", k, "x", HEAD_RING, chain("px", k) | {("p%d" % g, 5), ("p%d" % g, 6)})
    for k in range(NZ - 1):
        g = (k + 1) // 2
        add("qz", k, "z", TAIL_RING, chain("qz", k) | {("q%d" % g, 1), ("q%d" % g, 2)})
    if EARLY:
        for i in range(9):
            add("y", i, "y", EARLY * (8 if i < 4 else 4 * EARLY_Z[i - 4][1]))
        for k in range(NZ - 1):
            add("rp", k, "z", 2 * EARLY, chain("rp", k) | {("y", 4 + (k + 1) // 2)})
        for k in range(NX - 1):
            add("rq", k, "x", 4 * EARLY, chain("rq", k) | ({("y", 0)} if k == 0 else {("y", 1), ("y", 2)}))
        add("rpx", 0, "x", 2 * EARLY, {("rp", 5), ("rp", 6), ("y", 8)})
        add("rqz", 0, "z", 8 * EARLY, {("rq", 1), ("rq", 2), ("y", 3)})
    free, now, flying, arrived, waiting, order = dict.fromkeys("xyz", 0.0), 0.0, [], set(), list(link), []
    while waiting or flying:
        for axis in "zxy":
            while free[axis] - now < backlog:
                ready = [t for t in waiting if link[t] == axis and needs[t] <= arrived]
                if not ready:
                    break
                pick = min(ready, key=lambda t: (priority.index(t[0]), t[1]))
                waiting.remove(pick)
                free[axis] = max(free[axis], now) + cost[pick]
                late = FAR_LATE if pick[0] in ("rqz", "rpx", "y") else LATE
                flying.append((free[axis] + late, pick))
                order.append(("issue",) + pick)
        when, pick = min(flying)
        flying.remove((when, pick))
        now = max(now, when) + 0.15
        arrived.add(pick)
        order.append(("arrive",) + pick)
    return order, now


class Ring:
    def __init__(self, n, place, own, send, recv, send_sem, recv_sem, span=None):
        self.n, self.place, self.own, self.span = n, place, own, span
        self.send, self.recv, self.send_sem, self.recv_sem = send, recv, send_sem, recv_sem

    def at(self, d, k):
        return (d, k) if self.span is None else (d, k, pl.ds(*self.span))

    def copy(self, d, k):
        return pltpu.make_async_remote_copy(
            src_ref=self.send.at[self.at(d, k)], dst_ref=self.recv.at[self.at(d, k)],
            send_sem=self.send_sem.at[d, k], recv_sem=self.recv_sem.at[d, k],
            device_id=self.place(1 if d == 0 else -1), device_id_type=MESH,
        )

    def offset(self, d, k):
        return (1 if d == 0 else -1) * (self.n // 2 - (k + 1) // 2)

    def issue(self, k):
        for d in range(2):
            value = self.own(self.offset(d, k), (k + d) % 2)
            if k >= 2:
                value = value + self.recv[self.at(d, k - 2)]
            self.send[self.at(d, k)] = value
            self.copy(d, k).start()

    def arrive(self, k):
        for d in range(2):
            self.copy(d, k).wait_recv()

    def total(self, half):
        first, last = self.n - 3 + (half + 1) % 2, self.n - 3 + half
        return self.own(0, half) + self.recv[self.at(0, first)] + self.recv[self.at(1, last)]

    def sent(self):
        for d in range(2):
            for k in range(self.n - 1):
                self.copy(d, k).wait_send()


def split(value):
    high = value.astype(jnp.bfloat16)
    return high, (value - high.astype(F32)).astype(jnp.bfloat16)


def cross(left, right):
    (lh, ll), (rh, rl) = split(left), split(right)
    dims = (((0,), (0,)), ((), ()))
    dot = functools.partial(lax.dot_general, dimension_numbers=dims, preferred_element_type=F32)
    return dot(lh, rh) + (dot(lh, rl) + dot(ll, rh))


def kernel(part_hbm, mom_hbm, newm_ref, xg, gp, gq, part, mom_ref, fin, acc_p, acc_q,
           ry_send, ry_recv, rx_send, rx_recv, rp_send, rp_recv, rq_send, rq_recv, acc_rp, acc_rq, rp2_recv, rq2_recv,
           p_send, p_recv, px_send, px_recv, q_send, q_recv, qz_send, qz_recv,
           same_recv, side_send, side_recv, cross_send, cross_recv,
           src_p, src_q, one_p, one_q, tot_p, tot_q, two_p, two_q,
           load_sem, p_s, p_r, px_s, px_r, q_s, q_r, qz_s, qz_r, y_s, y_r,
           early_s, early_r, rp_s, rp_r, rq_s, rq_r, rp2_s, rp2_r, rq2_s, rq2_r,
           x_s, x_r, g1p_s, g1p_r, g1q_s, g1q_r, g2p_s, g2p_r, g2q_s, g2q_r,
           ap_s, ap_r, aq_s, aq_r, az_s, az_r, ax_s, ax_r, c_s, c_r):
    dp = lax.axis_index("dp")
    tp = lax.axis_index("tp")
    x, yh, z = dp // 16, (dp // 8) % 2, dp % 8
    lo, core = tp // 2, tp % 2
    sibling = (dp, tp ^ 1)
    pending = []

    def x_at(off):
        return lax.rem(x + off + 2 * NX, NX)

    def z_at(off):
        return lax.rem(z + off + 2 * NZ, NZ)

    def at(dx, dy, dz, other=0):
        return (x_at(dx) * 16 + lax.rem(yh + dy, NY) * 8 + z_at(dz), tp ^ (2 * other))

    def remote(src, dst, send_sem, recv_sem, device):
        return pltpu.make_async_remote_copy(
            src_ref=src, dst_ref=dst, send_sem=send_sem, recv_sem=recv_sem, device_id=device, device_id_type=MESH,
        )

    def begin(copy):
        copy.start()
        pending.append(copy)
        return copy

    def drain():
        for copy in pending:
            copy.wait_send()

    load = pltpu.make_async_copy(part_hbm, part, load_sem.at[0])
    load.start()
    load_momentum = pltpu.make_async_copy(mom_hbm, mom_ref, load_sem.at[1])
    load_momentum.start()
    peers = [at(dx, dy, 0, o) for dx in range(1, NX) for dy, o in ((0, 0), (1, 0), (0, 1))]
    peers += [at(0, dy, dz, o) for dz in range(1, NZ) for dy, o in ((0, 0), (1, 0), (0, 1))]
    peers += [at(0, 1, 0), at(0, 0, 0, 1), at(0, 1, 0, 1), sibling]
    barrier = pltpu.get_barrier_semaphore()
    for peer in peers:
        pl.semaphore_signal(barrier, inc=1, device_id=peer, device_id_type=MESH)
    load.wait()
    load_momentum.wait()
    pl.semaphore_wait(barrier, len(peers))

    def along_z(step):
        return at(0, 0, step)

    def along_x(step):
        return at(step, 0, 0)

    def early_rows(xx, yy, zz, first):
        return part[xx * 16 + yy * 8 + zz, first:first + EARLY, :].astype(F32)

    def early_copy(i):
        if i < 4:
            off = X_ORDER[i]
            src, dst = rx_send.at[off], rx_recv.at[off]
        else:
            span = pl.ds(*EARLY_Z[i - 4])
            src, dst = ry_send.at[span], ry_recv.at[span]
        return remote(src, dst, early_s.at[i], early_r.at[i], at(0, 1, 0))

    def early_issue(i):
        if i < 4:
            off = X_ORDER[i]
            for rel in range(NZ):
                rx_send[off, rel] = early_rows(x_at(off), 1 - yh, z_at(rel), ROWS - EARLY)
        else:
            first, count = EARLY_Z[i - 4]
            for j in range(first, first + count):
                for xx in range(NX):
                    ry_send[j, xx] = early_rows(xx, 1 - yh, z_at(Z_ORDER[j]), HEAD_RING)
        begin(early_copy(i))

    def early_arrive(i):
        early_copy(i).wait_recv()

    def own_rp(off, half):
        j = Z_ORDER.index(off % NZ)
        return jnp.stack([early_rows(xx, yh, z_at(off), HEAD_RING) + ry_recv[j, xx] for xx in (2 * half, 2 * half + 1)])

    def own_rq(off, half):
        return jnp.stack([early_rows(x_at(off), yh, z_at(rel), ROWS - EARLY) + rx_recv[off % NX, rel]
                          for rel in range(4 * half, 4 * half + 4)])

    def rp2_copy(dx):
        return remote(acc_rp.at[x_at(dx)], rp2_recv.at[dx - 1], rp2_s.at[dx - 1], rp2_r.at[dx - 1], along_x(dx))

    def rq2_copy(dz):
        return remote(acc_rq.at[dz], rq2_recv.at[dz - 1], rq2_s.at[dz - 1], rq2_r.at[dz - 1], along_z(dz))

    def early_total(acc, copies, recv, rows):
        total = acc
        for i, copy in enumerate(copies):
            copy.wait_recv()
            total = total + recv[i]
        fin[yh, rows] = total

    def own_p(group):
        first, count = X_GROUPS[group]

        def own(off, half):
            xs = [x_at(rel) for rel in X_ORDER[first:first + count]]
            return jnp.stack([part[xx * 16 + half * 8 + z_at(off), :HEAD_RING, :].astype(F32) for xx in xs])
        return own

    def own_q(group):
        first, count = Z_GROUPS[group]

        def own(off, half):
            zs = [z_at(rel) for rel in Z_ORDER[first:first + count]]
            return jnp.stack([part[x_at(off) * 16 + half * 8 + zz, HEAD:HEAD + TAIL_RING, :].astype(F32) for zz in zs])
        return own

    def own_px(off, half):
        return acc_p[half, X_ORDER.index(off % NX)]

    def own_qz(off, half):
        return acc_q[half, Z_ORDER.index(off % NZ)]

    rings = {
        "px": Ring(NX, along_x, own_px, px_send, px_recv, px_s, px_r),
        "qz": Ring(NZ, along_z, own_qz, qz_send, qz_recv, qz_s, qz_r),
        "rp": Ring(NZ, along_z, own_rp, rp_send, rp_recv, rp_s, rp_r),
        "rq": Ring(NX, along_x, own_rq, rq_send, rq_recv, rq_s, rq_r),
    }
    for g, span in enumerate(X_GROUPS):
        rings["p%d" % g] = Ring(NZ, along_z, own_p(g), p_send, p_recv, p_s.at[g], p_r.at[g], span)
    for g, span in enumerate(Z_GROUPS):
        rings["q%d" % g] = Ring(NX, along_x, own_q(g), q_send, q_recv, q_s.at[g], q_r.at[g], span)

    def final(name):
        if name == "columns0":
            early_total(acc_rp[x], [rp2_copy(dx) for dx in (1, 2, 3)], rp2_recv, pl.ds(HEAD_RING, EARLY))
            for half in range(2):
                fin[half, :HEAD_RING] = rings["px"].total(half)
            columns_start(0)
        elif name == "columns1":
            early_total(acc_rq[0], [rq2_copy(dz) for dz in range(1, NZ)], rq2_recv, pl.ds(ROWS - EARLY, EARLY))
            for half in range(2):
                fin[half, HEAD:HEAD + TAIL_RING] = rings["qz"].total(half)
            columns_start(1)
        elif name == "rpx":
            for half in range(2):
                acc_rp[pl.ds(2 * half, 2)] = rings["rp"].total(half)
            for dx in (2, 1, 3):
                begin(rp2_copy(dx))
        elif name == "rqz":
            for half in range(2):
                acc_rq[pl.ds(4 * half, 4)] = rings["rq"].total(half)
            for dz in (4, 3, 5, 2, 6, 1, 7):
                begin(rq2_copy(dz))
        else:
            acc = acc_p if name[0] == "p" else acc_q
            for half in range(2):
                acc[half, pl.ds(*rings[name].span)] = rings[name].total(half)

    def columns_start(i):
        rows = pl.ds(0, HEAD) if i == 0 else pl.ds(HEAD, TAIL)
        half = pl.ds(0, HEAD_RING) if i == 0 else pl.ds(HEAD, TAIL_RING)
        begin(remote(fin.at[1 - yh, half], same_recv.at[half], y_s.at[0, i], y_r.at[0, i], at(0, 1, 0)))
        cross_send[half] = NESTEROV_GRAD * fin[1 - yh, half]
        begin(remote(cross_send.at[half], cross_recv.at[half], y_s.at[1, i], y_r.at[1, i], at(0, 1, 0, 1)))
        side_send[rows] = NESTEROV_GRAD * fin[yh, rows] + MOMENTUM_DECAY * MOMENTUM_DECAY * mom_ref[rows]
        begin(remote(side_send.at[rows], side_recv.at[rows], y_s.at[2, i], y_r.at[2, i], at(0, 0, 0, 1)))

    def columns_end(i):
        rows = pl.ds(0, HEAD) if i == 0 else pl.ds(HEAD, TAIL)
        half = pl.ds(0, HEAD_RING) if i == 0 else pl.ds(HEAD, TAIL_RING)
        for buf, j, span in ((same_recv, 0, half), (cross_recv, 1, half), (side_recv, 2, rows)):
            remote(buf.at[span], buf.at[span], y_s.at[j, i], y_r.at[j, i], sibling).wait_recv()
        gradient = fin[yh, rows] + same_recv[rows]
        new_momentum = MOMENTUM_DECAY * mom_ref[rows] + gradient
        newm_ref[rows] = new_momentum
        xg[tp, rows] = gradient + MOMENTUM_DECAY * new_momentum
        xg[tp ^ 2, rows] = side_recv[rows] + cross_recv[rows]
        for j, slot in enumerate((tp, tp ^ 2)):
            mine = xg.at[slot, rows]
            begin(remote(mine, mine, x_s.at[j, i], x_r.at[j, i], sibling))

    def columns_wait(i):
        rows = pl.ds(0, HEAD) if i == 0 else pl.ds(HEAD, TAIL)
        for j, slot in enumerate((tp ^ 1, tp ^ 3)):
            other = xg.at[slot, rows]
            remote(other, other, x_s.at[j, i], x_r.at[j, i], sibling).wait_recv()

    for rows in (pl.ds(HEAD_RING, EARLY), pl.ds(ROWS - EARLY, EARLY)):
        same_recv[rows] = jnp.zeros((EARLY, W), F32)
        cross_recv[rows] = jnp.zeros((EARLY, W), F32)
    order, _ = plan(PRIORITY, BACKLOG)
    left = {name: {(name, ring.n - 3), (name, ring.n - 2)} for name, ring in rings.items() if ring.span is not None}
    left["columns0"] = {("px", 1), ("px", 2), ("rpx", 0), ("p2", 5), ("p2", 6)}
    left["columns1"] = {("qz", 5), ("qz", 6), ("rqz", 0), ("q4", 1), ("q4", 2)}
    for what, name, k in order:
        if what == "issue":
            if name == "y":
                early_issue(k)
            elif name in ("rpx", "rqz"):
                final(name)
            else:
                rings[name].issue(k)
            continue
        if name == "y":
            early_arrive(k)
        elif name in rings:
            rings[name].arrive(k)
        for key in [key for key in left if (name, k) in left[key]]:
            left[key].discard((name, k))
            if not left[key]:
                final(key)
    columns_end(0)
    for ring in rings.values():
        ring.sent()
    columns_end(1)
    columns_wait(0)

    def place(block, rows):
        for xx in range(NX):
            for zz in range(NZ):
                r = rows * ((xx % 2) * 8 + zz)
                yield xx, zz, block[r:r + rows, 128 * (xx // 2):128 * (xx // 2) + 128]

    own_x = xg[tp]
    for xx, zz, value in place(cross(own_x, own_x), 16):
        src_p[zz, xx] = value
    rp = [(dz, remote(src_p.at[z_at(dz)], one_p.at[dz - 1], g1p_s.at[dz - 1], g1p_r.at[dz - 1], along_z(dz)))
          for dz in (4, 3, 5, 2, 6, 1, 7)]
    for _, copy in rp:
        begin(copy)
    columns_wait(1)
    high_x = xg[tp % 2 + 2]
    left = jnp.where(tp < 2, high_x[:, :128], high_x[:, 128:])
    lower = jnp.concatenate([cross(xg[lax.rem(tp + 1, 4)], own_x), cross(left, xg[tp % 2])], axis=0)
    for xx, zz, value in place(lower, 24):
        src_q[xx, zz] = value
    rq = [(dx, remote(src_q.at[x_at(dx)], one_q.at[dx - 1], g1q_s.at[dx - 1], g1q_r.at[dx - 1], along_x(dx)))
          for dx in (2, 1, 3)]
    for _, copy in rq:
        begin(copy)

    for _, copy in rp:
        copy.wait_recv()
    total = src_p[z]
    for i in range(NZ - 1):
        total = total + one_p[i]
    tot_p[...] = total
    second_p, second_q = [], []
    for dx in (2, 1, 3, 0):
        for dy in range(2):
            if dx or dy:
                i = dy * NX + dx
                second_p.append(begin(remote(tot_p.at[x_at(dx)], two_p.at[i], g2p_s.at[i], g2p_r.at[i], at(dx, dy, 0))))
    for _, copy in rq:
        copy.wait_recv()
    total = src_q[x]
    for i in range(NX - 1):
        total = total + one_q[i]
    tot_q[...] = total
    for dz in (4, 3, 5, 2, 6, 1, 7, 0):
        for dy in range(2):
            if dz or dy:
                i = dy * NZ + dz
                second_q.append(begin(remote(tot_q.at[z_at(dz)], two_q.at[i], g2q_s.at[i], g2q_r.at[i], at(0, dy, dz))))

    near_p, near_q = [], []
    for copy in second_p:
        copy.wait_recv()
    total = tot_p[x]
    for i in range(1, 2 * NX):
        total = total + two_p[i]
    mine = gp.at[core, z, x, lo]
    mine[...] = total
    for dx in (2, 1, 3, 0):
        for dy in range(2):
            if dx or dy:
                i = dy * NX + dx
                near_p.append(begin(remote(mine, mine, ap_s.at[i], ap_r.at[i], at(dx, 0, 0, dy))))
    for copy in second_q:
        copy.wait_recv()
    total = tot_q[z]
    for i in range(1, 2 * NZ):
        total = total + two_q[i]
    mine_q = gq.at[core, x, z, lo]
    mine_q[...] = total
    for dz in (4, 3, 5, 2, 6, 1, 7, 0):
        for dy in range(2):
            if dz or dy:
                i = dy * NZ + dz
                near_q.append(begin(remote(mine_q, mine_q, aq_s.at[i], aq_r.at[i], at(0, 0, dz, dy))))

    def pass_z(d, hop, sub):
        sign = 1 if d == 0 else -1
        chunk = gp.at[core, z_at(-sign * hop), pl.ds(2 * sub, 2)]
        return remote(chunk, chunk, az_s.at[d, hop, sub], az_r.at[d, hop, sub], along_z(sign))

    def pass_x(d, part_at):
        sign = 1 if d == 0 else -1
        half = d if part_at != 1 else 1 - d
        chunk = gq.at[core, x if part_at < 2 else x_at(-sign), pl.ds(4 * half, 4)]
        return remote(chunk, chunk, ax_s.at[d, part_at], ax_r.at[d, part_at], along_x(sign))

    shared = []

    def share(chunk):
        i = len(shared)
        shared.append(begin(remote(chunk, chunk, c_s.at[i], c_r.at[i], sibling)))

    for copy in near_p:
        copy.wait_recv()
    for turn in range(2):
        for d in range(2):
            begin(pass_z(d, 0, d ^ turn))
    share(gp.at[core, z])

    def z_step(hop, turn):
        for d in range(2):
            sub = d ^ turn
            pass_z(d, hop, sub).wait_recv()
            if hop < 2 or (hop == 2 and turn == 0):
                begin(pass_z(d, hop + 1, sub))
        for d in range(2):
            sign = 1 if d == 0 else -1
            if hop == 3:
                share(gp.at[core, z_at(4), pl.ds(2 * d, 2)])
            elif turn == 1:
                share(gp.at[core, z_at(-sign * (hop + 1))])

    def x_step(part_at):
        for d in range(2):
            pass_x(d, part_at).wait_recv()
            if part_at == 0:
                begin(pass_x(d, 2))
        for d in range(2):
            sign = 1 if d == 0 else -1
            half = d if part_at != 1 else 1 - d
            share(gq.at[core, x_at(-sign if part_at < 2 else 2), pl.ds(4 * half, 4)])

    z_step(0, 0)
    for copy in near_q:
        copy.wait_recv()
    for part_at in range(2):
        for d in range(2):
            begin(pass_x(d, part_at))
    share(gq.at[core, x])
    z_step(0, 1)
    z_step(1, 0)
    z_step(1, 1)
    x_step(0)
    z_step(2, 0)
    z_step(2, 1)
    x_step(1)
    z_step(3, 0)
    x_step(2)
    for copy in shared:
        copy.wait_recv()
    drain()


def communicate(partials, momentum):
    def ring(n, *block):
        return [pltpu.VMEM((2, n - 1) + block, F32)] * 2

    def sems(*shape):
        return [pltpu.SemaphoreType.DMA(shape)] * 2

    vmem = pl.BlockSpec(memory_space=pltpu.VMEM)
    block = pltpu.VMEM((ROWS, W), F32)
    return pl.pallas_call(
        kernel,
        out_shape=[
            jax.ShapeDtypeStruct((ROWS, W), F32),
            jax.ShapeDtypeStruct((4, ROWS, W), F32),
            jax.ShapeDtypeStruct((2, NZ, NX, 2, 16, 128), F32),
            jax.ShapeDtypeStruct((2, NX, NZ, 2, 24, 128), F32),
        ],
        in_specs=[pl.BlockSpec(memory_space=pltpu.HBM)] * 2,
        out_specs=[vmem] * 4,
        scratch_shapes=[
            pltpu.VMEM((64, ROWS, W), jnp.bfloat16),
            block,
            pltpu.VMEM((2, ROWS, W), F32),
            pltpu.VMEM((2, NX, HEAD_RING, W), F32),
            pltpu.VMEM((2, NZ, TAIL_RING, W), F32),
            *[pltpu.VMEM((NZ, NX, EARLY, W), F32)] * 2, *[pltpu.VMEM((NX, NZ, EARLY, W), F32)] * 2,
            *ring(NZ, 2, EARLY, W), *ring(NX, 4, EARLY, W),
            pltpu.VMEM((NX, EARLY, W), F32), pltpu.VMEM((NZ, EARLY, W), F32),
            pltpu.VMEM((NX - 1, EARLY, W), F32), pltpu.VMEM((NZ - 1, EARLY, W), F32),
            *ring(NZ, NX, HEAD_RING, W), *ring(NX, HEAD_RING, W), *ring(NX, NZ, TAIL_RING, W), *ring(NZ, TAIL_RING, W),
            block, block, block, block, block,
            pltpu.VMEM((NZ, NX, 16, 128), F32), pltpu.VMEM((NX, NZ, 24, 128), F32),
            pltpu.VMEM((NZ - 1, NX, 16, 128), F32), pltpu.VMEM((NX - 1, NZ, 24, 128), F32),
            pltpu.VMEM((NX, 16, 128), F32), pltpu.VMEM((NZ, 24, 128), F32),
            pltpu.VMEM((2 * NX, 16, 128), F32), pltpu.VMEM((2 * NZ, 24, 128), F32),
            pltpu.SemaphoreType.DMA((2,)),
            *sems(3, 2, NZ - 1), *sems(2, NX - 1), *sems(5, 2, NX - 1), *sems(2, NZ - 1),
            *sems(3, 2),
            *sems(9), *sems(2, NZ - 1), *sems(2, NX - 1), *sems(NX - 1), *sems(NZ - 1),
            *sems(2, 2),
            *sems(NZ - 1), *sems(NX - 1), *sems(2 * NX), *sems(2 * NZ),
            *sems(2 * NX), *sems(2 * NZ), *sems(2, 4, 2), *sems(2, 3), *sems(18),
        ],
        compiler_params=pltpu.CompilerParams(collective_id=0, has_side_effects=True, vmem_limit_bytes=49 * 1024 * 1024),
    )(partials.reshape(64, ROWS, W), momentum)


def finish(x_ref, gp, gq, w_ref, m_ref, update_ref, neww_ref, newm_ref,
           a, a2, low, ah, al, a2h, a2l, mh, ml, mine):
    tp = lax.axis_index("tp")
    newm_ref[...] = m_ref[...]
    trace = jnp.zeros((1, 1), F32)
    for t in range(4):
        core, lo, base = t % 2, t // 2, 256 * t
        for xx in range(NX):
            for zz in range(NZ):
                r, c = (xx % 2) * 8 + zz, xx // 2
                a[base + 16 * r:base + 16 * r + 16, base + 128 * c:base + 128 * c + 128] = gp[core, zz, xx, lo]
                low[t, 24 * r:24 * r + 24, 128 * c:128 * c + 128] = gq[core, xx, zz, lo]
        block = a[base:base + 256, base:base + 256]
        on_diag = lax.broadcasted_iota(jnp.int32, (256, 256), 0) == lax.broadcasted_iota(jnp.int32, (256, 256), 1)
        trace = trace + jnp.sum(jnp.where(on_diag, block, 0.0), keepdims=True)
    for t in range(4):
        nxt = (t + 1) % 4
        side = low[t, :256, :]
        a[256 * nxt:256 * nxt + 256, 256 * t:256 * t + 256] = side
        a[256 * t:256 * t + 256, 256 * nxt:256 * nxt + 256] = side.T
        far = low[t, 256:, :]
        i, j = 256 * (t % 2 + 2) + 128 * (t // 2), 256 * (t % 2)
        a[i:i + 128, j:j + 256] = far
        a[j:j + 256, i:i + 128] = far.T
    inverse = 1.0 / (jnp.sqrt(trace) + NORM_EPS)
    scale = inverse * inverse

    def tiles(body):
        def step(i, carry):
            body(pl.ds(pl.multiple_of(i * 256, 256), 256), i)
            return carry
        lax.fori_loop(0, 4, step, 0)

    def prepare(rows, _):
        block = a[rows, :] * scale
        a[rows, :] = block
        ah[rows, :], al[rows, :] = split(block)

    tiles(prepare)

    def dot3(lh, ll, rh, rl):
        dot = functools.partial(jnp.dot, preferred_element_type=F32)
        return dot(lh, rh) + (dot(lh, rl) + dot(ll, rh))

    for i in range(4):
        rows = slice(256 * i, 256 * i + 256)
        for j in range(i, 4):
            cols = slice(256 * j, 256 * j + 256)
            block = dot3(ah[rows, :], al[rows, :], ah[:, cols], al[:, cols])
            a2[rows, cols] = block
            if j > i:
                a2[cols, rows] = block.T

    def mix(rows, i):
        square = a2[rows, :]
        a2h[rows, :], a2l[rows, :] = split(square)
        same = lax.broadcasted_iota(jnp.int32, (256, FF), 0) + i * 256 == lax.broadcasted_iota(jnp.int32, (256, FF), 1)
        value = COEF_B * a[rows, :] + COEF_C * square + jnp.where(same, COEF_A, 0.0)
        mh[rows, :], ml[rows, :] = split(value)

    tiles(mix)

    def times(x, high, lowp, cols=None):
        xh, xl = split(x)
        both = jnp.concatenate([xh, xl], axis=0)
        parts = []
        for at in [cols] if cols is not None else [slice(256 * j, 256 * j + 256) for j in range(4)]:
            first = jnp.dot(both, high[:, at], preferred_element_type=F32)
            second = jnp.dot(xh, lowp[:, at], preferred_element_type=F32)
            parts.append(first[:ROWS] + (first[ROWS:] + second))
        return parts[0] if cols is not None else jnp.concatenate(parts, axis=1)

    own = pl.ds(pl.multiple_of(tp * 256, 256), 256)
    start = jnp.concatenate([x_ref[t] for t in range(4)], axis=1) * inverse
    one = times(start, mh, ml)
    for t in range(4):
        mine[t] = one[:, 256 * t:256 * t + 256]
    turned = times(times(one, mh, ml), mh, ml)
    result = COEF_A * mine[tp] + COEF_B * times(turned, ah, al, own)
    result = result + COEF_C * times(times(times(turned, a2h, a2l), mh, ml), mh, ml, own)
    update = 0.2 * math.sqrt(max(D, FF)) * result
    update_ref[...] = update
    neww_ref[...] = w_ref[...] - LEARN_RATE * (update + WEIGHT_DECAY * w_ref[...])


def orthogonalize(x, gp, gq, weights, new_momentum):
    vmem = pl.BlockSpec(memory_space=pltpu.VMEM)
    block = jax.ShapeDtypeStruct((ROWS, W), F32)
    half = jnp.bfloat16
    return pl.pallas_call(
        finish,
        out_shape=[block] * 3,
        in_specs=[vmem] * 5,
        out_specs=[vmem] * 3,
        scratch_shapes=[
            pltpu.VMEM((FF, FF), F32), pltpu.VMEM((FF, FF), F32), pltpu.VMEM((4, 384, W), F32),
            *[pltpu.VMEM((FF, FF), half)] * 6,
            pltpu.VMEM((4, ROWS, W), F32),
        ],
        compiler_params=pltpu.CompilerParams(vmem_limit_bytes=40 * 1024 * 1024),
    )(x, gp, gq, weights, new_momentum)


def on_device(partials, momentum, weights):
    new_momentum, x, gp, gq = communicate(partials[0], momentum)
    return tuple(orthogonalize(x, gp, gq, weights, new_momentum))


def solution(mesh):
    return jax.shard_map(
        on_device,
        mesh=mesh,
        in_specs=(P("dp", None, "tp"), P("dp", "tp"), P("dp", "tp")),
        out_specs=(P("dp", "tp"), P("dp", "tp"), P("dp", "tp")),
        check_vma=False,
    )
```

```python
import functools
import math

import jax
import jax.numpy as jnp
from jax import lax
from jax.experimental import pallas as pl
from jax.experimental.pallas import tpu as pltpu
from jax.sharding import PartitionSpec as P

MESH = pl.DeviceIdType.MESH
F32 = jnp.float32
NX, NY, NZ = 4, 2, 8
ROWS = 112
HEAD = 48
EARLY = 16
TAIL = ROWS - HEAD
HEAD_RING = HEAD - EARLY
TAIL_RING = TAIL - EARLY
W = 256
X_ORDER = (2, 1, 3, 0)
Z_ORDER = (4, 3, 5, 2, 6, 1, 7, 0)
X_GROUPS = ((0, 1), (1, 2), (3, 1))
Z_GROUPS = ((0, 1), (1, 2), (3, 2), (5, 2), (7, 1))
EARLY_Z = Z_GROUPS
UNIT = 0.026
PRIORITY = ("y", "q4", "p1", "rp", "q0", "rqz", "rpx", "q2", "qz", "p0", "p2", "q1", "px", "rq", "q3")
BACKLOG = 6.0
LATE, FAR_LATE = 2.0, 3.0
D = 7168
FF = 1024
COEF_A = 3.4445
COEF_B = -4.775
COEF_C = 2.0315
MOMENTUM_DECAY = 0.95
LEARN_RATE = 0.02
WEIGHT_DECAY = 0.1
NORM_EPS = 1e-07
NESTEROV_GRAD = 1.0 + MOMENTUM_DECAY


def plan(priority, backlog):
    link, cost, needs = {}, {}, {}

    def add(name, k, axis, rows, after=()):
        link[name, k], cost[name, k], needs[name, k] = axis, rows * UNIT, set(after)

    def chain(name, k):
        return {(name, k - 2)} if k >= 2 else set()

    for g, count in enumerate((1, 2, 1)):
        for k in range(NZ - 1):
            add("p%d" % g, k, "z", count * HEAD_RING, chain("p%d" % g, k))
    for g, count in enumerate((1, 2, 2, 2, 1)):
        for k in range(NX - 1):
            add("q%d" % g, k, "x", count * TAIL_RING, chain("q%d" % g, k))
    for k in range(NX - 1):
        g = (k + 1) // 2
        add("px", k, "x", HEAD_RING, chain("px", k) | {("p%d" % g, 5), ("p%d" % g, 6)})
    for k in range(NZ - 1):
        g = (k + 1) // 2
        add("qz", k, "z", TAIL_RING, chain("qz", k) | {("q%d" % g, 1), ("q%d" % g, 2)})
    if EARLY:
        for i in range(9):
            add("y", i, "y", EARLY * (8 if i < 4 else 4 * EARLY_Z[i - 4][1]))
        for k in range(NZ - 1):
            add("rp", k, "z", 2 * EARLY, chain("rp", k) | {("y", 4 + (k + 1) // 2)})
        for k in range(NX - 1):
            add("rq", k, "x", 4 * EARLY, chain("rq", k) | ({("y", 0)} if k == 0 else {("y", 1), ("y", 2)}))
        add("rpx", 0, "x", 2 * EARLY, {("rp", 5), ("rp", 6), ("y", 8)})
        add("rqz", 0, "z", 8 * EARLY, {("rq", 1), ("rq", 2), ("y", 3)})
    free, now, flying, arrived, waiting, order = dict.fromkeys("xyz", 0.0), 0.0, [], set(), list(link), []
    while waiting or flying:
        for axis in "zxy":
            while free[axis] - now < backlog:
                ready = [t for t in waiting if link[t] == axis and needs[t] <= arrived]
                if not ready:
                    break
                pick = min(ready, key=lambda t: (priority.index(t[0]), t[1]))
                waiting.remove(pick)
                free[axis] = max(free[axis], now) + cost[pick]
                late = FAR_LATE if pick[0] in ("rqz", "rpx", "y") else LATE
                flying.append((free[axis] + late, pick))
                order.append(("issue",) + pick)
        when, pick = min(flying)
        flying.remove((when, pick))
        now = max(now, when) + 0.15
        arrived.add(pick)
        order.append(("arrive",) + pick)
    return order, now


class Ring:
    def __init__(self, n, place, own, send, recv, send_sem, recv_sem, span=None):
        self.n, self.place, self.own, self.span = n, place, own, span
        self.send, self.recv, self.send_sem, self.recv_sem = send, recv, send_sem, recv_sem

    def at(self, d, k):
        return (d, k) if self.span is None else (d, k, pl.ds(*self.span))

    def copy(self, d, k):
        return pltpu.make_async_remote_copy(
            src_ref=self.send.at[self.at(d, k)], dst_ref=self.recv.at[self.at(d, k)],
            send_sem=self.send_sem.at[d, k], recv_sem=self.recv_sem.at[d, k],
            device_id=self.place(1 if d == 0 else -1), device_id_type=MESH,
        )

    def offset(self, d, k):
        return (1 if d == 0 else -1) * (self.n // 2 - (k + 1) // 2)

    def issue(self, k):
        for d in range(2):
            value = self.own(self.offset(d, k), (k + d) % 2)
            if k >= 2:
                value = value + self.recv[self.at(d, k - 2)]
            self.send[self.at(d, k)] = value
            self.copy(d, k).start()

    def arrive(self, k):
        for d in range(2):
            self.copy(d, k).wait_recv()

    def total(self, half):
        first, last = self.n - 3 + (half + 1) % 2, self.n - 3 + half
        return self.own(0, half) + self.recv[self.at(0, first)] + self.recv[self.at(1, last)]

    def sent(self):
        for d in range(2):
            for k in range(self.n - 1):
                self.copy(d, k).wait_send()


def split(value):
    high = value.astype(jnp.bfloat16)
    return high, (value - high.astype(F32)).astype(jnp.bfloat16)


def cross(left, right):
    (lh, ll), (rh, rl) = split(left), split(right)
    dims = (((0,), (0,)), ((), ()))
    dot = functools.partial(lax.dot_general, dimension_numbers=dims, preferred_element_type=F32)
    return dot(lh, rh) + (dot(lh, rl) + dot(ll, rh))


def kernel(part_hbm, mom_hbm, newm_ref, xg, gp, gq, part, mom_ref, fin, acc_p, acc_q,
           ry_send, ry_recv, rx_send, rx_recv, rp_send, rp_recv, rq_send, rq_recv, acc_rp, acc_rq, rp2_recv, rq2_recv,
           p_send, p_recv, px_send, px_recv, q_send, q_recv, qz_send, qz_recv,
           same_recv, side_send, side_recv, cross_send, cross_recv,
           src_p, src_q, one_p, one_q, tot_p, tot_q, two_p, two_q,
           load_sem, p_s, p_r, px_s, px_r, q_s, q_r, qz_s, qz_r, y_s, y_r,
           early_s, early_r, rp_s, rp_r, rq_s, rq_r, rp2_s, rp2_r, rq2_s, rq2_r,
           x_s, x_r, g1p_s, g1p_r, g1q_s, g1q_r, g2p_s, g2p_r, g2q_s, g2q_r,
           ap_s, ap_r, aq_s, aq_r, az_s, az_r, ax_s, ax_r, c_s, c_r):
    dp = lax.axis_index("dp")
    tp = lax.axis_index("tp")
    x, yh, z = dp // 16, (dp // 8) % 2, dp % 8
    lo, core = tp // 2, tp % 2
    sibling = (dp, tp ^ 1)
    pending = []

    def x_at(off):
        return lax.rem(x + off + 2 * NX, NX)

    def z_at(off):
        return lax.rem(z + off + 2 * NZ, NZ)

    def at(dx, dy, dz, other=0):
        return (x_at(dx) * 16 + lax.rem(yh + dy, NY) * 8 + z_at(dz), tp ^ (2 * other))

    def remote(src, dst, send_sem, recv_sem, device):
        return pltpu.make_async_remote_copy(
            src_ref=src, dst_ref=dst, send_sem=send_sem, recv_sem=recv_sem, device_id=device, device_id_type=MESH,
        )

    def begin(copy):
        copy.start()
        pending.append(copy)
        return copy

    def drain():
        for copy in pending:
            copy.wait_send()

    load = pltpu.make_async_copy(part_hbm, part, load_sem.at[0])
    load.start()
    load_momentum = pltpu.make_async_copy(mom_hbm, mom_ref, load_sem.at[1])
    load_momentum.start()
    peers = [at(dx, dy, 0, o) for dx in range(1, NX) for dy, o in ((0, 0), (1, 0), (0, 1))]
    peers += [at(0, dy, dz, o) for dz in range(1, NZ) for dy, o in ((0, 0), (1, 0), (0, 1))]
    peers += [at(0, 1, 0), at(0, 0, 0, 1), at(0, 1, 0, 1), sibling]
    barrier = pltpu.get_barrier_semaphore()
    for peer in peers:
        pl.semaphore_signal(barrier, inc=1, device_id=peer, device_id_type=MESH)
    load.wait()
    load_momentum.wait()
    pl.semaphore_wait(barrier, len(peers))

    def along_z(step):
        return at(0, 0, step)

    def along_x(step):
        return at(step, 0, 0)

    def early_rows(xx, yy, zz, first):
        return part[xx * 16 + yy * 8 + zz, first:first + EARLY, :].astype(F32)

    def early_copy(i):
        if i < 4:
            off = X_ORDER[i]
            src, dst = rx_send.at[off], rx_recv.at[off]
        else:
            span = pl.ds(*EARLY_Z[i - 4])
            src, dst = ry_send.at[span], ry_recv.at[span]
        return remote(src, dst, early_s.at[i], early_r.at[i], at(0, 1, 0))

    def early_issue(i):
        if i < 4:
            off = X_ORDER[i]
            for rel in range(NZ):
                rx_send[off, rel] = early_rows(x_at(off), 1 - yh, z_at(rel), ROWS - EARLY)
        else:
            first, count = EARLY_Z[i - 4]
            for j in range(first, first + count):
                for xx in range(NX):
                    ry_send[j, xx] = early_rows(xx, 1 - yh, z_at(Z_ORDER[j]), HEAD_RING)
        begin(early_copy(i))

    def early_arrive(i):
        early_copy(i).wait_recv()

    def own_rp(off, half):
        j = Z_ORDER.index(off % NZ)
        return jnp.stack([early_rows(xx, yh, z_at(off), HEAD_RING) + ry_recv[j, xx] for xx in (2 * half, 2 * half + 1)])

    def own_rq(off, half):
        return jnp.stack([early_rows(x_at(off), yh, z_at(rel), ROWS - EARLY) + rx_recv[off % NX, rel]
                          for rel in range(4 * half, 4 * half + 4)])

    def rp2_copy(dx):
        return remote(acc_rp.at[x_at(dx)], rp2_recv.at[dx - 1], rp2_s.at[dx - 1], rp2_r.at[dx - 1], along_x(dx))

    def rq2_copy(dz):
        return remote(acc_rq.at[dz], rq2_recv.at[dz - 1], rq2_s.at[dz - 1], rq2_r.at[dz - 1], along_z(dz))

    def early_total(acc, copies, recv, rows):
        total = acc
        for i, copy in enumerate(copies):
            copy.wait_recv()
            total = total + recv[i]
        fin[yh, rows] = total

    def own_p(group):
        first, count = X_GROUPS[group]

        def own(off, half):
            xs = [x_at(rel) for rel in X_ORDER[first:first + count]]
            return jnp.stack([part[xx * 16 + half * 8 + z_at(off), :HEAD_RING, :].astype(F32) for xx in xs])
        return own

    def own_q(group):
        first, count = Z_GROUPS[group]

        def own(off, half):
            zs = [z_at(rel) for rel in Z_ORDER[first:first + count]]
            return jnp.stack([part[x_at(off) * 16 + half * 8 + zz, HEAD:HEAD + TAIL_RING, :].astype(F32) for zz in zs])
        return own

    def own_px(off, half):
        return acc_p[half, X_ORDER.index(off % NX)]

    def own_qz(off, half):
        return acc_q[half, Z_ORDER.index(off % NZ)]

    rings = {
        "px": Ring(NX, along_x, own_px, px_send, px_recv, px_s, px_r),
        "qz": Ring(NZ, along_z, own_qz, qz_send, qz_recv, qz_s, qz_r),
        "rp": Ring(NZ, along_z, own_rp, rp_send, rp_recv, rp_s, rp_r),
        "rq": Ring(NX, along_x, own_rq, rq_send, rq_recv, rq_s, rq_r),
    }
    for g, span in enumerate(X_GROUPS):
        rings["p%d" % g] = Ring(NZ, along_z, own_p(g), p_send, p_recv, p_s.at[g], p_r.at[g], span)
    for g, span in enumerate(Z_GROUPS):
        rings["q%d" % g] = Ring(NX, along_x, own_q(g), q_send, q_recv, q_s.at[g], q_r.at[g], span)

    def final(name):
        if name == "columns0":
            early_total(acc_rp[x], [rp2_copy(dx) for dx in (1, 2, 3)], rp2_recv, pl.ds(HEAD_RING, EARLY))
            for half in range(2):
                fin[half, :HEAD_RING] = rings["px"].total(half)
            columns_start(0)
        elif name == "columns1":
            early_total(acc_rq[0], [rq2_copy(dz) for dz in range(1, NZ)], rq2_recv, pl.ds(ROWS - EARLY, EARLY))
            for half in range(2):
                fin[half, HEAD:HEAD + TAIL_RING] = rings["qz"].total(half)
            columns_start(1)
        elif name == "rpx":
            for half in range(2):
                acc_rp[pl.ds(2 * half, 2)] = rings["rp"].total(half)
            for dx in (2, 1, 3):
                begin(rp2_copy(dx))
        elif name == "rqz":
            for half in range(2):
                acc_rq[pl.ds(4 * half, 4)] = rings["rq"].total(half)
            for dz in (4, 3, 5, 2, 6, 1, 7):
                begin(rq2_copy(dz))
        else:
            acc = acc_p if name[0] == "p" else acc_q
            for half in range(2):
                acc[half, pl.ds(*rings[name].span)] = rings[name].total(half)

    def columns_start(i):
        rows = pl.ds(0, HEAD) if i == 0 else pl.ds(HEAD, TAIL)
        half = pl.ds(0, HEAD_RING) if i == 0 else pl.ds(HEAD, TAIL_RING)
        begin(remote(fin.at[1 - yh, half], same_recv.at[half], y_s.at[0, i], y_r.at[0, i], at(0, 1, 0)))
        cross_send[half] = NESTEROV_GRAD * fin[1 - yh, half]
        begin(remote(cross_send.at[half], cross_recv.at[half], y_s.at[1, i], y_r.at[1, i], at(0, 1, 0, 1)))
        side_send[rows] = NESTEROV_GRAD * fin[yh, rows] + MOMENTUM_DECAY * MOMENTUM_DECAY * mom_ref[rows]
        begin(remote(side_send.at[rows], side_recv.at[rows], y_s.at[2, i], y_r.at[2, i], at(0, 0, 0, 1)))

    def columns_end(i):
        rows = pl.ds(0, HEAD) if i == 0 else pl.ds(HEAD, TAIL)
        half = pl.ds(0, HEAD_RING) if i == 0 else pl.ds(HEAD, TAIL_RING)
        for buf, j, span in ((same_recv, 0, half), (cross_recv, 1, half), (side_recv, 2, rows)):
            remote(buf.at[span], buf.at[span], y_s.at[j, i], y_r.at[j, i], sibling).wait_recv()
        gradient = fin[yh, rows] + same_recv[rows]
        new_momentum = MOMENTUM_DECAY * mom_ref[rows] + gradient
        newm_ref[rows] = new_momentum
        xg[tp, rows] = gradient + MOMENTUM_DECAY * new_momentum
        xg[tp ^ 2, rows] = side_recv[rows] + cross_recv[rows]
        for j, slot in enumerate((tp, tp ^ 2)):
            mine = xg.at[slot, rows]
            begin(remote(mine, mine, x_s.at[j, i], x_r.at[j, i], sibling))

    def columns_wait(i):
        rows = pl.ds(0, HEAD) if i == 0 else pl.ds(HEAD, TAIL)
        for j, slot in enumerate((tp ^ 1, tp ^ 3)):
            other = xg.at[slot, rows]
            remote(other, other, x_s.at[j, i], x_r.at[j, i], sibling).wait_recv()

    for rows in (pl.ds(HEAD_RING, EARLY), pl.ds(ROWS - EARLY, EARLY)):
        same_recv[rows] = jnp.zeros((EARLY, W), F32)
        cross_recv[rows] = jnp.zeros((EARLY, W), F32)
    order, _ = plan(PRIORITY, BACKLOG)
    left = {name: {(name, ring.n - 3), (name, ring.n - 2)} for name, ring in rings.items() if ring.span is not None}
    left["columns0"] = {("px", 1), ("px", 2), ("rpx", 0), ("p2", 5), ("p2", 6)}
    left["columns1"] = {("qz", 5), ("qz", 6), ("rqz", 0), ("q4", 1), ("q4", 2)}
    for what, name, k in order:
        if what == "issue":
            if name == "y":
                early_issue(k)
            elif name in ("rpx", "rqz"):
                final(name)
            else:
                rings[name].issue(k)
            continue
        if name == "y":
            early_arrive(k)
        elif name in rings:
            rings[name].arrive(k)
        for key in [key for key in left if (name, k) in left[key]]:
            left[key].discard((name, k))
            if not left[key]:
                final(key)
    columns_end(0)
    for ring in rings.values():
        ring.sent()
    columns_end(1)
    columns_wait(0)

    def place(block, rows):
        for xx in range(NX):
            for zz in range(NZ):
                r = rows * ((xx % 2) * 8 + zz)
                yield xx, zz, block[r:r + rows, 128 * (xx // 2):128 * (xx // 2) + 128]

    own_x = xg[tp]
    for xx, zz, value in place(cross(own_x, own_x), 16):
        src_p[zz, xx] = value
    rp = [(dz, remote(src_p.at[z_at(dz)], one_p.at[dz - 1], g1p_s.at[dz - 1], g1p_r.at[dz - 1], along_z(dz)))
          for dz in (4, 3, 5, 2, 6, 1, 7)]
    for _, copy in rp:
        begin(copy)
    columns_wait(1)
    high_x = xg[tp % 2 + 2]
    left = jnp.where(tp < 2, high_x[:, :128], high_x[:, 128:])
    lower = jnp.concatenate([cross(xg[lax.rem(tp + 1, 4)], own_x), cross(left, xg[tp % 2])], axis=0)
    for xx, zz, value in place(lower, 24):
        src_q[xx, zz] = value
    rq = [(dx, remote(src_q.at[x_at(dx)], one_q.at[dx - 1], g1q_s.at[dx - 1], g1q_r.at[dx - 1], along_x(dx)))
          for dx in (2, 1, 3)]
    for _, copy in rq:
        begin(copy)

    second_p, second_q = [], []
    for _, copy in rq:
        copy.wait_recv()
    total = src_q[x]
    for i in range(NX - 1):
        total = total + one_q[i]
    tot_q[...] = total
    for dz in (4, 3, 5, 2, 6, 1, 7, 0):
        for dy in range(2):
            if dz or dy:
                i = dy * NZ + dz
                second_q.append(begin(remote(tot_q.at[z_at(dz)], two_q.at[i], g2q_s.at[i], g2q_r.at[i], at(0, dy, dz))))
    for _, copy in rp:
        copy.wait_recv()
    total = src_p[z]
    for i in range(NZ - 1):
        total = total + one_p[i]
    tot_p[...] = total
    for dx in (2, 1, 3, 0):
        for dy in range(2):
            if dx or dy:
                i = dy * NX + dx
                second_p.append(begin(remote(tot_p.at[x_at(dx)], two_p.at[i], g2p_s.at[i], g2p_r.at[i], at(dx, dy, 0))))

    near_p, near_q = [], []
    for copy in second_p:
        copy.wait_recv()
    total = tot_p[x]
    for i in range(1, 2 * NX):
        total = total + two_p[i]
    mine = gp.at[core, z, x, lo]
    mine[...] = total
    for dx in (2, 1, 3, 0):
        for dy in range(2):
            if dx or dy:
                i = dy * NX + dx
                near_p.append(begin(remote(mine, mine, ap_s.at[i], ap_r.at[i], at(dx, 0, 0, dy))))
    for copy in second_q:
        copy.wait_recv()
    total = tot_q[z]
    for i in range(1, 2 * NZ):
        total = total + two_q[i]
    mine_q = gq.at[core, x, z, lo]
    mine_q[...] = total
    for dz in (4, 3, 5, 2, 6, 1, 7, 0):
        for dy in range(2):
            if dz or dy:
                i = dy * NZ + dz
                near_q.append(begin(remote(mine_q, mine_q, aq_s.at[i], aq_r.at[i], at(0, 0, dz, dy))))

    def pass_z(d, hop, sub):
        sign = 1 if d == 0 else -1
        chunk = gp.at[core, z_at(-sign * hop), pl.ds(2 * sub, 2)]
        return remote(chunk, chunk, az_s.at[d, hop, sub], az_r.at[d, hop, sub], along_z(sign))

    def pass_x(d, part_at):
        sign = 1 if d == 0 else -1
        half = d if part_at != 1 else 1 - d
        chunk = gq.at[core, x if part_at < 2 else x_at(-sign), pl.ds(4 * half, 4)]
        return remote(chunk, chunk, ax_s.at[d, part_at], ax_r.at[d, part_at], along_x(sign))

    shared = []

    def share(chunk):
        i = len(shared)
        shared.append(begin(remote(chunk, chunk, c_s.at[i], c_r.at[i], sibling)))

    for copy in near_p:
        copy.wait_recv()
    for turn in range(2):
        for d in range(2):
            begin(pass_z(d, 0, d ^ turn))
    share(gp.at[core, z])

    def z_step(hop, turn):
        for d in range(2):
            sub = d ^ turn
            pass_z(d, hop, sub).wait_recv()
            if hop < 2 or (hop == 2 and turn == 0):
                begin(pass_z(d, hop + 1, sub))
        for d in range(2):
            sign = 1 if d == 0 else -1
            if hop == 3:
                share(gp.at[core, z_at(4), pl.ds(2 * d, 2)])
            elif turn == 1:
                share(gp.at[core, z_at(-sign * (hop + 1))])

    def x_step(part_at):
        for d in range(2):
            pass_x(d, part_at).wait_recv()
            if part_at == 0:
                begin(pass_x(d, 2))
        for d in range(2):
            sign = 1 if d == 0 else -1
            half = d if part_at != 1 else 1 - d
            share(gq.at[core, x_at(-sign if part_at < 2 else 2), pl.ds(4 * half, 4)])

    z_step(0, 0)
    for copy in near_q:
        copy.wait_recv()
    for part_at in range(2):
        for d in range(2):
            begin(pass_x(d, part_at))
    share(gq.at[core, x])
    z_step(0, 1)
    z_step(1, 0)
    z_step(1, 1)
    x_step(0)
    z_step(2, 0)
    z_step(2, 1)
    x_step(1)
    z_step(3, 0)
    x_step(2)
    for copy in shared:
        copy.wait_recv()
    drain()


def communicate(partials, momentum):
    def ring(n, *block):
        return [pltpu.VMEM((2, n - 1) + block, F32)] * 2

    def sems(*shape):
        return [pltpu.SemaphoreType.DMA(shape)] * 2

    vmem = pl.BlockSpec(memory_space=pltpu.VMEM)
    block = pltpu.VMEM((ROWS, W), F32)
    return pl.pallas_call(
        kernel,
        out_shape=[
            jax.ShapeDtypeStruct((ROWS, W), F32),
            jax.ShapeDtypeStruct((4, ROWS, W), F32),
            jax.ShapeDtypeStruct((2, NZ, NX, 2, 16, 128), F32),
            jax.ShapeDtypeStruct((2, NX, NZ, 2, 24, 128), F32),
        ],
        in_specs=[pl.BlockSpec(memory_space=pltpu.HBM)] * 2,
        out_specs=[vmem] * 4,
        scratch_shapes=[
            pltpu.VMEM((64, ROWS, W), jnp.bfloat16),
            block,
            pltpu.VMEM((2, ROWS, W), F32),
            pltpu.VMEM((2, NX, HEAD_RING, W), F32),
            pltpu.VMEM((2, NZ, TAIL_RING, W), F32),
            *[pltpu.VMEM((NZ, NX, EARLY, W), F32)] * 2, *[pltpu.VMEM((NX, NZ, EARLY, W), F32)] * 2,
            *ring(NZ, 2, EARLY, W), *ring(NX, 4, EARLY, W),
            pltpu.VMEM((NX, EARLY, W), F32), pltpu.VMEM((NZ, EARLY, W), F32),
            pltpu.VMEM((NX - 1, EARLY, W), F32), pltpu.VMEM((NZ - 1, EARLY, W), F32),
            *ring(NZ, NX, HEAD_RING, W), *ring(NX, HEAD_RING, W), *ring(NX, NZ, TAIL_RING, W), *ring(NZ, TAIL_RING, W),
            block, block, block, block, block,
            pltpu.VMEM((NZ, NX, 16, 128), F32), pltpu.VMEM((NX, NZ, 24, 128), F32),
            pltpu.VMEM((NZ - 1, NX, 16, 128), F32), pltpu.VMEM((NX - 1, NZ, 24, 128), F32),
            pltpu.VMEM((NX, 16, 128), F32), pltpu.VMEM((NZ, 24, 128), F32),
            pltpu.VMEM((2 * NX, 16, 128), F32), pltpu.VMEM((2 * NZ, 24, 128), F32),
            pltpu.SemaphoreType.DMA((2,)),
            *sems(3, 2, NZ - 1), *sems(2, NX - 1), *sems(5, 2, NX - 1), *sems(2, NZ - 1),
            *sems(3, 2),
            *sems(9), *sems(2, NZ - 1), *sems(2, NX - 1), *sems(NX - 1), *sems(NZ - 1),
            *sems(2, 2),
            *sems(NZ - 1), *sems(NX - 1), *sems(2 * NX), *sems(2 * NZ),
            *sems(2 * NX), *sems(2 * NZ), *sems(2, 4, 2), *sems(2, 3), *sems(18),
        ],
        compiler_params=pltpu.CompilerParams(collective_id=0, has_side_effects=True, vmem_limit_bytes=49 * 1024 * 1024),
    )(partials.reshape(64, ROWS, W), momentum)


def finish(x_ref, gp, gq, w_ref, m_ref, update_ref, neww_ref, newm_ref,
           a, low, ah, al, a2h, a2l, mh, ml, mine):
    tp = lax.axis_index("tp")
    newm_ref[...] = m_ref[...]
    row, col = (lax.broadcasted_iota(jnp.int32, (16, 128), axis) for axis in range(2))
    square = jnp.zeros((16, 128), F32)
    for t in range(4):
        for zz in range(NZ):
            for xx in (0, 3):
                square = square + jnp.where(col - row == 16 * zz, gp[t % 2, zz, xx, t // 2], 0.0)
    inverse = 1.0 / (jnp.sqrt(jnp.sum(square, keepdims=True)) + NORM_EPS)
    scale = inverse * inverse

    def put(first_row, first_col, value):
        rows = slice(first_row, first_row + value.shape[0])
        cols = slice(first_col, first_col + value.shape[1])
        a[rows, cols] = value
        ah[rows, cols], al[rows, cols] = split(value)

    for t in range(4):
        core, lo, base = t % 2, t // 2, 256 * t
        for xx in range(NX):
            for zz in range(NZ):
                r, c = (xx % 2) * 8 + zz, xx // 2
                put(base + 16 * r, base + 128 * c, gp[core, zz, xx, lo] * scale)
                low[t, 24 * r:24 * r + 24, 128 * c:128 * c + 128] = gq[core, xx, zz, lo] * scale
    for t in range(4):
        nxt = (t + 1) % 4
        side = low[t, :256, :]
        put(256 * nxt, 256 * t, side)
        put(256 * t, 256 * nxt, side.T)
        far = low[t, 256:, :]
        i, j = 256 * (t % 2 + 2) + 128 * (t // 2), 256 * (t % 2)
        put(i, j, far)
        put(j, i, far.T)

    def dot3(lh, ll, rh, rl):
        dot = functools.partial(jnp.dot, preferred_element_type=F32)
        return dot(lh, rh) + (dot(lh, rl) + dot(ll, rh))

    same = lax.broadcasted_iota(jnp.int32, (256, 256), 0) == lax.broadcasted_iota(jnp.int32, (256, 256), 1)

    def store(rows, cols, block):
        a2h[rows, cols], a2l[rows, cols] = split(block)
        value = COEF_B * a[rows, cols] + COEF_C * block
        if rows == cols:
            value = value + jnp.where(same, COEF_A, 0.0)
        mh[rows, cols], ml[rows, cols] = split(value)

    for i in range(4):
        rows = slice(256 * i, 256 * i + 256)
        for j in range(i, 4):
            cols = slice(256 * j, 256 * j + 256)
            block = dot3(ah[rows, :], al[rows, :], ah[:, cols], al[:, cols])
            store(rows, cols, block)
            if j > i:
                store(cols, rows, block.T)

    def times(x, high, lowp, cols=None):
        xh, xl = split(x)
        both = jnp.concatenate([xh, xl], axis=0)
        parts = []
        for at in [cols] if cols is not None else [slice(256 * j, 256 * j + 256) for j in range(4)]:
            first = jnp.dot(both, high[:, at], preferred_element_type=F32)
            second = jnp.dot(xh, lowp[:, at], preferred_element_type=F32)
            parts.append(first[:ROWS] + (first[ROWS:] + second))
        return parts[0] if cols is not None else jnp.concatenate(parts, axis=1)

    own = pl.ds(pl.multiple_of(tp * 256, 256), 256)
    start = jnp.concatenate([x_ref[t] for t in range(4)], axis=1) * inverse
    one = times(start, mh, ml)
    for t in range(4):
        mine[t] = one[:, 256 * t:256 * t + 256]
    turned = times(times(one, mh, ml), mh, ml)
    result = COEF_A * mine[tp] + COEF_B * times(turned, ah, al, own)
    result = result + COEF_C * times(times(times(turned, a2h, a2l), mh, ml), mh, ml, own)
    update = 0.2 * math.sqrt(max(D, FF)) * result
    update_ref[...] = update
    neww_ref[...] = w_ref[...] - LEARN_RATE * (update + WEIGHT_DECAY * w_ref[...])


def orthogonalize(x, gp, gq, weights, new_momentum):
    vmem = pl.BlockSpec(memory_space=pltpu.VMEM)
    block = jax.ShapeDtypeStruct((ROWS, W), F32)
    half = jnp.bfloat16
    return pl.pallas_call(
        finish,
        out_shape=[block] * 3,
        in_specs=[vmem] * 5,
        out_specs=[vmem] * 3,
        scratch_shapes=[
            pltpu.VMEM((FF, FF), F32), pltpu.VMEM((4, 384, W), F32),
            *[pltpu.VMEM((FF, FF), half)] * 6,
            pltpu.VMEM((4, ROWS, W), F32),
        ],
        compiler_params=pltpu.CompilerParams(vmem_limit_bytes=40 * 1024 * 1024),
    )(x, gp, gq, weights, new_momentum)


def on_device(partials, momentum, weights):
    new_momentum, x, gp, gq = communicate(partials[0], momentum)
    return tuple(orthogonalize(x, gp, gq, weights, new_momentum))


def solution(mesh):
    return jax.shard_map(
        on_device,
        mesh=mesh,
        in_specs=(P("dp", None, "tp"), P("dp", "tp"), P("dp", "tp")),
        out_specs=(P("dp", "tp"), P("dp", "tp"), P("dp", "tp")),
        check_vma=False,
    )
```

```python
import functools
import math

import jax
import jax.numpy as jnp
from jax import lax
from jax.experimental import pallas as pl
from jax.experimental.pallas import tpu as pltpu
from jax.sharding import PartitionSpec as P

MESH = pl.DeviceIdType.MESH
F32 = jnp.float32
NX, NY, NZ = 4, 2, 8
ROWS = 112
HEAD = 48
EARLY = 16
TAIL = ROWS - HEAD
HEAD_RING = HEAD - EARLY
TAIL_RING = TAIL - EARLY
W = 256
X_ORDER = (2, 1, 3, 0)
Z_ORDER = (4, 3, 5, 2, 6, 1, 7, 0)
X_GROUPS = ((0, 1), (1, 2), (3, 1))
Z_GROUPS = ((0, 1), (1, 2), (3, 2), (5, 2), (7, 1))
EARLY_Z = Z_GROUPS
UNIT = 0.026
PRIORITY = ("y", "q4", "p1", "rp", "q0", "rqz", "rpx", "q2", "qz", "p0", "p2", "q1", "px", "rq", "q3")
BACKLOG = 6.0
LATE, FAR_LATE = 2.0, 3.0
D = 7168
FF = 1024
COEF_A = 3.4445
COEF_B = -4.775
COEF_C = 2.0315
MOMENTUM_DECAY = 0.95
LEARN_RATE = 0.02
WEIGHT_DECAY = 0.1
NORM_EPS = 1e-07
NESTEROV_GRAD = 1.0 + MOMENTUM_DECAY


def plan(priority, backlog):
    link, cost, needs = {}, {}, {}

    def add(name, k, axis, rows, after=()):
        link[name, k], cost[name, k], needs[name, k] = axis, rows * UNIT, set(after)

    def chain(name, k):
        return {(name, k - 2)} if k >= 2 else set()

    for g, count in enumerate((1, 2, 1)):
        for k in range(NZ - 1):
            add("p%d" % g, k, "z", count * HEAD_RING, chain("p%d" % g, k))
    for g, count in enumerate((1, 2, 2, 2, 1)):
        for k in range(NX - 1):
            add("q%d" % g, k, "x", count * TAIL_RING, chain("q%d" % g, k))
    for k in range(NX - 1):
        g = (k + 1) // 2
        add("px", k, "x", HEAD_RING, chain("px", k) | {("p%d" % g, 5), ("p%d" % g, 6)})
    for k in range(NZ - 1):
        g = (k + 1) // 2
        add("qz", k, "z", TAIL_RING, chain("qz", k) | {("q%d" % g, 1), ("q%d" % g, 2)})
    if EARLY:
        for i in range(9):
            add("y", i, "y", EARLY * (8 if i < 4 else 4 * EARLY_Z[i - 4][1]))
        for k in range(NZ - 1):
            add("rp", k, "z", 2 * EARLY, chain("rp", k) | {("y", 4 + (k + 1) // 2)})
        for k in range(NX - 1):
            add("rq", k, "x", 4 * EARLY, chain("rq", k) | ({("y", 0)} if k == 0 else {("y", 1), ("y", 2)}))
        add("rpx", 0, "x", 2 * EARLY, {("rp", 5), ("rp", 6), ("y", 8)})
        add("rqz", 0, "z", 8 * EARLY, {("rq", 1), ("rq", 2), ("y", 3)})
    free, now, flying, arrived, waiting, order = dict.fromkeys("xyz", 0.0), 0.0, [], set(), list(link), []
    while waiting or flying:
        for axis in "zxy":
            while free[axis] - now < backlog:
                ready = [t for t in waiting if link[t] == axis and needs[t] <= arrived]
                if not ready:
                    break
                pick = min(ready, key=lambda t: (priority.index(t[0]), t[1]))
                waiting.remove(pick)
                free[axis] = max(free[axis], now) + cost[pick]
                late = FAR_LATE if pick[0] in ("rqz", "rpx", "y") else LATE
                flying.append((free[axis] + late, pick))
                order.append(("issue",) + pick)
        when, pick = min(flying)
        flying.remove((when, pick))
        now = max(now, when) + 0.15
        arrived.add(pick)
        order.append(("arrive",) + pick)
    return order, now


class Ring:
    def __init__(self, n, place, own, send, recv, send_sem, recv_sem, span=None):
        self.n, self.place, self.own, self.span = n, place, own, span
        self.send, self.recv, self.send_sem, self.recv_sem = send, recv, send_sem, recv_sem

    def at(self, d, k):
        return (d, k) if self.span is None else (d, k, pl.ds(*self.span))

    def copy(self, d, k):
        return pltpu.make_async_remote_copy(
            src_ref=self.send.at[self.at(d, k)], dst_ref=self.recv.at[self.at(d, k)],
            send_sem=self.send_sem.at[d, k], recv_sem=self.recv_sem.at[d, k],
            device_id=self.place(1 if d == 0 else -1), device_id_type=MESH,
        )

    def offset(self, d, k):
        return (1 if d == 0 else -1) * (self.n // 2 - (k + 1) // 2)

    def issue(self, k):
        for d in range(2):
            value = self.own(self.offset(d, k), (k + d) % 2)
            if k >= 2:
                value = value + self.recv[self.at(d, k - 2)]
            self.send[self.at(d, k)] = value
            self.copy(d, k).start()

    def arrive(self, k):
        for d in range(2):
            self.copy(d, k).wait_recv()

    def total(self, half):
        first, last = self.n - 3 + (half + 1) % 2, self.n - 3 + half
        return self.own(0, half) + self.recv[self.at(0, first)] + self.recv[self.at(1, last)]

    def sent(self):
        for d in range(2):
            for k in range(self.n - 1):
                self.copy(d, k).wait_send()


def split(value):
    high = value.astype(jnp.bfloat16)
    return high, (value - high.astype(F32)).astype(jnp.bfloat16)


def cross(left, right):
    (lh, ll), (rh, rl) = split(left), split(right)
    dims = (((0,), (0,)), ((), ()))
    dot = functools.partial(lax.dot_general, dimension_numbers=dims, preferred_element_type=F32)
    return dot(lh, rh) + (dot(lh, rl) + dot(ll, rh))


def kernel(part_hbm, mom_hbm, newm_ref, xg, gp, gq, part, mom_ref, fin, acc_p, acc_q,
           ry_send, ry_recv, rx_send, rx_recv, rp_send, rp_recv, rq_send, rq_recv, acc_rp, acc_rq, rp2_recv, rq2_recv,
           p_send, p_recv, px_send, px_recv, q_send, q_recv, qz_send, qz_recv,
           same_recv, side_send, side_recv, cross_send, cross_recv,
           src_p, src_q, one_p, one_q, tot_p, tot_q, two_p, two_q,
           load_sem, p_s, p_r, px_s, px_r, q_s, q_r, qz_s, qz_r, y_s, y_r,
           early_s, early_r, rp_s, rp_r, rq_s, rq_r, rp2_s, rp2_r, rq2_s, rq2_r,
           x_s, x_r, g1p_s, g1p_r, g1q_s, g1q_r, g2p_s, g2p_r, g2q_s, g2q_r,
           ap_s, ap_r, aq_s, aq_r, az_s, az_r, ax_s, ax_r, c_s, c_r):
    dp = lax.axis_index("dp")
    tp = lax.axis_index("tp")
    x, yh, z = dp // 16, (dp // 8) % 2, dp % 8
    lo, core = tp // 2, tp % 2
    sibling = (dp, tp ^ 1)
    pending = []

    def x_at(off):
        return lax.rem(x + off + 2 * NX, NX)

    def z_at(off):
        return lax.rem(z + off + 2 * NZ, NZ)

    def at(dx, dy, dz, other=0):
        return (x_at(dx) * 16 + lax.rem(yh + dy, NY) * 8 + z_at(dz), tp ^ (2 * other))

    def remote(src, dst, send_sem, recv_sem, device):
        return pltpu.make_async_remote_copy(
            src_ref=src, dst_ref=dst, send_sem=send_sem, recv_sem=recv_sem, device_id=device, device_id_type=MESH,
        )

    def begin(copy):
        copy.start()
        pending.append(copy)
        return copy

    def drain():
        for copy in pending:
            copy.wait_send()

    def along_z(step):
        return at(0, 0, step)

    def along_x(step):
        return at(step, 0, 0)

    load = pltpu.make_async_copy(part_hbm, part, load_sem.at[0])
    load.start()
    load_momentum = pltpu.make_async_copy(mom_hbm, mom_ref, load_sem.at[1])
    load_momentum.start()
    peers = [along_z(1), along_z(-1), along_x(1), along_x(-1), at(0, 1, 0), at(0, 0, 0, 1), at(0, 1, 0, 1), sibling]
    barrier = pltpu.get_barrier_semaphore()
    for peer in peers:
        pl.semaphore_signal(barrier, inc=1, device_id=peer, device_id_type=MESH)
    load.wait()
    load_momentum.wait()
    pl.semaphore_wait(barrier, len(peers))

    def early_rows(xx, yy, zz, first):
        return part[xx * 16 + yy * 8 + zz, first:first + EARLY, :].astype(F32)

    def early_copy(i):
        if i < 4:
            off = X_ORDER[i]
            src, dst = rx_send.at[off], rx_recv.at[off]
        else:
            span = pl.ds(*EARLY_Z[i - 4])
            src, dst = ry_send.at[span], ry_recv.at[span]
        return remote(src, dst, early_s.at[i], early_r.at[i], at(0, 1, 0))

    def early_issue(i):
        if i < 4:
            off = X_ORDER[i]
            for rel in range(NZ):
                rx_send[off, rel] = early_rows(x_at(off), 1 - yh, z_at(rel), ROWS - EARLY)
        else:
            first, count = EARLY_Z[i - 4]
            for j in range(first, first + count):
                for xx in range(NX):
                    ry_send[j, xx] = early_rows(xx, 1 - yh, z_at(Z_ORDER[j]), HEAD_RING)
        begin(early_copy(i))

    def early_arrive(i):
        early_copy(i).wait_recv()

    def own_rp(off, half):
        j = Z_ORDER.index(off % NZ)
        return jnp.stack([early_rows(xx, yh, z_at(off), HEAD_RING) + ry_recv[j, xx] for xx in (2 * half, 2 * half + 1)])

    def own_rq(off, half):
        return jnp.stack([early_rows(x_at(off), yh, z_at(rel), ROWS - EARLY) + rx_recv[off % NX, rel]
                          for rel in range(4 * half, 4 * half + 4)])

    def rp2_copy(dx):
        return remote(acc_rp.at[x_at(dx)], rp2_recv.at[dx - 1], rp2_s.at[dx - 1], rp2_r.at[dx - 1], along_x(dx))

    def rq2_copy(dz):
        return remote(acc_rq.at[dz], rq2_recv.at[dz - 1], rq2_s.at[dz - 1], rq2_r.at[dz - 1], along_z(dz))

    def early_total(acc, copies, recv, rows):
        total = acc
        for i, copy in enumerate(copies):
            copy.wait_recv()
            total = total + recv[i]
        fin[yh, rows] = total

    def own_p(group):
        first, count = X_GROUPS[group]

        def own(off, half):
            xs = [x_at(rel) for rel in X_ORDER[first:first + count]]
            return jnp.stack([part[xx * 16 + half * 8 + z_at(off), :HEAD_RING, :].astype(F32) for xx in xs])
        return own

    def own_q(group):
        first, count = Z_GROUPS[group]

        def own(off, half):
            zs = [z_at(rel) for rel in Z_ORDER[first:first + count]]
            return jnp.stack([part[x_at(off) * 16 + half * 8 + zz, HEAD:HEAD + TAIL_RING, :].astype(F32) for zz in zs])
        return own

    def own_px(off, half):
        return acc_p[half, X_ORDER.index(off % NX)]

    def own_qz(off, half):
        return acc_q[half, Z_ORDER.index(off % NZ)]

    rings = {
        "px": Ring(NX, along_x, own_px, px_send, px_recv, px_s, px_r),
        "qz": Ring(NZ, along_z, own_qz, qz_send, qz_recv, qz_s, qz_r),
        "rp": Ring(NZ, along_z, own_rp, rp_send, rp_recv, rp_s, rp_r),
        "rq": Ring(NX, along_x, own_rq, rq_send, rq_recv, rq_s, rq_r),
    }
    for g, span in enumerate(X_GROUPS):
        rings["p%d" % g] = Ring(NZ, along_z, own_p(g), p_send, p_recv, p_s.at[g], p_r.at[g], span)
    for g, span in enumerate(Z_GROUPS):
        rings["q%d" % g] = Ring(NX, along_x, own_q(g), q_send, q_recv, q_s.at[g], q_r.at[g], span)

    def final(name):
        if name == "columns0":
            early_total(acc_rp[x], [rp2_copy(dx) for dx in (1, 2, 3)], rp2_recv, pl.ds(HEAD_RING, EARLY))
            for half in range(2):
                fin[half, :HEAD_RING] = rings["px"].total(half)
            columns_start(0)
        elif name == "columns1":
            early_total(acc_rq[0], [rq2_copy(dz) for dz in range(1, NZ)], rq2_recv, pl.ds(ROWS - EARLY, EARLY))
            for half in range(2):
                fin[half, HEAD:HEAD + TAIL_RING] = rings["qz"].total(half)
            columns_start(1)
        elif name == "rpx":
            for half in range(2):
                acc_rp[pl.ds(2 * half, 2)] = rings["rp"].total(half)
            for dx in (2, 1, 3):
                begin(rp2_copy(dx))
        elif name == "rqz":
            for half in range(2):
                acc_rq[pl.ds(4 * half, 4)] = rings["rq"].total(half)
            for dz in (4, 3, 5, 2, 6, 1, 7):
                begin(rq2_copy(dz))
        else:
            acc = acc_p if name[0] == "p" else acc_q
            for half in range(2):
                acc[half, pl.ds(*rings[name].span)] = rings[name].total(half)

    def columns_start(i):
        rows = pl.ds(0, HEAD) if i == 0 else pl.ds(HEAD, TAIL)
        half = pl.ds(0, HEAD_RING) if i == 0 else pl.ds(HEAD, TAIL_RING)
        begin(remote(fin.at[1 - yh, half], same_recv.at[half], y_s.at[0, i], y_r.at[0, i], at(0, 1, 0)))
        cross_send[half] = NESTEROV_GRAD * fin[1 - yh, half]
        begin(remote(cross_send.at[half], cross_recv.at[half], y_s.at[1, i], y_r.at[1, i], at(0, 1, 0, 1)))
        side_send[rows] = NESTEROV_GRAD * fin[yh, rows] + MOMENTUM_DECAY * MOMENTUM_DECAY * mom_ref[rows]
        begin(remote(side_send.at[rows], side_recv.at[rows], y_s.at[2, i], y_r.at[2, i], at(0, 0, 0, 1)))

    def columns_end(i):
        rows = pl.ds(0, HEAD) if i == 0 else pl.ds(HEAD, TAIL)
        half = pl.ds(0, HEAD_RING) if i == 0 else pl.ds(HEAD, TAIL_RING)
        for buf, j, span in ((same_recv, 0, half), (cross_recv, 1, half), (side_recv, 2, rows)):
            remote(buf.at[span], buf.at[span], y_s.at[j, i], y_r.at[j, i], sibling).wait_recv()
        gradient = fin[yh, rows] + same_recv[rows]
        new_momentum = MOMENTUM_DECAY * mom_ref[rows] + gradient
        newm_ref[rows] = new_momentum
        xg[tp, rows] = gradient + MOMENTUM_DECAY * new_momentum
        xg[tp ^ 2, rows] = side_recv[rows] + cross_recv[rows]
        for j, slot in enumerate((tp, tp ^ 2)):
            mine = xg.at[slot, rows]
            begin(remote(mine, mine, x_s.at[j, i], x_r.at[j, i], sibling))

    def columns_wait(i):
        rows = pl.ds(0, HEAD) if i == 0 else pl.ds(HEAD, TAIL)
        for j, slot in enumerate((tp ^ 1, tp ^ 3)):
            other = xg.at[slot, rows]
            remote(other, other, x_s.at[j, i], x_r.at[j, i], sibling).wait_recv()

    for rows in (pl.ds(HEAD_RING, EARLY), pl.ds(ROWS - EARLY, EARLY)):
        same_recv[rows] = jnp.zeros((EARLY, W), F32)
        cross_recv[rows] = jnp.zeros((EARLY, W), F32)
    order, _ = plan(PRIORITY, BACKLOG)
    left = {name: {(name, ring.n - 3), (name, ring.n - 2)} for name, ring in rings.items() if ring.span is not None}
    left["columns0"] = {("px", 1), ("px", 2), ("rpx", 0), ("p2", 5), ("p2", 6)}
    left["columns1"] = {("qz", 5), ("qz", 6), ("rqz", 0), ("q4", 1), ("q4", 2)}
    for what, name, k in order:
        if what == "issue":
            if name == "y":
                early_issue(k)
            elif name in ("rpx", "rqz"):
                final(name)
            else:
                rings[name].issue(k)
            continue
        if name == "y":
            early_arrive(k)
        elif name in rings:
            rings[name].arrive(k)
        for key in [key for key in left if (name, k) in left[key]]:
            left[key].discard((name, k))
            if not left[key]:
                final(key)
    columns_end(0)
    for ring in rings.values():
        ring.sent()
    columns_end(1)
    columns_wait(0)

    def place(block, rows):
        for xx in range(NX):
            for zz in range(NZ):
                r = rows * ((xx % 2) * 8 + zz)
                yield xx, zz, block[r:r + rows, 128 * (xx // 2):128 * (xx // 2) + 128]

    own_x = xg[tp]
    for xx, zz, value in place(cross(own_x, own_x), 16):
        src_p[zz, xx] = value
    rp = [(dz, remote(src_p.at[z_at(dz)], one_p.at[dz - 1], g1p_s.at[dz - 1], g1p_r.at[dz - 1], along_z(dz)))
          for dz in (4, 3, 5, 2, 6, 1, 7)]
    for _, copy in rp:
        begin(copy)
    columns_wait(1)
    high_x = xg[tp % 2 + 2]
    left = jnp.where(tp < 2, high_x[:, :128], high_x[:, 128:])
    lower = jnp.concatenate([cross(xg[lax.rem(tp + 1, 4)], own_x), cross(left, xg[tp % 2])], axis=0)
    for xx, zz, value in place(lower, 24):
        src_q[xx, zz] = value
    rq = [(dx, remote(src_q.at[x_at(dx)], one_q.at[dx - 1], g1q_s.at[dx - 1], g1q_r.at[dx - 1], along_x(dx)))
          for dx in (2, 1, 3)]
    for _, copy in rq:
        begin(copy)

    second_p, second_q = [], []
    for _, copy in rq:
        copy.wait_recv()
    total = src_q[x]
    for i in range(NX - 1):
        total = total + one_q[i]
    tot_q[...] = total
    for dz in (4, 3, 5, 2, 6, 1, 7, 0):
        for dy in range(2):
            if dz or dy:
                i = dy * NZ + dz
                second_q.append(begin(remote(tot_q.at[z_at(dz)], two_q.at[i], g2q_s.at[i], g2q_r.at[i], at(0, dy, dz))))
    for _, copy in rp:
        copy.wait_recv()
    total = src_p[z]
    for i in range(NZ - 1):
        total = total + one_p[i]
    tot_p[...] = total
    for dx in (2, 1, 3, 0):
        for dy in range(2):
            if dx or dy:
                i = dy * NX + dx
                second_p.append(begin(remote(tot_p.at[x_at(dx)], two_p.at[i], g2p_s.at[i], g2p_r.at[i], at(dx, dy, 0))))

    near_p, near_q = [], []
    for copy in second_p:
        copy.wait_recv()
    total = tot_p[x]
    for i in range(1, 2 * NX):
        total = total + two_p[i]
    mine = gp.at[core, z, x, lo]
    mine[...] = total
    for dx in (2, 1, 3, 0):
        for dy in range(2):
            if dx or dy:
                i = dy * NX + dx
                near_p.append(begin(remote(mine, mine, ap_s.at[i], ap_r.at[i], at(dx, 0, 0, dy))))
    for copy in second_q:
        copy.wait_recv()
    total = tot_q[z]
    for i in range(1, 2 * NZ):
        total = total + two_q[i]
    mine_q = gq.at[core, x, z, lo]
    mine_q[...] = total
    for dz in (4, 3, 5, 2, 6, 1, 7, 0):
        for dy in range(2):
            if dz or dy:
                i = dy * NZ + dz
                near_q.append(begin(remote(mine_q, mine_q, aq_s.at[i], aq_r.at[i], at(0, 0, dz, dy))))

    def pass_z(d, hop, sub):
        sign = 1 if d == 0 else -1
        chunk = gp.at[core, z_at(-sign * hop), pl.ds(2 * sub, 2)]
        return remote(chunk, chunk, az_s.at[d, hop, sub], az_r.at[d, hop, sub], along_z(sign))

    def pass_x(d, part_at):
        sign = 1 if d == 0 else -1
        half = d if part_at != 1 else 1 - d
        chunk = gq.at[core, x if part_at < 2 else x_at(-sign), pl.ds(4 * half, 4)]
        return remote(chunk, chunk, ax_s.at[d, part_at], ax_r.at[d, part_at], along_x(sign))

    shared = []

    def share(chunk):
        i = len(shared)
        shared.append(begin(remote(chunk, chunk, c_s.at[i], c_r.at[i], sibling)))

    for copy in near_p:
        copy.wait_recv()
    for turn in range(2):
        for d in range(2):
            begin(pass_z(d, 0, d ^ turn))
    share(gp.at[core, z])

    def z_step(hop, turn):
        for d in range(2):
            sub = d ^ turn
            pass_z(d, hop, sub).wait_recv()
            if hop < 2 or (hop == 2 and turn == 0):
                begin(pass_z(d, hop + 1, sub))
        for d in range(2):
            sign = 1 if d == 0 else -1
            if hop == 3:
                share(gp.at[core, z_at(4), pl.ds(2 * d, 2)])
            elif turn == 1:
                share(gp.at[core, z_at(-sign * (hop + 1))])

    def x_step(part_at):
        for d in range(2):
            pass_x(d, part_at).wait_recv()
            if part_at == 0:
                begin(pass_x(d, 2))
        for d in range(2):
            sign = 1 if d == 0 else -1
            half = d if part_at != 1 else 1 - d
            share(gq.at[core, x_at(-sign if part_at < 2 else 2), pl.ds(4 * half, 4)])

    z_step(0, 0)
    for copy in near_q:
        copy.wait_recv()
    for part_at in range(2):
        for d in range(2):
            begin(pass_x(d, part_at))
    share(gq.at[core, x])
    z_step(0, 1)
    z_step(1, 0)
    z_step(1, 1)
    x_step(0)
    z_step(2, 0)
    z_step(2, 1)
    x_step(1)
    z_step(3, 0)
    x_step(2)
    for copy in shared:
        copy.wait_recv()
    drain()


def communicate(partials, momentum):
    def ring(n, *block):
        return [pltpu.VMEM((2, n - 1) + block, F32)] * 2

    def sems(*shape):
        return [pltpu.SemaphoreType.DMA(shape)] * 2

    vmem = pl.BlockSpec(memory_space=pltpu.VMEM)
    block = pltpu.VMEM((ROWS, W), F32)
    return pl.pallas_call(
        kernel,
        out_shape=[
            jax.ShapeDtypeStruct((ROWS, W), F32),
            jax.ShapeDtypeStruct((4, ROWS, W), F32),
            jax.ShapeDtypeStruct((2, NZ, NX, 2, 16, 128), F32),
            jax.ShapeDtypeStruct((2, NX, NZ, 2, 24, 128), F32),
        ],
        in_specs=[pl.BlockSpec(memory_space=pltpu.HBM)] * 2,
        out_specs=[vmem] * 4,
        scratch_shapes=[
            pltpu.VMEM((64, ROWS, W), jnp.bfloat16),
            block,
            pltpu.VMEM((2, ROWS, W), F32),
            pltpu.VMEM((2, NX, HEAD_RING, W), F32),
            pltpu.VMEM((2, NZ, TAIL_RING, W), F32),
            *[pltpu.VMEM((NZ, NX, EARLY, W), F32)] * 2, *[pltpu.VMEM((NX, NZ, EARLY, W), F32)] * 2,
            *ring(NZ, 2, EARLY, W), *ring(NX, 4, EARLY, W),
            pltpu.VMEM((NX, EARLY, W), F32), pltpu.VMEM((NZ, EARLY, W), F32),
            pltpu.VMEM((NX - 1, EARLY, W), F32), pltpu.VMEM((NZ - 1, EARLY, W), F32),
            *ring(NZ, NX, HEAD_RING, W), *ring(NX, HEAD_RING, W), *ring(NX, NZ, TAIL_RING, W), *ring(NZ, TAIL_RING, W),
            block, block, block, block, block,
            pltpu.VMEM((NZ, NX, 16, 128), F32), pltpu.VMEM((NX, NZ, 24, 128), F32),
            pltpu.VMEM((NZ - 1, NX, 16, 128), F32), pltpu.VMEM((NX - 1, NZ, 24, 128), F32),
            pltpu.VMEM((NX, 16, 128), F32), pltpu.VMEM((NZ, 24, 128), F32),
            pltpu.VMEM((2 * NX, 16, 128), F32), pltpu.VMEM((2 * NZ, 24, 128), F32),
            pltpu.SemaphoreType.DMA((2,)),
            *sems(3, 2, NZ - 1), *sems(2, NX - 1), *sems(5, 2, NX - 1), *sems(2, NZ - 1),
            *sems(3, 2),
            *sems(9), *sems(2, NZ - 1), *sems(2, NX - 1), *sems(NX - 1), *sems(NZ - 1),
            *sems(2, 2),
            *sems(NZ - 1), *sems(NX - 1), *sems(2 * NX), *sems(2 * NZ),
            *sems(2 * NX), *sems(2 * NZ), *sems(2, 4, 2), *sems(2, 3), *sems(18),
        ],
        compiler_params=pltpu.CompilerParams(collective_id=0, has_side_effects=True, vmem_limit_bytes=49 * 1024 * 1024),
    )(partials.reshape(64, ROWS, W), momentum)


def finish(x_ref, gp, gq, w_ref, m_ref, update_ref, neww_ref, newm_ref,
           a, low, ah, al, a2h, a2l, mh, ml, mine):
    tp = lax.axis_index("tp")
    newm_ref[...] = m_ref[...]
    row, col = (lax.broadcasted_iota(jnp.int32, (16, 128), axis) for axis in range(2))
    square = jnp.zeros((16, 128), F32)
    for t in range(4):
        for zz in range(NZ):
            for xx in (0, 3):
                square = square + jnp.where(col - row == 16 * zz, gp[t % 2, zz, xx, t // 2], 0.0)
    inverse = 1.0 / (jnp.sqrt(jnp.sum(square, keepdims=True)) + NORM_EPS)
    scale = inverse * inverse

    def put(first_row, first_col, value):
        rows = slice(first_row, first_row + value.shape[0])
        cols = slice(first_col, first_col + value.shape[1])
        a[rows, cols] = value
        ah[rows, cols], al[rows, cols] = split(value)

    for t in range(4):
        core, lo, base = t % 2, t // 2, 256 * t
        for xx in range(NX):
            for zz in range(NZ):
                r, c = (xx % 2) * 8 + zz, xx // 2
                put(base + 16 * r, base + 128 * c, gp[core, zz, xx, lo] * scale)
                low[t, 24 * r:24 * r + 24, 128 * c:128 * c + 128] = gq[core, xx, zz, lo] * scale
    for t in range(4):
        nxt = (t + 1) % 4
        side = low[t, :256, :]
        put(256 * nxt, 256 * t, side)
        put(256 * t, 256 * nxt, side.T)
        far = low[t, 256:, :]
        i, j = 256 * (t % 2 + 2) + 128 * (t // 2), 256 * (t % 2)
        put(i, j, far)
        put(j, i, far.T)

    def dot3(lh, ll, rh, rl):
        dot = functools.partial(jnp.dot, preferred_element_type=F32)
        return dot(lh, rh) + (dot(lh, rl) + dot(ll, rh))

    same = lax.broadcasted_iota(jnp.int32, (256, 256), 0) == lax.broadcasted_iota(jnp.int32, (256, 256), 1)

    def store(rows, cols, block):
        a2h[rows, cols], a2l[rows, cols] = split(block)
        value = COEF_B * a[rows, cols] + COEF_C * block
        if rows == cols:
            value = value + jnp.where(same, COEF_A, 0.0)
        mh[rows, cols], ml[rows, cols] = split(value)

    for i in range(4):
        rows = slice(256 * i, 256 * i + 256)
        for j in range(i, 4):
            cols = slice(256 * j, 256 * j + 256)
            block = dot3(ah[rows, :], al[rows, :], ah[:, cols], al[:, cols])
            store(rows, cols, block)
            if j > i:
                store(cols, rows, block.T)

    def times(x, high, lowp, cols=None):
        xh, xl = split(x)
        both = jnp.concatenate([xh, xl], axis=0)
        parts = []
        for at in [cols] if cols is not None else [slice(256 * j, 256 * j + 256) for j in range(4)]:
            first = jnp.dot(both, high[:, at], preferred_element_type=F32)
            second = jnp.dot(xh, lowp[:, at], preferred_element_type=F32)
            parts.append(first[:ROWS] + (first[ROWS:] + second))
        return parts[0] if cols is not None else jnp.concatenate(parts, axis=1)

    own = pl.ds(pl.multiple_of(tp * 256, 256), 256)
    start = jnp.concatenate([x_ref[t] for t in range(4)], axis=1) * inverse
    one = times(start, mh, ml)
    for t in range(4):
        mine[t] = one[:, 256 * t:256 * t + 256]
    turned = times(times(one, mh, ml), mh, ml)
    result = COEF_A * mine[tp] + COEF_B * times(turned, ah, al, own)
    result = result + COEF_C * times(times(times(turned, a2h, a2l), mh, ml), mh, ml, own)
    update = 0.2 * math.sqrt(max(D, FF)) * result
    update_ref[...] = update
    neww_ref[...] = w_ref[...] - LEARN_RATE * (update + WEIGHT_DECAY * w_ref[...])


def orthogonalize(x, gp, gq, weights, new_momentum):
    vmem = pl.BlockSpec(memory_space=pltpu.VMEM)
    block = jax.ShapeDtypeStruct((ROWS, W), F32)
    half = jnp.bfloat16
    return pl.pallas_call(
        finish,
        out_shape=[block] * 3,
        in_specs=[vmem] * 5,
        out_specs=[vmem] * 3,
        scratch_shapes=[
            pltpu.VMEM((FF, FF), F32), pltpu.VMEM((4, 384, W), F32),
            *[pltpu.VMEM((FF, FF), half)] * 6,
            pltpu.VMEM((4, ROWS, W), F32),
        ],
        compiler_params=pltpu.CompilerParams(vmem_limit_bytes=40 * 1024 * 1024),
    )(x, gp, gq, weights, new_momentum)


def on_device(partials, momentum, weights):
    new_momentum, x, gp, gq = communicate(partials[0], momentum)
    return tuple(orthogonalize(x, gp, gq, weights, new_momentum))


def solution(mesh):
    return jax.shard_map(
        on_device,
        mesh=mesh,
        in_specs=(P("dp", None, "tp"), P("dp", "tp"), P("dp", "tp")),
        out_specs=(P("dp", "tp"), P("dp", "tp"), P("dp", "tp")),
        check_vma=False,
    )
```

```python
import functools
import math

import jax
import jax.numpy as jnp
from jax import lax
from jax.experimental import pallas as pl
from jax.experimental.pallas import tpu as pltpu
from jax.sharding import PartitionSpec as P

MESH = pl.DeviceIdType.MESH
F32 = jnp.float32
NX, NY, NZ = 4, 2, 8
ROWS = 112
HEAD = 48
EARLY = 16
TAIL = ROWS - HEAD
HEAD_RING = HEAD - EARLY
TAIL_RING = TAIL - EARLY
W = 256
X_ORDER = (2, 1, 3, 0)
Z_ORDER = (4, 3, 5, 2, 6, 1, 7, 0)
X_GROUPS = ((0, 1), (1, 2), (3, 1))
Z_GROUPS = ((0, 1), (1, 2), (3, 2), (5, 2), (7, 1))
EARLY_Z = Z_GROUPS
UNIT = 0.026
PRIORITY = ("q0", "rp", "q2", "rqz", "rpx", "px", "p1", "q4", "p2", "p0", "q1", "qz", "rq", "q3", "y")
BACKLOG = 5.0
LATE, FAR_LATE = 2.0, 3.0
D = 7168
FF = 1024
COEF_A = 3.4445
COEF_B = -4.775
COEF_C = 2.0315
MOMENTUM_DECAY = 0.95
LEARN_RATE = 0.02
WEIGHT_DECAY = 0.1
NORM_EPS = 1e-07
NESTEROV_GRAD = 1.0 + MOMENTUM_DECAY


def plan(priority, backlog):
    link, cost, needs = {}, {}, {}

    def add(name, k, axis, rows, after=()):
        link[name, k], cost[name, k], needs[name, k] = axis, rows * UNIT, set(after)

    def chain(name, k):
        return {(name, k - 2)} if k >= 2 else set()

    for g, count in enumerate((1, 2, 1)):
        for k in range(NZ - 1):
            add("p%d" % g, k, "z", count * HEAD_RING, chain("p%d" % g, k))
    for g, count in enumerate((1, 2, 2, 2, 1)):
        for k in range(NX - 1):
            add("q%d" % g, k, "x", count * TAIL_RING, chain("q%d" % g, k))
    for k in range(NX - 1):
        g = (k + 1) // 2
        add("px", k, "x", HEAD_RING, chain("px", k) | {("p%d" % g, 5), ("p%d" % g, 6)})
    for k in range(NZ - 1):
        g = (k + 1) // 2
        add("qz", k, "z", TAIL_RING, chain("qz", k) | {("q%d" % g, 1), ("q%d" % g, 2)})
    if EARLY:
        for i in range(9):
            add("y", i, "y", EARLY * (8 if i < 4 else 4 * EARLY_Z[i - 4][1]))
        for k in range(NZ - 1):
            add("rp", k, "z", 2 * EARLY, chain("rp", k) | {("y", 4 + (k + 1) // 2)})
        for k in range(NX - 1):
            add("rq", k, "x", 4 * EARLY, chain("rq", k) | ({("y", 0)} if k == 0 else {("y", 1), ("y", 2)}))
        add("rpx", 0, "x", 2 * EARLY, {("rp", 5), ("rp", 6), ("y", 8)})
        add("rqz", 0, "z", 8 * EARLY, {("rq", 1), ("rq", 2), ("y", 3)})
    free, now, flying, arrived, waiting, order = dict.fromkeys("xyz", 0.0), 0.0, [], set(), list(link), []
    while waiting or flying:
        for axis in "zxy":
            while free[axis] - now < backlog:
                ready = [t for t in waiting if link[t] == axis and needs[t] <= arrived]
                if not ready:
                    break
                pick = min(ready, key=lambda t: (priority.index(t[0]), t[1]))
                waiting.remove(pick)
                free[axis] = max(free[axis], now) + cost[pick]
                late = FAR_LATE if pick[0] in ("rqz", "rpx", "y") else LATE
                flying.append((free[axis] + late, pick))
                order.append(("issue",) + pick)
        when, pick = min(flying)
        flying.remove((when, pick))
        now = max(now, when) + 0.15
        arrived.add(pick)
        order.append(("arrive",) + pick)
    return order, now


class Ring:
    def __init__(self, n, place, own, send, recv, send_sem, recv_sem, span=None):
        self.n, self.place, self.own, self.span = n, place, own, span
        self.send, self.recv, self.send_sem, self.recv_sem = send, recv, send_sem, recv_sem

    def at(self, d, k):
        return (d, k) if self.span is None else (d, k, pl.ds(*self.span))

    def copy(self, d, k):
        return pltpu.make_async_remote_copy(
            src_ref=self.send.at[self.at(d, k)], dst_ref=self.recv.at[self.at(d, k)],
            send_sem=self.send_sem.at[d, k], recv_sem=self.recv_sem.at[d, k],
            device_id=self.place(1 if d == 0 else -1), device_id_type=MESH,
        )

    def offset(self, d, k):
        return (1 if d == 0 else -1) * (self.n // 2 - (k + 1) // 2)

    def issue(self, k):
        for d in range(2):
            value = self.own(self.offset(d, k), (k + d) % 2)
            if k >= 2:
                value = value + self.recv[self.at(d, k - 2)]
            self.send[self.at(d, k)] = value
            self.copy(d, k).start()

    def arrive(self, k):
        for d in range(2):
            self.copy(d, k).wait_recv()

    def total(self, half):
        first, last = self.n - 3 + (half + 1) % 2, self.n - 3 + half
        return self.own(0, half) + self.recv[self.at(0, first)] + self.recv[self.at(1, last)]

    def sent(self):
        for d in range(2):
            for k in range(self.n - 1):
                self.copy(d, k).wait_send()


def split(value):
    high = value.astype(jnp.bfloat16)
    return high, (value - high.astype(F32)).astype(jnp.bfloat16)


def cross(left, right):
    (lh, ll), (rh, rl) = split(left), split(right)
    dims = (((0,), (0,)), ((), ()))
    dot = functools.partial(lax.dot_general, dimension_numbers=dims, preferred_element_type=F32)
    return dot(lh, rh) + (dot(lh, rl) + dot(ll, rh))


def kernel(part_hbm, mom_hbm, newm_ref, xg, gp, gq, part, mom_ref, fin, acc_p, acc_q,
           ry_send, ry_recv, rx_send, rx_recv, rp_send, rp_recv, rq_send, rq_recv, acc_rp, acc_rq, rp2_recv, rq2_recv,
           p_send, p_recv, px_send, px_recv, q_send, q_recv, qz_send, qz_recv,
           same_recv, side_send, side_recv, cross_send, cross_recv,
           src_p, src_q, one_p, one_q, tot_p, tot_q, two_p, two_q,
           load_sem, p_s, p_r, px_s, px_r, q_s, q_r, qz_s, qz_r, y_s, y_r,
           early_s, early_r, rp_s, rp_r, rq_s, rq_r, rp2_s, rp2_r, rq2_s, rq2_r,
           x_s, x_r, g1p_s, g1p_r, g1q_s, g1q_r, g2p_s, g2p_r, g2q_s, g2q_r,
           ap_s, ap_r, aq_s, aq_r, az_s, az_r, ax_s, ax_r, c_s, c_r):
    dp = lax.axis_index("dp")
    tp = lax.axis_index("tp")
    x, yh, z = dp // 16, (dp // 8) % 2, dp % 8
    lo, core = tp // 2, tp % 2
    sibling = (dp, tp ^ 1)
    pending = []

    def x_at(off):
        return lax.rem(x + off + 2 * NX, NX)

    def z_at(off):
        return lax.rem(z + off + 2 * NZ, NZ)

    def at(dx, dy, dz, other=0):
        return (x_at(dx) * 16 + lax.rem(yh + dy, NY) * 8 + z_at(dz), tp ^ (2 * other))

    def remote(src, dst, send_sem, recv_sem, device):
        return pltpu.make_async_remote_copy(
            src_ref=src, dst_ref=dst, send_sem=send_sem, recv_sem=recv_sem, device_id=device, device_id_type=MESH,
        )

    def begin(copy):
        copy.start()
        pending.append(copy)
        return copy

    def drain(keep=0):
        while len(pending) > keep:
            pending.pop(0).wait_send()

    def along_z(step):
        return at(0, 0, step)

    def along_x(step):
        return at(step, 0, 0)

    loads = {}
    for rel in X_ORDER:
        rows = pl.ds(x_at(rel) * 16, 16)
        loads[rel] = pltpu.make_async_copy(part_hbm.at[rows], part.at[rows], load_sem.at[rel])
        loads[rel].start()
    loads["momentum"] = pltpu.make_async_copy(mom_hbm, mom_ref, load_sem.at[NX])
    loads["momentum"].start()

    def need(*names):
        for name in names:
            if name in loads:
                loads.pop(name).wait()

    peers = [along_z(1), along_z(-1), along_x(1), along_x(-1), at(0, 1, 0), at(0, 0, 0, 1), at(0, 1, 0, 1), sibling]
    barrier = pltpu.get_barrier_semaphore()
    for peer in peers:
        pl.semaphore_signal(barrier, inc=1, device_id=peer, device_id_type=MESH)
    pl.semaphore_wait(barrier, len(peers))

    def early_rows(xx, yy, zz, first):
        return part[xx * 16 + yy * 8 + zz, first:first + EARLY, :].astype(F32)

    def early_copy(i):
        if i < 4:
            off = X_ORDER[i]
            src, dst = rx_send.at[off], rx_recv.at[off]
        else:
            span = pl.ds(*EARLY_Z[i - 4])
            src, dst = ry_send.at[span], ry_recv.at[span]
        return remote(src, dst, early_s.at[i], early_r.at[i], at(0, 1, 0))

    def early_issue(i):
        if i < 4:
            off = X_ORDER[i]
            need(off)
            for rel in range(NZ):
                rx_send[off, rel] = early_rows(x_at(off), 1 - yh, z_at(rel), ROWS - EARLY)
        else:
            need(*X_ORDER)
            first, count = EARLY_Z[i - 4]
            for j in range(first, first + count):
                for xx in range(NX):
                    ry_send[j, xx] = early_rows(xx, 1 - yh, z_at(Z_ORDER[j]), HEAD_RING)
        begin(early_copy(i))

    def early_arrive(i):
        early_copy(i).wait_recv()

    def own_rp(off, half):
        need(*X_ORDER)
        j = Z_ORDER.index(off % NZ)
        return jnp.stack([early_rows(xx, yh, z_at(off), HEAD_RING) + ry_recv[j, xx] for xx in (2 * half, 2 * half + 1)])

    def own_rq(off, half):
        need(off % NX)
        return jnp.stack([early_rows(x_at(off), yh, z_at(rel), ROWS - EARLY) + rx_recv[off % NX, rel]
                          for rel in range(4 * half, 4 * half + 4)])

    def rp2_copy(dx):
        return remote(acc_rp.at[x_at(dx)], rp2_recv.at[dx - 1], rp2_s.at[dx - 1], rp2_r.at[dx - 1], along_x(dx))

    def rq2_copy(dz):
        return remote(acc_rq.at[dz], rq2_recv.at[dz - 1], rq2_s.at[dz - 1], rq2_r.at[dz - 1], along_z(dz))

    def early_total(acc, copies, recv, rows):
        total = acc
        for i, copy in enumerate(copies):
            copy.wait_recv()
            total = total + recv[i]
        fin[yh, rows] = total

    def own_p(group):
        first, count = X_GROUPS[group]

        def own(off, half):
            need(*X_ORDER[first:first + count])
            xs = [x_at(rel) for rel in X_ORDER[first:first + count]]
            return jnp.stack([part[xx * 16 + half * 8 + z_at(off), :HEAD_RING, :].astype(F32) for xx in xs])
        return own

    def own_q(group):
        first, count = Z_GROUPS[group]

        def own(off, half):
            need(off % NX)
            zs = [z_at(rel) for rel in Z_ORDER[first:first + count]]
            return jnp.stack([part[x_at(off) * 16 + half * 8 + zz, HEAD:HEAD + TAIL_RING, :].astype(F32) for zz in zs])
        return own

    def own_px(off, half):
        return acc_p[half, X_ORDER.index(off % NX)]

    def own_qz(off, half):
        return acc_q[half, Z_ORDER.index(off % NZ)]

    rings = {
        "px": Ring(NX, along_x, own_px, px_send, px_recv, px_s, px_r),
        "qz": Ring(NZ, along_z, own_qz, qz_send, qz_recv, qz_s, qz_r),
        "rp": Ring(NZ, along_z, own_rp, rp_send, rp_recv, rp_s, rp_r),
        "rq": Ring(NX, along_x, own_rq, rq_send, rq_recv, rq_s, rq_r),
    }
    for g, span in enumerate(X_GROUPS):
        rings["p%d" % g] = Ring(NZ, along_z, own_p(g), p_send, p_recv, p_s.at[g], p_r.at[g], span)
    for g, span in enumerate(Z_GROUPS):
        rings["q%d" % g] = Ring(NX, along_x, own_q(g), q_send, q_recv, q_s.at[g], q_r.at[g], span)

    def final(name):
        if name == "columns0":
            early_total(acc_rp[x], [rp2_copy(dx) for dx in (1, 2, 3)], rp2_recv, pl.ds(HEAD_RING, EARLY))
            for half in range(2):
                fin[half, :HEAD_RING] = rings["px"].total(half)
            columns_start(0)
        elif name == "columns1":
            early_total(acc_rq[0], [rq2_copy(dz) for dz in range(1, NZ)], rq2_recv, pl.ds(ROWS - EARLY, EARLY))
            for half in range(2):
                fin[half, HEAD:HEAD + TAIL_RING] = rings["qz"].total(half)
            columns_start(1)
        elif name == "rpx":
            for half in range(2):
                acc_rp[pl.ds(2 * half, 2)] = rings["rp"].total(half)
            for dx in (2, 1, 3):
                begin(rp2_copy(dx))
        elif name == "rqz":
            for half in range(2):
                acc_rq[pl.ds(4 * half, 4)] = rings["rq"].total(half)
            for dz in (4, 3, 5, 2, 6, 1, 7):
                begin(rq2_copy(dz))
        else:
            acc = acc_p if name[0] == "p" else acc_q
            for half in range(2):
                acc[half, pl.ds(*rings[name].span)] = rings[name].total(half)

    def columns_start(i):
        need("momentum")
        rows = pl.ds(0, HEAD) if i == 0 else pl.ds(HEAD, TAIL)
        half = pl.ds(0, HEAD_RING) if i == 0 else pl.ds(HEAD, TAIL_RING)
        begin(remote(fin.at[1 - yh, half], same_recv.at[half], y_s.at[0, i], y_r.at[0, i], at(0, 1, 0)))
        cross_send[half] = NESTEROV_GRAD * fin[1 - yh, half]
        begin(remote(cross_send.at[half], cross_recv.at[half], y_s.at[1, i], y_r.at[1, i], at(0, 1, 0, 1)))
        side_send[rows] = NESTEROV_GRAD * fin[yh, rows] + MOMENTUM_DECAY * MOMENTUM_DECAY * mom_ref[rows]
        begin(remote(side_send.at[rows], side_recv.at[rows], y_s.at[2, i], y_r.at[2, i], at(0, 0, 0, 1)))

    def columns_end(i):
        rows = pl.ds(0, HEAD) if i == 0 else pl.ds(HEAD, TAIL)
        half = pl.ds(0, HEAD_RING) if i == 0 else pl.ds(HEAD, TAIL_RING)
        for buf, j, span in ((same_recv, 0, half), (cross_recv, 1, half), (side_recv, 2, rows)):
            remote(buf.at[span], buf.at[span], y_s.at[j, i], y_r.at[j, i], sibling).wait_recv()
        gradient = fin[yh, rows] + same_recv[rows]
        new_momentum = MOMENTUM_DECAY * mom_ref[rows] + gradient
        newm_ref[rows] = new_momentum
        xg[tp, rows] = gradient + MOMENTUM_DECAY * new_momentum
        xg[tp ^ 2, rows] = side_recv[rows] + cross_recv[rows]
        for j, slot in enumerate((tp, tp ^ 2)):
            mine = xg.at[slot, rows]
            begin(remote(mine, mine, x_s.at[j, i], x_r.at[j, i], sibling))

    def columns_wait(i):
        rows = pl.ds(0, HEAD) if i == 0 else pl.ds(HEAD, TAIL)
        for j, slot in enumerate((tp ^ 1, tp ^ 3)):
            other = xg.at[slot, rows]
            remote(other, other, x_s.at[j, i], x_r.at[j, i], sibling).wait_recv()

    for rows in (pl.ds(HEAD_RING, EARLY), pl.ds(ROWS - EARLY, EARLY)):
        same_recv[rows] = jnp.zeros((EARLY, W), F32)
        cross_recv[rows] = jnp.zeros((EARLY, W), F32)
    order, _ = plan(PRIORITY, BACKLOG)
    left = {name: {(name, ring.n - 3), (name, ring.n - 2)} for name, ring in rings.items() if ring.span is not None}
    left["columns0"] = {("px", 1), ("px", 2), ("rpx", 0), ("p2", 5), ("p2", 6)}
    left["columns1"] = {("qz", 5), ("qz", 6), ("rqz", 0), ("q4", 1), ("q4", 2)}
    for what, name, k in order:
        if what == "issue":
            if name == "y":
                early_issue(k)
            elif name in ("rpx", "rqz"):
                final(name)
            else:
                rings[name].issue(k)
            continue
        if name == "y":
            early_arrive(k)
        elif name in rings:
            rings[name].arrive(k)
        for key in [key for key in left if (name, k) in left[key]]:
            left[key].discard((name, k))
            if not left[key]:
                final(key)
    columns_end(0)
    columns_end(1)
    columns_wait(0)

    def place(block, rows):
        for xx in range(NX):
            for zz in range(NZ):
                r = rows * ((xx % 2) * 8 + zz)
                yield xx, zz, block[r:r + rows, 128 * (xx // 2):128 * (xx // 2) + 128]

    own_x = xg[tp]
    for xx, zz, value in place(cross(own_x, own_x), 16):
        src_p[zz, xx] = value
    rp = [(dz, remote(src_p.at[z_at(dz)], one_p.at[dz - 1], g1p_s.at[dz - 1], g1p_r.at[dz - 1], along_z(dz)))
          for dz in (4, 3, 5, 2, 6, 1, 7)]
    for _, copy in rp:
        begin(copy)
    columns_wait(1)
    high_x = xg[tp % 2 + 2]
    left = jnp.where(tp < 2, high_x[:, :128], high_x[:, 128:])
    lower = jnp.concatenate([cross(xg[lax.rem(tp + 1, 4)], own_x), cross(left, xg[tp % 2])], axis=0)
    for xx, zz, value in place(lower, 24):
        src_q[xx, zz] = value
    rq = [(dx, remote(src_q.at[x_at(dx)], one_q.at[dx - 1], g1q_s.at[dx - 1], g1q_r.at[dx - 1], along_x(dx)))
          for dx in (2, 1, 3)]
    for _, copy in rq:
        begin(copy)
    for ring in rings.values():
        ring.sent()

    second_p, second_q = [], []
    for _, copy in rq:
        copy.wait_recv()
    total = src_q[x]
    for i in range(NX - 1):
        total = total + one_q[i]
    tot_q[...] = total
    for dz in (4, 3, 5, 2, 6, 1, 7, 0):
        for dy in range(2):
            if dz or dy:
                i = dy * NZ + dz
                second_q.append(begin(remote(tot_q.at[z_at(dz)], two_q.at[i], g2q_s.at[i], g2q_r.at[i], at(0, dy, dz))))
    for _, copy in rp:
        copy.wait_recv()
    total = src_p[z]
    for i in range(NZ - 1):
        total = total + one_p[i]
    tot_p[...] = total
    for dx in (2, 1, 3, 0):
        for dy in range(2):
            if dx or dy:
                i = dy * NX + dx
                second_p.append(begin(remote(tot_p.at[x_at(dx)], two_p.at[i], g2p_s.at[i], g2p_r.at[i], at(dx, dy, 0))))

    near_p, near_q = [], []
    for copy in second_p:
        copy.wait_recv()
    total = tot_p[x]
    for i in range(1, 2 * NX):
        total = total + two_p[i]
    mine = gp.at[core, z, x, lo]
    mine[...] = total
    for dx in (2, 1, 3, 0):
        for dy in range(2):
            if dx or dy:
                i = dy * NX + dx
                near_p.append(begin(remote(mine, mine, ap_s.at[i], ap_r.at[i], at(dx, 0, 0, dy))))
    for copy in second_q:
        copy.wait_recv()
    total = tot_q[z]
    for i in range(1, 2 * NZ):
        total = total + two_q[i]
    mine_q = gq.at[core, x, z, lo]
    mine_q[...] = total
    for dz in (4, 3, 5, 2, 6, 1, 7, 0):
        for dy in range(2):
            if dz or dy:
                i = dy * NZ + dz
                near_q.append(begin(remote(mine_q, mine_q, aq_s.at[i], aq_r.at[i], at(0, 0, dz, dy))))

    drain(len(near_p) + len(near_q))

    def pass_z(d, hop, sub):
        sign = 1 if d == 0 else -1
        chunk = gp.at[core, z_at(-sign * hop), pl.ds(2 * sub, 2)]
        return remote(chunk, chunk, az_s.at[d, hop, sub], az_r.at[d, hop, sub], along_z(sign))

    def pass_x(d, part_at):
        sign = 1 if d == 0 else -1
        half = d if part_at != 1 else 1 - d
        chunk = gq.at[core, x if part_at < 2 else x_at(-sign), pl.ds(4 * half, 4)]
        return remote(chunk, chunk, ax_s.at[d, part_at], ax_r.at[d, part_at], along_x(sign))

    shared = []

    def share(chunk):
        i = len(shared)
        shared.append(remote(chunk, chunk, c_s.at[i], c_r.at[i], sibling))
        shared[-1].start()

    for copy in near_p:
        copy.wait_recv()
    for turn in range(2):
        for d in range(2):
            begin(pass_z(d, 0, d ^ turn))
    share(gp.at[core, z])

    def z_step(hop, turn):
        for d in range(2):
            sub = d ^ turn
            pass_z(d, hop, sub).wait_recv()
            if hop < 2 or (hop == 2 and turn == 0):
                begin(pass_z(d, hop + 1, sub))
        for d in range(2):
            sign = 1 if d == 0 else -1
            if hop == 3:
                share(gp.at[core, z_at(4), pl.ds(2 * d, 2)])
            elif turn == 1:
                share(gp.at[core, z_at(-sign * (hop + 1))])

    def x_step(part_at):
        for d in range(2):
            pass_x(d, part_at).wait_recv()
            if part_at == 0:
                begin(pass_x(d, 2))
        for d in range(2):
            sign = 1 if d == 0 else -1
            half = d if part_at != 1 else 1 - d
            share(gq.at[core, x_at(-sign if part_at < 2 else 2), pl.ds(4 * half, 4)])

    z_step(0, 0)
    for copy in near_q:
        copy.wait_recv()
    for part_at in range(2):
        for d in range(2):
            begin(pass_x(d, part_at))
    share(gq.at[core, x])
    z_step(0, 1)
    z_step(1, 0)
    z_step(1, 1)
    x_step(0)
    z_step(2, 0)
    z_step(2, 1)
    x_step(1)
    z_step(3, 0)
    x_step(2)
    drain()
    for copy in shared:
        copy.wait()


def communicate(partials, momentum):
    def ring(n, *block):
        return [pltpu.VMEM((2, n - 1) + block, F32)] * 2

    def sems(*shape):
        return [pltpu.SemaphoreType.DMA(shape)] * 2

    vmem = pl.BlockSpec(memory_space=pltpu.VMEM)
    block = pltpu.VMEM((ROWS, W), F32)
    return pl.pallas_call(
        kernel,
        out_shape=[
            jax.ShapeDtypeStruct((ROWS, W), F32),
            jax.ShapeDtypeStruct((4, ROWS, W), F32),
            jax.ShapeDtypeStruct((2, NZ, NX, 2, 16, 128), F32),
            jax.ShapeDtypeStruct((2, NX, NZ, 2, 24, 128), F32),
        ],
        in_specs=[pl.BlockSpec(memory_space=pltpu.HBM)] * 2,
        out_specs=[vmem] * 4,
        scratch_shapes=[
            pltpu.VMEM((64, ROWS, W), jnp.bfloat16),
            block,
            pltpu.VMEM((2, ROWS, W), F32),
            pltpu.VMEM((2, NX, HEAD_RING, W), F32),
            pltpu.VMEM((2, NZ, TAIL_RING, W), F32),
            *[pltpu.VMEM((NZ, NX, EARLY, W), F32)] * 2, *[pltpu.VMEM((NX, NZ, EARLY, W), F32)] * 2,
            *ring(NZ, 2, EARLY, W), *ring(NX, 4, EARLY, W),
            pltpu.VMEM((NX, EARLY, W), F32), pltpu.VMEM((NZ, EARLY, W), F32),
            pltpu.VMEM((NX - 1, EARLY, W), F32), pltpu.VMEM((NZ - 1, EARLY, W), F32),
            *ring(NZ, NX, HEAD_RING, W), *ring(NX, HEAD_RING, W), *ring(NX, NZ, TAIL_RING, W), *ring(NZ, TAIL_RING, W),
            block, block, block, block, block,
            pltpu.VMEM((NZ, NX, 16, 128), F32), pltpu.VMEM((NX, NZ, 24, 128), F32),
            pltpu.VMEM((NZ - 1, NX, 16, 128), F32), pltpu.VMEM((NX - 1, NZ, 24, 128), F32),
            pltpu.VMEM((NX, 16, 128), F32), pltpu.VMEM((NZ, 24, 128), F32),
            pltpu.VMEM((2 * NX, 16, 128), F32), pltpu.VMEM((2 * NZ, 24, 128), F32),
            pltpu.SemaphoreType.DMA((NX + 1,)),
            *sems(3, 2, NZ - 1), *sems(2, NX - 1), *sems(5, 2, NX - 1), *sems(2, NZ - 1),
            *sems(3, 2),
            *sems(9), *sems(2, NZ - 1), *sems(2, NX - 1), *sems(NX - 1), *sems(NZ - 1),
            *sems(2, 2),
            *sems(NZ - 1), *sems(NX - 1), *sems(2 * NX), *sems(2 * NZ),
            *sems(2 * NX), *sems(2 * NZ), *sems(2, 4, 2), *sems(2, 3), *sems(18),
        ],
        compiler_params=pltpu.CompilerParams(collective_id=0, has_side_effects=True, vmem_limit_bytes=49 * 1024 * 1024),
    )(partials.reshape(64, ROWS, W), momentum)


def finish(x_ref, gp, gq, w_ref, m_ref, update_ref, neww_ref, newm_ref,
           a, low, ah, al, a2h, a2l, mh, ml, mine):
    tp = lax.axis_index("tp")
    newm_ref[...] = m_ref[...]
    row, col = (lax.broadcasted_iota(jnp.int32, (16, 128), axis) for axis in range(2))
    square = jnp.zeros((16, 128), F32)
    for t in range(4):
        for zz in range(NZ):
            for xx in (0, 3):
                square = square + jnp.where(col - row == 16 * zz, gp[t % 2, zz, xx, t // 2], 0.0)
    inverse = 1.0 / (jnp.sqrt(jnp.sum(square, keepdims=True)) + NORM_EPS)
    scale = inverse * inverse

    def put(first_row, first_col, value):
        rows = slice(first_row, first_row + value.shape[0])
        cols = slice(first_col, first_col + value.shape[1])
        a[rows, cols] = value
        ah[rows, cols], al[rows, cols] = split(value)

    for t in range(4):
        core, lo, base = t % 2, t // 2, 256 * t
        for xx in range(NX):
            for zz in range(NZ):
                r, c = (xx % 2) * 8 + zz, xx // 2
                put(base + 16 * r, base + 128 * c, gp[core, zz, xx, lo] * scale)
                low[t, 24 * r:24 * r + 24, 128 * c:128 * c + 128] = gq[core, xx, zz, lo] * scale
    for t in range(4):
        nxt = (t + 1) % 4
        side = low[t, :256, :]
        put(256 * nxt, 256 * t, side)
        put(256 * t, 256 * nxt, side.T)
        far = low[t, 256:, :]
        i, j = 256 * (t % 2 + 2) + 128 * (t // 2), 256 * (t % 2)
        put(i, j, far)
        put(j, i, far.T)

    def dot3(lh, ll, rh, rl):
        dot = functools.partial(jnp.dot, preferred_element_type=F32)
        return dot(lh, rh) + (dot(lh, rl) + dot(ll, rh))

    same = lax.broadcasted_iota(jnp.int32, (256, 256), 0) == lax.broadcasted_iota(jnp.int32, (256, 256), 1)

    def store(rows, cols, block):
        a2h[rows, cols], a2l[rows, cols] = split(block)
        value = COEF_B * a[rows, cols] + COEF_C * block
        if rows == cols:
            value = value + jnp.where(same, COEF_A, 0.0)
        mh[rows, cols], ml[rows, cols] = split(value)

    for i in range(4):
        rows = slice(256 * i, 256 * i + 256)
        for j in range(i, 4):
            cols = slice(256 * j, 256 * j + 256)
            block = dot3(ah[rows, :], al[rows, :], ah[:, cols], al[:, cols])
            store(rows, cols, block)
            if j > i:
                store(cols, rows, block.T)

    def times(x, high, lowp, cols=None):
        xh, xl = split(x)
        both = jnp.concatenate([xh, xl], axis=0)
        parts = []
        for at in [cols] if cols is not None else [slice(256 * j, 256 * j + 256) for j in range(4)]:
            first = jnp.dot(both, high[:, at], preferred_element_type=F32)
            second = jnp.dot(xh, lowp[:, at], preferred_element_type=F32)
            parts.append(first[:ROWS] + (first[ROWS:] + second))
        return parts[0] if cols is not None else jnp.concatenate(parts, axis=1)

    own = pl.ds(pl.multiple_of(tp * 256, 256), 256)
    start = jnp.concatenate([x_ref[t] for t in range(4)], axis=1) * inverse
    one = times(start, mh, ml)
    for t in range(4):
        mine[t] = one[:, 256 * t:256 * t + 256]
    turned = times(times(one, mh, ml), mh, ml)
    result = COEF_A * mine[tp] + COEF_B * times(turned, ah, al, own)
    result = result + COEF_C * times(times(times(turned, a2h, a2l), mh, ml), mh, ml, own)
    update = 0.2 * math.sqrt(max(D, FF)) * result
    update_ref[...] = update
    neww_ref[...] = w_ref[...] - LEARN_RATE * (update + WEIGHT_DECAY * w_ref[...])


def orthogonalize(x, gp, gq, weights, new_momentum):
    vmem = pl.BlockSpec(memory_space=pltpu.VMEM)
    block = jax.ShapeDtypeStruct((ROWS, W), F32)
    half = jnp.bfloat16
    return pl.pallas_call(
        finish,
        out_shape=[block] * 3,
        in_specs=[vmem] * 5,
        out_specs=[vmem] * 3,
        scratch_shapes=[
            pltpu.VMEM((FF, FF), F32), pltpu.VMEM((4, 384, W), F32),
            *[pltpu.VMEM((FF, FF), half)] * 6,
            pltpu.VMEM((4, ROWS, W), F32),
        ],
        compiler_params=pltpu.CompilerParams(vmem_limit_bytes=40 * 1024 * 1024),
    )(x, gp, gq, weights, new_momentum)


def on_device(partials, momentum, weights):
    new_momentum, x, gp, gq = communicate(partials[0], momentum)
    return tuple(orthogonalize(x, gp, gq, weights, new_momentum))


def solution(mesh):
    return jax.shard_map(
        on_device,
        mesh=mesh,
        in_specs=(P("dp", None, "tp"), P("dp", "tp"), P("dp", "tp")),
        out_specs=(P("dp", "tp"), P("dp", "tp"), P("dp", "tp")),
        check_vma=False,
    )
```

```python
import functools
import math

import jax
import jax.numpy as jnp
from jax import lax
from jax.experimental import pallas as pl
from jax.experimental.pallas import tpu as pltpu
from jax.sharding import PartitionSpec as P

MESH = pl.DeviceIdType.MESH
F32 = jnp.float32
NX, NY, NZ = 4, 2, 8
ROWS = 112
HEAD = 48
EARLY = 16
TAIL = ROWS - HEAD
HEAD_RING = HEAD - EARLY
TAIL_RING = TAIL - EARLY
W = 256
X_ORDER = (2, 1, 3, 0)
Z_ORDER = (4, 3, 5, 2, 6, 1, 7, 0)
X_GROUPS = ((0, 1), (1, 2), (3, 1))
Z_GROUPS = ((0, 1), (1, 2), (3, 2), (5, 2), (7, 1))
EARLY_Z = Z_GROUPS
UNIT = 0.026
PRIORITY = ("q0", "rp", "q2", "rqz", "rpx", "px", "p1", "q4", "p2", "p0", "q1", "qz", "rq", "q3", "y")
BACKLOG = 5.0
LATE, FAR_LATE = 2.0, 3.0
D = 7168
FF = 1024
COEF_A = 3.4445
COEF_B = -4.775
COEF_C = 2.0315
MOMENTUM_DECAY = 0.95
LEARN_RATE = 0.02
WEIGHT_DECAY = 0.1
NORM_EPS = 1e-07
NESTEROV_GRAD = 1.0 + MOMENTUM_DECAY


def plan(priority, backlog):
    link, cost, needs = {}, {}, {}

    def add(name, k, axis, rows, after=()):
        link[name, k], cost[name, k], needs[name, k] = axis, rows * UNIT, set(after)

    def chain(name, k):
        return {(name, k - 2)} if k >= 2 else set()

    for g, count in enumerate((1, 2, 1)):
        for k in range(NZ - 1):
            add("p%d" % g, k, "z", count * HEAD_RING, chain("p%d" % g, k))
    for g, count in enumerate((1, 2, 2, 2, 1)):
        for k in range(NX - 1):
            add("q%d" % g, k, "x", count * TAIL_RING, chain("q%d" % g, k))
    for k in range(NX - 1):
        g = (k + 1) // 2
        add("px", k, "x", HEAD_RING, chain("px", k) | {("p%d" % g, 5), ("p%d" % g, 6)})
    for k in range(NZ - 1):
        g = (k + 1) // 2
        add("qz", k, "z", TAIL_RING, chain("qz", k) | {("q%d" % g, 1), ("q%d" % g, 2)})
    if EARLY:
        for i in range(9):
            add("y", i, "y", EARLY * (8 if i < 4 else 4 * EARLY_Z[i - 4][1]))
        for k in range(NZ - 1):
            add("rp", k, "z", 2 * EARLY, chain("rp", k) | {("y", 4 + (k + 1) // 2)})
        for k in range(NX - 1):
            add("rq", k, "x", 4 * EARLY, chain("rq", k) | ({("y", 0)} if k == 0 else {("y", 1), ("y", 2)}))
        add("rpx", 0, "x", 2 * EARLY, {("rp", 5), ("rp", 6), ("y", 8)})
        add("rqz", 0, "z", 8 * EARLY, {("rq", 1), ("rq", 2), ("y", 3)})
    free, now, flying, arrived, waiting, order = dict.fromkeys("xyz", 0.0), 0.0, [], set(), list(link), []
    while waiting or flying:
        for axis in "zxy":
            while free[axis] - now < backlog:
                ready = [t for t in waiting if link[t] == axis and needs[t] <= arrived]
                if not ready:
                    break
                pick = min(ready, key=lambda t: (priority.index(t[0]), t[1]))
                waiting.remove(pick)
                free[axis] = max(free[axis], now) + cost[pick]
                late = FAR_LATE if pick[0] in ("rqz", "rpx", "y") else LATE
                flying.append((free[axis] + late, pick))
                order.append(("issue",) + pick)
        when, pick = min(flying)
        flying.remove((when, pick))
        now = max(now, when) + 0.15
        arrived.add(pick)
        order.append(("arrive",) + pick)
    return order, now


class Ring:
    def __init__(self, n, place, own, send, recv, send_sem, recv_sem, span=None):
        self.n, self.place, self.own, self.span = n, place, own, span
        self.send, self.recv, self.send_sem, self.recv_sem = send, recv, send_sem, recv_sem

    def at(self, d, k):
        return (d, k) if self.span is None else (d, k, pl.ds(*self.span))

    def copy(self, d, k):
        return pltpu.make_async_remote_copy(
            src_ref=self.send.at[self.at(d, k)], dst_ref=self.recv.at[self.at(d, k)],
            send_sem=self.send_sem.at[d, k], recv_sem=self.recv_sem.at[d, k],
            device_id=self.place(1 if d == 0 else -1), device_id_type=MESH,
        )

    def offset(self, d, k):
        return (1 if d == 0 else -1) * (self.n // 2 - (k + 1) // 2)

    def issue(self, k):
        for d in range(2):
            value = self.own(self.offset(d, k), (k + d) % 2)
            if k >= 2:
                value = value + self.recv[self.at(d, k - 2)]
            self.send[self.at(d, k)] = value
            self.copy(d, k).start()

    def arrive(self, k):
        for d in range(2):
            self.copy(d, k).wait_recv()

    def total(self, half):
        first, last = self.n - 3 + (half + 1) % 2, self.n - 3 + half
        return self.own(0, half) + self.recv[self.at(0, first)] + self.recv[self.at(1, last)]

    def sent(self):
        for d in range(2):
            for k in range(self.n - 1):
                self.copy(d, k).wait_send()


def split(value):
    high = value.astype(jnp.bfloat16)
    return high, (value - high.astype(F32)).astype(jnp.bfloat16)


def cross(left, right):
    (lh, ll), (rh, rl) = split(left), split(right)
    dims = (((0,), (0,)), ((), ()))
    dot = functools.partial(lax.dot_general, dimension_numbers=dims, preferred_element_type=F32)
    return dot(lh, rh) + (dot(lh, rl) + dot(ll, rh))


def kernel(part_hbm, mom_hbm, newm_ref, xg, gp, gq, part, mom_ref, fin, acc_p, acc_q,
           ry_send, ry_recv, rx_send, rx_recv, rp_send, rp_recv, rq_send, rq_recv, acc_rp, acc_rq, rp2_recv, rq2_recv,
           p_send, p_recv, px_send, px_recv, q_send, q_recv, qz_send, qz_recv,
           same_recv, side_send, side_recv, cross_send, cross_recv,
           src_p, src_q, one_p, one_q, tot_p, tot_q, two_p, two_q,
           load_sem, p_s, p_r, px_s, px_r, q_s, q_r, qz_s, qz_r, y_s, y_r,
           early_s, early_r, rp_s, rp_r, rq_s, rq_r, rp2_s, rp2_r, rq2_s, rq2_r,
           x_s, x_r, g1p_s, g1p_r, g1q_s, g1q_r, g2p_s, g2p_r, g2q_s, g2q_r,
           ap_s, ap_r, aq_s, aq_r, az_s, az_r, ax_s, ax_r, c_s, c_r):
    dp = lax.axis_index("dp")
    tp = lax.axis_index("tp")
    x, yh, z = dp // 16, (dp // 8) % 2, dp % 8
    lo, core = tp // 2, tp % 2
    sibling = (dp, tp ^ 1)
    pending = []

    def x_at(off):
        return lax.rem(x + off + 2 * NX, NX)

    def z_at(off):
        return lax.rem(z + off + 2 * NZ, NZ)

    def at(dx, dy, dz, other=0):
        return (x_at(dx) * 16 + lax.rem(yh + dy, NY) * 8 + z_at(dz), tp ^ (2 * other))

    def remote(src, dst, send_sem, recv_sem, device):
        return pltpu.make_async_remote_copy(
            src_ref=src, dst_ref=dst, send_sem=send_sem, recv_sem=recv_sem, device_id=device, device_id_type=MESH,
        )

    def begin(copy):
        copy.start()
        pending.append(copy)
        return copy

    def drain(keep=0):
        while len(pending) > keep:
            pending.pop(0).wait_send()

    def along_z(step):
        return at(0, 0, step)

    def along_x(step):
        return at(step, 0, 0)

    loads = {}
    for rel in X_ORDER:
        rows = pl.ds(x_at(rel) * 16, 16)
        loads[rel] = pltpu.make_async_copy(part_hbm.at[rows], part.at[rows], load_sem.at[rel])
        loads[rel].start()
    loads["momentum"] = pltpu.make_async_copy(mom_hbm, mom_ref, load_sem.at[NX])
    loads["momentum"].start()

    def need(*names):
        for name in names:
            if name in loads:
                loads.pop(name).wait()

    peers = [along_z(1), along_z(-1), along_x(1), along_x(-1), at(0, 1, 0), at(0, 0, 0, 1), at(0, 1, 0, 1), sibling]
    barrier = pltpu.get_barrier_semaphore()
    for peer in peers:
        pl.semaphore_signal(barrier, inc=1, device_id=peer, device_id_type=MESH)
    pl.semaphore_wait(barrier, len(peers))

    def early_rows(xx, yy, zz, first):
        return part[xx * 16 + yy * 8 + zz, first:first + EARLY, :].astype(F32)

    def early_copy(i):
        if i < 4:
            off = X_ORDER[i]
            src, dst = rx_send.at[off], rx_recv.at[off]
        else:
            span = pl.ds(*EARLY_Z[i - 4])
            src, dst = ry_send.at[span], ry_recv.at[span]
        return remote(src, dst, early_s.at[i], early_r.at[i], at(0, 1, 0))

    def early_issue(i):
        if i < 4:
            off = X_ORDER[i]
            need(off)
            for rel in range(NZ):
                rx_send[off, rel] = early_rows(x_at(off), 1 - yh, z_at(rel), ROWS - EARLY)
        else:
            need(*X_ORDER)
            first, count = EARLY_Z[i - 4]
            for j in range(first, first + count):
                for xx in range(NX):
                    ry_send[j, xx] = early_rows(xx, 1 - yh, z_at(Z_ORDER[j]), HEAD_RING)
        begin(early_copy(i))

    def early_arrive(i):
        early_copy(i).wait_recv()

    def own_rp(off, half):
        need(*X_ORDER)
        j = Z_ORDER.index(off % NZ)
        return jnp.stack([early_rows(xx, yh, z_at(off), HEAD_RING) + ry_recv[j, xx] for xx in (2 * half, 2 * half + 1)])

    def own_rq(off, half):
        need(off % NX)
        return jnp.stack([early_rows(x_at(off), yh, z_at(rel), ROWS - EARLY) + rx_recv[off % NX, rel]
                          for rel in range(4 * half, 4 * half + 4)])

    def rp2_copy(dx):
        return remote(acc_rp.at[x_at(dx)], rp2_recv.at[dx - 1], rp2_s.at[dx - 1], rp2_r.at[dx - 1], along_x(dx))

    def rq2_copy(dz):
        return remote(acc_rq.at[dz], rq2_recv.at[dz - 1], rq2_s.at[dz - 1], rq2_r.at[dz - 1], along_z(dz))

    def early_total(acc, copies, recv, rows):
        total = acc
        for i, copy in enumerate(copies):
            copy.wait_recv()
            total = total + recv[i]
        fin[yh, rows] = total

    def own_p(group):
        first, count = X_GROUPS[group]

        def own(off, half):
            need(*X_ORDER[first:first + count])
            xs = [x_at(rel) for rel in X_ORDER[first:first + count]]
            return jnp.stack([part[xx * 16 + half * 8 + z_at(off), :HEAD_RING, :].astype(F32) for xx in xs])
        return own

    def own_q(group):
        first, count = Z_GROUPS[group]

        def own(off, half):
            need(off % NX)
            zs = [z_at(rel) for rel in Z_ORDER[first:first + count]]
            return jnp.stack([part[x_at(off) * 16 + half * 8 + zz, HEAD:HEAD + TAIL_RING, :].astype(F32) for zz in zs])
        return own

    def own_px(off, half):
        return acc_p[half, X_ORDER.index(off % NX)]

    def own_qz(off, half):
        return acc_q[half, Z_ORDER.index(off % NZ)]

    rings = {
        "px": Ring(NX, along_x, own_px, px_send, px_recv, px_s, px_r),
        "qz": Ring(NZ, along_z, own_qz, qz_send, qz_recv, qz_s, qz_r),
        "rp": Ring(NZ, along_z, own_rp, rp_send, rp_recv, rp_s, rp_r),
        "rq": Ring(NX, along_x, own_rq, rq_send, rq_recv, rq_s, rq_r),
    }
    for g, span in enumerate(X_GROUPS):
        rings["p%d" % g] = Ring(NZ, along_z, own_p(g), p_send, p_recv, p_s.at[g], p_r.at[g], span)
    for g, span in enumerate(Z_GROUPS):
        rings["q%d" % g] = Ring(NX, along_x, own_q(g), q_send, q_recv, q_s.at[g], q_r.at[g], span)

    def final(name):
        if name == "columns0":
            early_total(acc_rp[x], [rp2_copy(dx) for dx in (1, 2, 3)], rp2_recv, pl.ds(HEAD_RING, EARLY))
            for half in range(2):
                fin[half, :HEAD_RING] = rings["px"].total(half)
            columns_start(0)
        elif name == "columns1":
            early_total(acc_rq[0], [rq2_copy(dz) for dz in range(1, NZ)], rq2_recv, pl.ds(ROWS - EARLY, EARLY))
            for half in range(2):
                fin[half, HEAD:HEAD + TAIL_RING] = rings["qz"].total(half)
            columns_start(1)
        elif name == "rpx":
            for half in range(2):
                acc_rp[pl.ds(2 * half, 2)] = rings["rp"].total(half)
            for dx in (2, 1, 3):
                begin(rp2_copy(dx))
        elif name == "rqz":
            for half in range(2):
                acc_rq[pl.ds(4 * half, 4)] = rings["rq"].total(half)
            for dz in (4, 3, 5, 2, 6, 1, 7):
                begin(rq2_copy(dz))
        else:
            acc = acc_p if name[0] == "p" else acc_q
            for half in range(2):
                acc[half, pl.ds(*rings[name].span)] = rings[name].total(half)

    def columns_start(i):
        need("momentum")
        rows = pl.ds(0, HEAD) if i == 0 else pl.ds(HEAD, TAIL)
        half = pl.ds(0, HEAD_RING) if i == 0 else pl.ds(HEAD, TAIL_RING)
        begin(remote(fin.at[1 - yh, half], same_recv.at[half], y_s.at[0, i], y_r.at[0, i], at(0, 1, 0)))
        cross_send[half] = NESTEROV_GRAD * fin[1 - yh, half]
        begin(remote(cross_send.at[half], cross_recv.at[half], y_s.at[1, i], y_r.at[1, i], at(0, 1, 0, 1)))
        side_send[rows] = NESTEROV_GRAD * fin[yh, rows] + MOMENTUM_DECAY * MOMENTUM_DECAY * mom_ref[rows]
        begin(remote(side_send.at[rows], side_recv.at[rows], y_s.at[2, i], y_r.at[2, i], at(0, 0, 0, 1)))

    def columns_end(i):
        rows = pl.ds(0, HEAD) if i == 0 else pl.ds(HEAD, TAIL)
        half = pl.ds(0, HEAD_RING) if i == 0 else pl.ds(HEAD, TAIL_RING)
        for buf, j, span in ((same_recv, 0, half), (cross_recv, 1, half), (side_recv, 2, rows)):
            remote(buf.at[span], buf.at[span], y_s.at[j, i], y_r.at[j, i], sibling).wait_recv()
        gradient = fin[yh, rows] + same_recv[rows]
        new_momentum = MOMENTUM_DECAY * mom_ref[rows] + gradient
        newm_ref[rows] = new_momentum
        xg[tp, rows] = gradient + MOMENTUM_DECAY * new_momentum
        xg[tp ^ 2, rows] = side_recv[rows] + cross_recv[rows]
        for j, slot in enumerate((tp, tp ^ 2)):
            mine = xg.at[slot, rows]
            begin(remote(mine, mine, x_s.at[j, i], x_r.at[j, i], sibling))

    def columns_wait(i):
        rows = pl.ds(0, HEAD) if i == 0 else pl.ds(HEAD, TAIL)
        for j, slot in enumerate((tp ^ 1, tp ^ 3)):
            other = xg.at[slot, rows]
            remote(other, other, x_s.at[j, i], x_r.at[j, i], sibling).wait_recv()

    for rows in (pl.ds(HEAD_RING, EARLY), pl.ds(ROWS - EARLY, EARLY)):
        same_recv[rows] = jnp.zeros((EARLY, W), F32)
        cross_recv[rows] = jnp.zeros((EARLY, W), F32)
    order, _ = plan(PRIORITY, BACKLOG)
    left = {name: {(name, ring.n - 3), (name, ring.n - 2)} for name, ring in rings.items() if ring.span is not None}
    left["columns0"] = {("px", 1), ("px", 2), ("rpx", 0), ("p2", 5), ("p2", 6)}
    left["columns1"] = {("qz", 5), ("qz", 6), ("rqz", 0), ("q4", 1), ("q4", 2)}
    for what, name, k in order:
        if what == "issue":
            if name == "y":
                early_issue(k)
            elif name in ("rpx", "rqz"):
                final(name)
            else:
                rings[name].issue(k)
            continue
        if name == "y":
            early_arrive(k)
        elif name in rings:
            rings[name].arrive(k)
        for key in [key for key in left if (name, k) in left[key]]:
            left[key].discard((name, k))
            if not left[key]:
                final(key)
    columns_end(0)
    columns_end(1)
    columns_wait(0)

    def place(block, rows):
        for xx in range(NX):
            for zz in range(NZ):
                r = rows * ((xx % 2) * 8 + zz)
                yield xx, zz, block[r:r + rows, 128 * (xx // 2):128 * (xx // 2) + 128]

    own_x = xg[tp]
    for xx, zz, value in place(cross(own_x, own_x), 16):
        src_p[zz, xx] = value
    rp = [(dz, remote(src_p.at[z_at(dz)], one_p.at[dz - 1], g1p_s.at[dz - 1], g1p_r.at[dz - 1], along_z(dz)))
          for dz in (4, 3, 5, 2, 6, 1, 7)]
    for _, copy in rp:
        begin(copy)
    columns_wait(1)
    high_x = xg[tp % 2 + 2]
    left = jnp.where(tp < 2, high_x[:, :128], high_x[:, 128:])
    lower = jnp.concatenate([cross(xg[lax.rem(tp + 1, 4)], own_x), cross(left, xg[tp % 2])], axis=0)
    for xx, zz, value in place(lower, 24):
        src_q[xx, zz] = value
    rq = [(dx, remote(src_q.at[x_at(dx)], one_q.at[dx - 1], g1q_s.at[dx - 1], g1q_r.at[dx - 1], along_x(dx)))
          for dx in (2, 1, 3)]
    for _, copy in rq:
        begin(copy)
    for ring in rings.values():
        ring.sent()

    second_p, second_q = [], []
    for _, copy in rq:
        copy.wait_recv()
    total = src_q[x]
    for i in range(NX - 1):
        total = total + one_q[i]
    tot_q[...] = total
    for dz in (4, 3, 5, 2, 6, 1, 7, 0):
        for dy in range(2):
            if dz or dy:
                i = dy * NZ + dz
                second_q.append(begin(remote(tot_q.at[z_at(dz)], two_q.at[i], g2q_s.at[i], g2q_r.at[i], at(0, dy, dz))))
    for _, copy in rp:
        copy.wait_recv()
    total = src_p[z]
    for i in range(NZ - 1):
        total = total + one_p[i]
    tot_p[...] = total
    for dx in (2, 1, 3, 0):
        for dy in range(2):
            if dx or dy:
                i = dy * NX + dx
                second_p.append(begin(remote(tot_p.at[x_at(dx)], two_p.at[i], g2p_s.at[i], g2p_r.at[i], at(dx, dy, 0))))

    near_p, near_q = [], []
    for copy in second_p:
        copy.wait_recv()
    total = tot_p[x]
    for i in range(1, 2 * NX):
        total = total + two_p[i]
    mine = gp.at[core, z, x, lo]
    mine[...] = total
    for dx in (2, 1, 3, 0):
        for dy in range(2):
            if dx or dy:
                i = dy * NX + dx
                near_p.append(begin(remote(mine, mine, ap_s.at[i], ap_r.at[i], at(dx, 0, 0, dy))))
    for copy in second_q:
        copy.wait_recv()
    total = tot_q[z]
    for i in range(1, 2 * NZ):
        total = total + two_q[i]
    mine_q = gq.at[core, x, z, lo]
    mine_q[...] = total
    for dz in (4, 3, 5, 2, 6, 1, 7, 0):
        for dy in range(2):
            if dz or dy:
                i = dy * NZ + dz
                near_q.append(begin(remote(mine_q, mine_q, aq_s.at[i], aq_r.at[i], at(0, 0, dz, dy))))

    drain(len(near_p) + len(near_q))

    def pass_z(d, hop, sub):
        sign = 1 if d == 0 else -1
        chunk = gp.at[core, z_at(-sign * hop), pl.ds(2 * sub, 2)]
        return remote(chunk, chunk, az_s.at[d, hop, sub], az_r.at[d, hop, sub], along_z(sign))

    def pass_x(d, part_at):
        sign = 1 if d == 0 else -1
        half = d if part_at != 1 else 1 - d
        chunk = gq.at[core, x if part_at < 2 else x_at(-sign), pl.ds(4 * half, 4)]
        return remote(chunk, chunk, ax_s.at[d, part_at], ax_r.at[d, part_at], along_x(sign))

    shared = []

    def share(chunk):
        i = len(shared)
        shared.append(remote(chunk, chunk, c_s.at[i], c_r.at[i], sibling))
        shared[-1].start()

    for copy in near_p:
        copy.wait_recv()
    for turn in range(2):
        for d in range(2):
            begin(pass_z(d, 0, d ^ turn))
    share(gp.at[core, z])

    def z_step(hop, turn):
        for d in range(2):
            sub = d ^ turn
            pass_z(d, hop, sub).wait_recv()
            if hop < 2 or (hop == 2 and turn == 0):
                begin(pass_z(d, hop + 1, sub))
        for d in range(2):
            sign = 1 if d == 0 else -1
            if hop == 3:
                share(gp.at[core, z_at(4), pl.ds(2 * d, 2)])
            elif turn == 1:
                share(gp.at[core, z_at(-sign * (hop + 1))])

    def x_step(part_at):
        for d in range(2):
            pass_x(d, part_at).wait_recv()
            if part_at == 0:
                begin(pass_x(d, 2))
        for d in range(2):
            sign = 1 if d == 0 else -1
            half = d if part_at != 1 else 1 - d
            share(gq.at[core, x_at(-sign if part_at < 2 else 2), pl.ds(4 * half, 4)])

    z_step(0, 0)
    for copy in near_q:
        copy.wait_recv()
    for part_at in range(2):
        for d in range(2):
            begin(pass_x(d, part_at))
    share(gq.at[core, x])
    z_step(0, 1)
    z_step(1, 0)
    x_step(0)
    z_step(1, 1)
    z_step(2, 0)
    x_step(1)
    z_step(2, 1)
    z_step(3, 0)
    x_step(2)
    drain()
    for copy in shared:
        copy.wait()


def communicate(partials, momentum):
    def ring(n, *block):
        return [pltpu.VMEM((2, n - 1) + block, F32)] * 2

    def sems(*shape):
        return [pltpu.SemaphoreType.DMA(shape)] * 2

    vmem = pl.BlockSpec(memory_space=pltpu.VMEM)
    block = pltpu.VMEM((ROWS, W), F32)
    return pl.pallas_call(
        kernel,
        out_shape=[
            jax.ShapeDtypeStruct((ROWS, W), F32),
            jax.ShapeDtypeStruct((4, ROWS, W), F32),
            jax.ShapeDtypeStruct((2, NZ, NX, 2, 16, 128), F32),
            jax.ShapeDtypeStruct((2, NX, NZ, 2, 24, 128), F32),
        ],
        in_specs=[pl.BlockSpec(memory_space=pltpu.HBM)] * 2,
        out_specs=[vmem] * 4,
        scratch_shapes=[
            pltpu.VMEM((64, ROWS, W), jnp.bfloat16),
            block,
            pltpu.VMEM((2, ROWS, W), F32),
            pltpu.VMEM((2, NX, HEAD_RING, W), F32),
            pltpu.VMEM((2, NZ, TAIL_RING, W), F32),
            *[pltpu.VMEM((NZ, NX, EARLY, W), F32)] * 2, *[pltpu.VMEM((NX, NZ, EARLY, W), F32)] * 2,
            *ring(NZ, 2, EARLY, W), *ring(NX, 4, EARLY, W),
            pltpu.VMEM((NX, EARLY, W), F32), pltpu.VMEM((NZ, EARLY, W), F32),
            pltpu.VMEM((NX - 1, EARLY, W), F32), pltpu.VMEM((NZ - 1, EARLY, W), F32),
            *ring(NZ, NX, HEAD_RING, W), *ring(NX, HEAD_RING, W), *ring(NX, NZ, TAIL_RING, W), *ring(NZ, TAIL_RING, W),
            block, block, block, block, block,
            pltpu.VMEM((NZ, NX, 16, 128), F32), pltpu.VMEM((NX, NZ, 24, 128), F32),
            pltpu.VMEM((NZ - 1, NX, 16, 128), F32), pltpu.VMEM((NX - 1, NZ, 24, 128), F32),
            pltpu.VMEM((NX, 16, 128), F32), pltpu.VMEM((NZ, 24, 128), F32),
            pltpu.VMEM((2 * NX, 16, 128), F32), pltpu.VMEM((2 * NZ, 24, 128), F32),
            pltpu.SemaphoreType.DMA((NX + 1,)),
            *sems(3, 2, NZ - 1), *sems(2, NX - 1), *sems(5, 2, NX - 1), *sems(2, NZ - 1),
            *sems(3, 2),
            *sems(9), *sems(2, NZ - 1), *sems(2, NX - 1), *sems(NX - 1), *sems(NZ - 1),
            *sems(2, 2),
            *sems(NZ - 1), *sems(NX - 1), *sems(2 * NX), *sems(2 * NZ),
            *sems(2 * NX), *sems(2 * NZ), *sems(2, 4, 2), *sems(2, 3), *sems(18),
        ],
        compiler_params=pltpu.CompilerParams(collective_id=0, has_side_effects=True, vmem_limit_bytes=49 * 1024 * 1024),
    )(partials.reshape(64, ROWS, W), momentum)


def finish(x_ref, gp, gq, w_ref, m_ref, update_ref, neww_ref, newm_ref,
           a, low, ah, al, a2h, a2l, mh, ml, mine):
    tp = lax.axis_index("tp")
    newm_ref[...] = m_ref[...]
    row, col = (lax.broadcasted_iota(jnp.int32, (16, 128), axis) for axis in range(2))
    square = jnp.zeros((16, 128), F32)
    for t in range(4):
        for zz in range(NZ):
            for xx in (0, 3):
                square = square + jnp.where(col - row == 16 * zz, gp[t % 2, zz, xx, t // 2], 0.0)
    inverse = 1.0 / (jnp.sqrt(jnp.sum(square, keepdims=True)) + NORM_EPS)
    scale = inverse * inverse

    def put(first_row, first_col, value):
        rows = slice(first_row, first_row + value.shape[0])
        cols = slice(first_col, first_col + value.shape[1])
        a[rows, cols] = value
        ah[rows, cols], al[rows, cols] = split(value)

    for t in range(4):
        core, lo, base = t % 2, t // 2, 256 * t
        for xx in range(NX):
            for zz in range(NZ):
                r, c = (xx % 2) * 8 + zz, xx // 2
                put(base + 16 * r, base + 128 * c, gp[core, zz, xx, lo] * scale)
                low[t, 24 * r:24 * r + 24, 128 * c:128 * c + 128] = gq[core, xx, zz, lo] * scale
    for t in range(4):
        nxt = (t + 1) % 4
        side = low[t, :256, :]
        put(256 * nxt, 256 * t, side)
        put(256 * t, 256 * nxt, side.T)
        far = low[t, 256:, :]
        i, j = 256 * (t % 2 + 2) + 128 * (t // 2), 256 * (t % 2)
        put(i, j, far)
        put(j, i, far.T)

    def dot3(lh, ll, rh, rl):
        dot = functools.partial(jnp.dot, preferred_element_type=F32)
        return dot(lh, rh) + (dot(lh, rl) + dot(ll, rh))

    same = lax.broadcasted_iota(jnp.int32, (256, 256), 0) == lax.broadcasted_iota(jnp.int32, (256, 256), 1)

    def store(rows, cols, block):
        a2h[rows, cols], a2l[rows, cols] = split(block)
        value = COEF_B * a[rows, cols] + COEF_C * block
        if rows == cols:
            value = value + jnp.where(same, COEF_A, 0.0)
        mh[rows, cols], ml[rows, cols] = split(value)

    for i in range(4):
        rows = slice(256 * i, 256 * i + 256)
        for j in range(i, 4):
            cols = slice(256 * j, 256 * j + 256)
            block = dot3(ah[rows, :], al[rows, :], ah[:, cols], al[:, cols])
            store(rows, cols, block)
            if j > i:
                store(cols, rows, block.T)

    def times(x, high, lowp, cols=None):
        xh, xl = split(x)
        both = jnp.concatenate([xh, xl], axis=0)
        parts = []
        for at in [cols] if cols is not None else [slice(256 * j, 256 * j + 256) for j in range(4)]:
            first = jnp.dot(both, high[:, at], preferred_element_type=F32)
            second = jnp.dot(xh, lowp[:, at], preferred_element_type=F32)
            parts.append(first[:ROWS] + (first[ROWS:] + second))
        return parts[0] if cols is not None else jnp.concatenate(parts, axis=1)

    own = pl.ds(pl.multiple_of(tp * 256, 256), 256)
    start = jnp.concatenate([x_ref[t] for t in range(4)], axis=1) * inverse
    one = times(start, mh, ml)
    for t in range(4):
        mine[t] = one[:, 256 * t:256 * t + 256]
    turned = times(times(one, mh, ml), mh, ml)
    result = COEF_A * mine[tp] + COEF_B * times(turned, ah, al, own)
    result = result + COEF_C * times(times(times(turned, a2h, a2l), mh, ml), mh, ml, own)
    update = 0.2 * math.sqrt(max(D, FF)) * result
    update_ref[...] = update
    neww_ref[...] = w_ref[...] - LEARN_RATE * (update + WEIGHT_DECAY * w_ref[...])


def orthogonalize(x, gp, gq, weights, new_momentum):
    vmem = pl.BlockSpec(memory_space=pltpu.VMEM)
    block = jax.ShapeDtypeStruct((ROWS, W), F32)
    half = jnp.bfloat16
    return pl.pallas_call(
        finish,
        out_shape=[block] * 3,
        in_specs=[vmem] * 5,
        out_specs=[vmem] * 3,
        scratch_shapes=[
            pltpu.VMEM((FF, FF), F32), pltpu.VMEM((4, 384, W), F32),
            *[pltpu.VMEM((FF, FF), half)] * 6,
            pltpu.VMEM((4, ROWS, W), F32),
        ],
        compiler_params=pltpu.CompilerParams(vmem_limit_bytes=40 * 1024 * 1024),
    )(x, gp, gq, weights, new_momentum)


def on_device(partials, momentum, weights):
    new_momentum, x, gp, gq = communicate(partials[0], momentum)
    return tuple(orthogonalize(x, gp, gq, weights, new_momentum))


def solution(mesh):
    return jax.shard_map(
        on_device,
        mesh=mesh,
        in_specs=(P("dp", None, "tp"), P("dp", "tp"), P("dp", "tp")),
        out_specs=(P("dp", "tp"), P("dp", "tp"), P("dp", "tp")),
        check_vma=False,
    )
```
